32 devices in a mesh: wide: 8 (over z, core), narrow: 4 (over y, x).
Axes of the slice: x: 2, y: 2, z: 4, core: 2. Of those that a mesh axis runs over, the one named last changes fastest.
Arguments:
- right_sides: float32 [4, 512, 128], P(None, ('wide', 'narrow')), may hold values from -6 to 6
- brinkman: float32 [512, 128], P(('wide', 'narrow')), may hold values from 0.1 to 1
- east_faces: float32 [512, 128], P(('wide', 'narrow')), may hold values from 0.1 to 10
- north_faces: float32 [512, 128], P(('wide', 'narrow')), may hold values from 0.1 to 10
- support: int32 [1024, 4], P(('wide', 'narrow')), may hold values from 0 to 31
- basis: float32 [1024, 64, 256], P(('wide', 'narrow')), may hold values from -0.75 to 0.75
- links: int32 [32, 4], P('wide'), may hold values from 0 to 31
- coarse_block_inverses: float32 [32, 64, 64], P('wide')
- coarse_coupling: float32 [32, 64, 256], P('wide')
Outputs:
- solution: float32 [4, 512, 128], P(None, ('wide', 'narrow'))
- coarse_solution: float32 [32, 256], P('wide')
The draws below stay inside these ranges and needn't reach their ends.
All inputs are finite; a program needn't handle non-finite values.
Results may differ from the reference program's by a relative error of at most 0.0001.
Values sent between devices are 32-bit elements; how exact they have to be, the bound alone decides.
No kernel may reach another device: no remote copies, remote signals or barrier semaphores. Data moves between devices by JAX's collectives and lax.ppermute only.
A program may use at most 64 MiB of HBM per device.

```python
import math
import jax
import jax.numpy as jnp
from jax import lax

ROW_CELLS = 128
BLOCK_SIZE = 64
SUPPORT = 4
COARSE_LINKS = 4
ADJOINTS = 4
SWEEPS = 2
COARSE_SWEEPS = 3
FINE_ROWS = 512
FINE_BLOCKS = 1024
COARSE_BLOCKS = 32


def draw_coarse_block_inverses(key, part):
    first_key, second_key = jax.random.split(jax.random.fold_in(key, 11))
    fine_share = FINE_BLOCKS * SUPPORT * BLOCK_SIZE / COARSE_BLOCKS
    factor = 1.0 / math.sqrt(fine_share)
    diagonal = jax.random.uniform(first_key, (COARSE_BLOCKS, BLOCK_SIZE), jnp.float32, 1.0, 2.0)
    diagonal_perturbation = jax.random.normal(second_key, (COARSE_BLOCKS, BLOCK_SIZE, BLOCK_SIZE), jnp.float32) * 0.04
    identity = jnp.eye(BLOCK_SIZE, dtype=jnp.float32)
    return factor * (diagonal_perturbation + identity[None] * diagonal[:, :, None])


def draw_coarse_coupling(key, part):
    fine_share = FINE_BLOCKS * SUPPORT * BLOCK_SIZE / COARSE_BLOCKS
    factor = 0.33 * math.sqrt(fine_share) / math.sqrt(BLOCK_SIZE * COARSE_LINKS)
    values = jax.random.normal(jax.random.fold_in(key, 23), (COARSE_BLOCKS, BLOCK_SIZE, COARSE_LINKS * BLOCK_SIZE), jnp.float32)
    return factor * values


def plant(entries, stream_key, least, top_value):
    longest = entries.shape.index(max(entries.shape))
    spots = []
    for shift in (0, 1):
        where = [jax.random.randint(jax.random.fold_in(stream_key, axis), (), 0, length) for axis, length in enumerate(entries.shape)]
        where[longest] = (where[longest] + shift) % entries.shape[longest]
        spots.append(tuple(where))
    return entries.at[spots[0]].set(least).at[spots[1]].set(top_value)


def level_of(own_key, extent, cuts, low, high):
    gain, own = 1.0, jax.random.fold_in(own_key, 6)
    for axis_at, parts in cuts:
        heights = jnp.exp(jax.random.uniform(jax.random.fold_in(own, axis_at), (parts,), jnp.float32, low / len(cuts), high / len(cuts)))
        gain = gain * jnp.repeat(heights, extent[axis_at] // parts).reshape([-1 if axis == axis_at else 1 for axis in range(len(extent))])
    return gain


def bell_draw(rng, dims, spread, bound, pieces=(), kind=jnp.bfloat16):
    values = jax.random.normal(rng, dims, jnp.float32) * spread
    if len(pieces) > 0:
        values = level_of(rng, dims, pieces, -0.22, 0.18) * values
    return jnp.clip(values, min=-bound, max=bound).astype(kind)


def setup_inputs(seed: int = 0) -> dict:
    splits = jax.random.split(jax.random.key(seed), 10)
    return {
        "right_sides": bell_draw(splits[0], (ADJOINTS, FINE_ROWS, ROW_CELLS), 1.0, 6.0, ((1, 32),), jnp.float32),
        "brinkman": jnp.clip(jnp.exp(math.log(1.0) - 2.3025851 * jax.random.uniform(splits[1], (FINE_ROWS, ROW_CELLS), jnp.float32) ** level_of(splits[1], (FINE_ROWS, ROW_CELLS), ((0, 32),), -0.2, 0.2)), 0.1, 1.0),
        "east_faces": jnp.clip(jnp.exp(math.log(10.0) - 4.6051702 * jax.random.uniform(splits[2], (FINE_ROWS, ROW_CELLS), jnp.float32) ** level_of(splits[2], (FINE_ROWS, ROW_CELLS), ((0, 32),), -0.2, 0.2)), 0.1, 10.0),
        "north_faces": jnp.clip(jnp.exp(math.log(10.0) - 4.6051702 * jax.random.uniform(splits[3], (FINE_ROWS, ROW_CELLS), jnp.float32) ** level_of(splits[3], (FINE_ROWS, ROW_CELLS), ((0, 32),), -0.2, 0.2)), 0.1, 10.0),
        "support": plant(jax.random.randint(splits[4], (FINE_BLOCKS, SUPPORT), 0, COARSE_BLOCKS), jax.random.fold_in(splits[4], 1), 0, COARSE_BLOCKS - 1).astype(jnp.int32),
        "basis": bell_draw(splits[5], (FINE_BLOCKS, BLOCK_SIZE, SUPPORT * BLOCK_SIZE), BLOCK_SIZE ** -0.5, 0.75, ((0, 32),), jnp.float32),
        "links": plant(jax.random.randint(splits[6], (COARSE_BLOCKS, COARSE_LINKS), 0, COARSE_BLOCKS), jax.random.fold_in(splits[6], 1), 0, COARSE_BLOCKS - 1).astype(jnp.int32),
        "coarse_block_inverses": draw_coarse_block_inverses(jax.random.fold_in(splits[9], 71), 0),
        "coarse_coupling": draw_coarse_coupling(jax.random.fold_in(splits[9], 71), 0),
    }


relax_weight = 0.7


def reference(right_sides, brinkman, east_faces, north_faces, support, basis, links, coarse_block_inverses, coarse_coupling):
    top_precision = lax.Precision.HIGHEST
    south = jnp.concatenate([jnp.zeros((1, ROW_CELLS), jnp.float32), north_faces[:-1]], 0)
    west = jnp.roll(east_faces, 1, axis=1)
    diagonal = brinkman + east_faces + west + north_faces + south

    def operate(field):
        padded = jnp.pad(field, ((0, 0), (1, 1), (0, 0)))
        above = padded[:, :-2]
        below = padded[:, 2:]
        return (diagonal * field - north_faces * below - south * above
                - east_faces * jnp.roll(field, -1, axis=2) - west * jnp.roll(field, 1, axis=2))

    def sweep(field):
        return field + relax_weight * (right_sides - operate(field)) / diagonal

    field = jnp.zeros_like(right_sides)
    for step in range(SWEEPS):
        field = sweep(field)
    resid = (right_sides - operate(field)).reshape(ADJOINTS, FINE_BLOCKS, BLOCK_SIZE)
    contrib = jnp.einsum('bfm,abf->bam', basis, resid, precision=top_precision)
    contrib = contrib.reshape(FINE_BLOCKS, ADJOINTS, SUPPORT, BLOCK_SIZE).transpose(0, 2, 1, 3)
    coarse_rhs = jax.ops.segment_sum(contrib.reshape(FINE_BLOCKS * SUPPORT, ADJOINTS * BLOCK_SIZE),
                                     support.reshape(-1), num_segments=COARSE_BLOCKS)
    coarse_rhs = coarse_rhs.reshape(COARSE_BLOCKS, ADJOINTS, BLOCK_SIZE)

    def apply_inverse(adjoint_vector):
        return jnp.einsum('lzo,lso->lsz', coarse_block_inverses, adjoint_vector, precision=top_precision)

    coarse = apply_inverse(coarse_rhs)
    for step in range(COARSE_SWEEPS):
        nearby = coarse[links].transpose(0, 2, 1, 3).reshape(COARSE_BLOCKS, ADJOINTS, COARSE_LINKS * BLOCK_SIZE)
        pulled = jnp.einsum('icm,iam->iac', coarse_coupling, nearby, precision=top_precision)
        coarse = apply_inverse(coarse_rhs + pulled)
    chosen = coarse[support].transpose(0, 2, 1, 3).reshape(FINE_BLOCKS, ADJOINTS, SUPPORT * BLOCK_SIZE)
    coarse_update = jnp.einsum('bfm,bam->abf', basis, chosen, precision=top_precision)
    field = field + coarse_update.reshape(ADJOINTS, FINE_ROWS, ROW_CELLS)
    for step in range(SWEEPS):
        field = sweep(field)
    return field, coarse.reshape(COARSE_BLOCKS, ADJOINTS * BLOCK_SIZE)
```

```python
import functools

import jax
import jax.numpy as jnp
from jax import lax
from jax.experimental import pallas as pl
from jax.experimental.pallas import tpu as pltpu
from jax.sharding import PartitionSpec as P

SWEEPS = 2
COARSE_SWEEPS = 3
relax_weight = 0.7

BOTH = ("wide", "narrow")
HALO = 3
FIELD = 24
PIECE = 88
F32 = jnp.float32
BF16 = jnp.bfloat16


def swap(value, axis, bits):
    size = lax.axis_size(axis)
    return lax.ppermute(value, axis, [(i, i ^ bits) for i in range(size)])


def pair_swaps(to_first, to_second):
    count = lax.axis_size(BOTH)
    first = lax.ppermute(to_first, BOTH, [(i, i ^ 1) for i in range(count)])
    odd = [(i, i + 1) for i in range(1, count - 1, 2)] + [(count - 1, 0)]
    second = lax.ppermute(to_second, BOTH, odd + [(target, source) for source, target in odd])
    return first, second


def groups_of(size):
    rounds, base = [], 1
    while base < size:
        span = 4 if base * 4 <= size else 2
        rounds.append([base * k for k in range(1, span)])
        base *= span
    return rounds


def sum_all(value):
    value = value + swap(value, "wide", 1)
    for masks in groups_of(lax.axis_size("narrow")):
        value = sum([swap(value, "narrow", k) for k in masks], value)
    for masks in groups_of(lax.axis_size("wide") // 2):
        value = sum([swap(value, "wide", 2 * k) for k in masks], value)
    return value


def place():
    wide, narrow = lax.axis_index("wide"), lax.axis_index("narrow")
    line = wide * lax.axis_size("narrow") + narrow
    count = lax.axis_size("wide") * lax.axis_size("narrow")
    return line, count


def lanes(shape):
    return lax.broadcasted_iota(jnp.int32, shape, len(shape) - 1)


def rows(shape):
    return lax.broadcasted_iota(jnp.int32, shape, len(shape) - 2)


def split(value):
    high = value.astype(BF16)
    return high, (value - high.astype(F32)).astype(BF16)


def dot(left, right):
    return lax.dot_general(left, right, (((1,), (0,)), ((), ())), preferred_element_type=F32)


def dot_t(left, right):
    return lax.dot_general(left, right, (((1,), (1,)), ((), ())), preferred_element_type=F32)


def half_turn(value):
    return pltpu.roll(value, 64, 1)


def edges_kernel(r, b, e, n, first, second):
    grid_rows = b.shape[0]
    line, _ = place()
    even = lax.rem(line, 2) == 0

    def message(start, north_start):
        parts = [r[a, start:start + HALO, :] for a in range(r.shape[0])]
        parts += [b[start:start + HALO, :], e[start:start + HALO, :]]
        parts += [n[north_start:north_start + HALO + 1, :], jnp.zeros((2, b.shape[1]), F32)]
        return parts

    top = message(0, 0)
    bottom = message(grid_rows - HALO, grid_rows - HALO - 1)
    at = 0
    for low, high in zip(top, bottom):
        size = low.shape[0]
        first[at:at + size, :] = jnp.where(even, high, low)
        second[at:at + size, :] = jnp.where(even, low, high)
        at += size


def pack_kernel(owned, links, coupling, inverses, block, own):
    q = lax.rem(lax.axis_index("narrow"), owned)
    lane = lanes((8, 256))
    for j_rel in range(owned):
        j = jnp.bitwise_xor(q, j_rel)
        base = j_rel * PIECE
        matrix = coupling[j]
        inverse = inverses[j]
        packed = jnp.concatenate([inverse[16 * t:16 * t + 16, :] for t in range(4)], axis=1)
        tail = jnp.zeros((8, 256), F32)
        for l in range(links.shape[1]):
            tail = jnp.where(lane == l, links[j, l].astype(F32), tail)
        block[base:base + 64, :] = matrix
        block[base + 64:base + 80, :] = packed
        block[base + 80:base + 88, :] = tail
        if j_rel == 0:
            own[0:64, :] = matrix
            own[64:80, :] = packed
            own[80:88, :] = tail


class Fine:
    def __init__(self, r, b, e, n, from_first, from_second, rx, bx, ex, nx, field):
        line, count = place()
        even = lax.rem(line, 2) == 0
        low_ok, high_ok = line > 0, line < count - 1
        one, two = from_first[...], from_second[...]
        low = jnp.where(low_ok, jnp.where(even, two, one), 0.0)
        high = jnp.where(high_ok, jnp.where(even, one, two), 0.0)
        self.even, self.low_ok, self.high_ok = even, low_ok, high_ok
        self.adjoints, self.grid_rows, width = r.shape
        top = HALO + self.grid_rows
        zeros = jnp.zeros((8, width), F32)
        for a in range(self.adjoints):
            rx[a, 16:24, :] = zeros
            rx[a, 0:HALO, :] = low[3 * a:3 * a + 3]
            rx[a, HALO:top, :] = r[a]
            rx[a, top:top + HALO, :] = high[3 * a:3 * a + 3]
            field[a, 0:8, :] = zeros
            field[a, 32:40, :] = zeros
        bx[16:24, :] = zeros
        bx[0:HALO, :] = low[12:15]
        bx[HALO:top, :] = b[...]
        bx[top:top + HALO, :] = high[12:15]
        ex[16:24, :] = zeros
        ex[0:HALO, :] = low[15:18]
        ex[HALO:top, :] = e[...]
        ex[top:top + HALO, :] = high[15:18]
        nx[16:24, :] = zeros
        nx[24:32, :] = zeros
        nx[0:HALO + 1, :] = low[18:22]
        nx[HALO + 1:top + 1, :] = n[...]
        nx[top + 1:top + 1 + HALO, :] = high[18:21]
        self.r = rx[...]
        self.east = ex[...]
        self.north = nx[1:1 + FIELD, :]
        self.south = nx[0:FIELD, :]
        self.west = pltpu.roll(self.east, 1, 1)
        self.diagonal = bx[...] + self.east + self.west + self.north + self.south
        t = rows((FIELD, width))
        valid = ((t >= HALO) | low_ok) & ((t < top) | high_ok) & (t < top + HALO)
        self.scale = jnp.where(valid, relax_weight / jnp.where(valid, self.diagonal, 1.0), 0.0)
        self.field = field
        self.width = width

    def apply(self, x):
        self.field[:, 8:32, :] = x
        above = self.field[:, 7:31, :]
        below = self.field[:, 9:33, :]
        east = pltpu.roll(x, self.width - 1, 2)
        west = pltpu.roll(x, 1, 2)
        return self.diagonal * x - self.north * below - self.south * above - self.east * east - self.west * west

    def sweep(self, x):
        return x + self.scale * (self.r - self.apply(x))


def fine_scratch(adjoints, width):
    return [
        pltpu.VMEM((adjoints, FIELD, width), F32),
        pltpu.VMEM((FIELD, width), F32),
        pltpu.VMEM((FIELD, width), F32),
        pltpu.VMEM((32, width), F32),
        pltpu.VMEM((adjoints, 40, width), F32),
    ]


def restrict_kernel(coarse_rows, r, b, e, n, from_first, from_second, basis, sup, out, x_out,
                    rx, bx, ex, nx, field, by_row, contrib):
    fine = Fine(r, b, e, n, from_first, from_second, rx, bx, ex, nx, field)
    x = fine.scale * fine.r
    for step in range(SWEEPS - 1):
        x = fine.sweep(x)
    resid = fine.r - fine.apply(x)
    for a in range(fine.adjoints):
        x_out[a] = field[a, 8 + HALO:8 + HALO + fine.grid_rows, :]
    field[:, 8:32, :] = resid
    for a in range(fine.adjoints):
        by_row[pl.ds(a, fine.grid_rows, stride=4), :] = field[a, 8 + HALO:8 + HALO + fine.grid_rows, :]
    left = lanes((8, 128)) < 64
    upper = rows((8, 128)) < 4
    for g in range(fine.grid_rows // 2):
        z = by_row[8 * g:8 * g + 8, :]
        parts = []
        for here in (left, ~left):
            held = jnp.where(here, z, 0.0)
            parts.append(jnp.concatenate([jnp.where(upper, held, 0.0), jnp.where(upper, 0.0, held)], axis=1))
        high, low = split(jnp.concatenate(parts, axis=0))
        w_high, w_low = split(basis[256 * g:256 * g + 256, :])
        both = dot(jnp.concatenate([high, low], axis=0), w_high)
        contrib[16 * g:16 * g + 16, :] = both[0:16] + both[16:32] + dot(high, w_low)
    c_high, c_low = split(contrib[...])
    weights = jnp.concatenate([
        jnp.concatenate([c_high[:, 0:128], c_low[:, 0:128]], axis=1),
        jnp.concatenate([c_high[:, 128:256], c_low[:, 128:256]], axis=1)], axis=0)
    size = 4 * coarse_rows
    at = rows((size, 128))
    hot = [jnp.where(at == sup[k:k + 1, :], 1.0, 0.0).astype(BF16) for k in range(4)]
    hots = jnp.concatenate([
        jnp.concatenate([hot[0], hot[2]], axis=1), jnp.concatenate([hot[1], hot[3]], axis=1)], axis=0)
    total = dot(hots, weights)
    total = total[:, 0:128] + total[:, 128:256]
    here = lanes((size, 128)) < 64
    even = jnp.where(here, total[0:size], 0.0)
    odd = jnp.where(here, 0.0, total[size:2 * size])
    mid = size // 2
    out[...] = even[0:mid] + half_turn(odd[0:mid]) + half_turn(even[mid:size]) + odd[mid:size]


def coarse_kernel(owned, coarse_rows, zs, refs):
    refs = list(refs)

    def take(count):
        got = refs[:count]
        del refs[:count]
        return got

    (rhs_ref,) = take(1)
    pieces = take(2 * (1 + owned))
    basis, sup, x_ref = take(3)
    y_ref, coarse_ref, first, second = take(4)
    w_high, w_low, w_inv, link_rows, hots, product, u_ref, by_row = refs
    size = 4 * coarse_rows
    wide, narrow = lax.axis_index("wide"), lax.axis_index("narrow")
    q = lax.rem(narrow, owned)
    mine = wide * owned + q

    lane16 = lanes((16, 128)) < 64
    for z_rel in range(zs):
        for c_rel in range(2):
            for j_rel in range(owned):
                i = (z_rel * 2 + c_rel) * owned + j_rel
                if z_rel == 0:
                    piece, base = pieces[c_rel * (1 + owned)], j_rel * PIECE
                else:
                    piece, base = pieces[c_rel * (1 + owned) + 1 + j_rel], (z_rel - 1) * PIECE
                high, low = split(piece[base:base + 64, :])
                w_high[64 * i:64 * i + 64, :] = high
                w_low[64 * i:64 * i + 64, :] = low
                quarters = []
                for half in range(2):
                    packed = piece[base + 64:base + 80, 128 * half:128 * half + 128]
                    turned = half_turn(packed)
                    quarters += [jnp.where(lane16, packed, turned), jnp.where(lane16, turned, packed)]
                high, low = split(jnp.concatenate(quarters, axis=0))
                w_inv[64 * i:64 * i + 64, 0:128] = high
                w_inv[64 * i:64 * i + 64, 128:256] = low
                link_rows[4 * i:4 * i + 4, :] = piece[base + 80:base + 84, 0:128]

    lane = lanes((size, size))
    a_col = jnp.bitwise_and(rows((size, 1)), 3)
    for l in range(4):
        target = jnp.bitwise_xor(link_rows[:, l:l + 1].astype(jnp.int32), mine) * 4 + a_col
        hots[size * l:size * l + size, :] = jnp.where(lane == target, 1.0, 0.0).astype(BF16)

    here = lanes((size, 128)) < 64
    packed = rhs_ref[...]
    turned = half_turn(packed)
    here_mid = here[0:size // 2]
    rhs = jnp.concatenate([jnp.where(here_mid, packed, turned), jnp.where(here_mid, turned, packed)], axis=0)

    def hi_lo(value):
        high, low = split(value)
        return jnp.concatenate([high, low], axis=1)

    source = jnp.bitwise_xor(rows((size, 1)), mine * 4)
    order = jnp.where(lane == source, 1.0, 0.0).astype(BF16)
    rhs = dot(order, hi_lo(rhs))
    rhs = rhs[:, 0:128] + rhs[:, 128:256]

    own_block = jnp.bitwise_and(lax.shift_right_logical(rows((size, 256)), 2), 3) == lax.shift_right_logical(
        lanes((size, 256)), 6)

    def fold():
        value = jnp.where(own_block, product[...], 0.0)
        value = value[:, 0:128] + value[:, 128:256]
        return value + half_turn(value)

    def apply_inverse(value):
        high, low = split(value)
        mixed = jnp.where(here, high.astype(F32), low.astype(F32)).astype(BF16)
        mixed = jnp.concatenate([mixed, mixed], axis=1)
        for g in range(coarse_rows // 4):
            product[16 * g:16 * g + 16, :] = dot_t(mixed[16 * g:16 * g + 16], w_inv[256 * g:256 * g + 256, :])
        return fold()

    def pick(got, step):
        sel = lanes((step, 128)) < 64
        high = [jnp.where(sel, got[step * k:step * k + step, 0:128], got[step * k + step:step * k + 2 * step, 0:128])
                for k in (0, 2)]
        low = [jnp.where(sel, got[step * k:step * k + step, 128:256],
                         got[step * k + step:step * k + 2 * step, 128:256]) for k in (0, 2)]
        return jnp.concatenate(high, axis=1).astype(BF16), jnp.concatenate(low, axis=1).astype(BF16)

    u = apply_inverse(rhs)
    for step in range(COARSE_SWEEPS):
        high, low = pick(dot(hots[...], hi_lo(u)), size)
        for g in range(coarse_rows // 4):
            near = slice(16 * g, 16 * g + 16)
            block = slice(256 * g, 256 * g + 256)
            both = dot_t(jnp.concatenate([high[near], low[near]], axis=0), w_high[block, :])
            product[near, :] = both[0:16] + both[16:32] + dot_t(high[near], w_low[block, :])
        u = apply_inverse(rhs + fold())

    u_ref[...] = u[0:4 * owned]
    here1 = lanes((1, 128)) < 64
    for j in range(owned):
        got = u_ref[pl.ds(jnp.bitwise_xor(q, j) * 4, 4), :]
        coarse_ref[j:j + 1, 0:128] = jnp.where(here1, got[0:1], got[1:2])
        coarse_ref[j:j + 1, 128:256] = jnp.where(here1, got[2:3], got[3:4])

    blocks4 = sup.shape[0]
    lane_s = lanes((blocks4, size))
    sup_hots = jnp.concatenate(
        [jnp.where(lane_s == sup[:, k:k + 1], 1.0, 0.0).astype(BF16) for k in range(4)], axis=0)
    high, low = pick(dot(sup_hots, hi_lo(u)), blocks4)
    left = lanes((8, 128)) < 64
    upper = rows((8, 128)) < 4
    for g in range(blocks4 // 16):
        b_high, b_low = split(basis[256 * g:256 * g + 256, :])
        near = slice(16 * g, 16 * g + 16)
        both = dot_t(jnp.concatenate([high[near], low[near]], axis=0), b_high)
        got = both[0:16] + both[16:32] + dot_t(high[near], b_low)
        halves = [jnp.where(upper, got[8 * h:8 * h + 8, 0:128], got[8 * h:8 * h + 8, 128:256]) for h in range(2)]
        by_row[8 * g:8 * g + 8, :] = jnp.where(left, halves[0], halves[1])
    line, _ = place()
    even = lax.rem(line, 2) == 0
    adjoints, grid_rows, _ = x_ref.shape
    for a in range(adjoints):
        y = x_ref[a] + by_row[pl.ds(a, grid_rows, stride=4), :]
        y_ref[a] = y
        top, bottom = y[0:2], y[grid_rows - 2:grid_rows]
        first[2 * a:2 * a + 2, :] = jnp.where(even, bottom, top)
        second[2 * a:2 * a + 2, :] = jnp.where(even, top, bottom)


def post_kernel(r, b, e, n, from_first, from_second, y_ref, y_first, y_second, out, rx, bx, ex, nx, field, yx):
    fine = Fine(r, b, e, n, from_first, from_second, rx, bx, ex, nx, field)
    one, two = y_first[...], y_second[...]
    low = jnp.where(fine.low_ok, jnp.where(fine.even, two, one), 0.0)
    high = jnp.where(fine.high_ok, jnp.where(fine.even, one, two), 0.0)
    top = HALO + fine.grid_rows
    for a in range(fine.adjoints):
        yx[a, 0:8, :] = jnp.zeros((8, fine.width), F32)
        yx[a, 16:24, :] = jnp.zeros((8, fine.width), F32)
        yx[a, HALO - 2:HALO, :] = low[2 * a:2 * a + 2]
        yx[a, HALO:top, :] = y_ref[a]
        yx[a, top:top + 2, :] = high[2 * a:2 * a + 2]
    x = yx[...]
    for step in range(SWEEPS):
        x = fine.sweep(x)
    field[:, 8:32, :] = x
    for a in range(fine.adjoints):
        out[a] = field[a, 8 + HALO:8 + HALO + fine.grid_rows, :]


def shape(*dims):
    return jax.ShapeDtypeStruct(dims, F32)


def params(mebibytes):
    return pltpu.CompilerParams(vmem_limit_bytes=mebibytes * 2 ** 20)


def body(right_sides, brinkman, east_faces, north_faces, support, basis, links, coarse_block_inverses, coarse_coupling):
    adjoints, grid_rows, width = right_sides.shape
    blocks, block_size, _ = basis.shape
    owned = coarse_block_inverses.shape[0]
    coarse_rows = owned * lax.axis_size("wide")
    zs = lax.axis_size("wide") // 2
    size = 4 * coarse_rows
    basis = basis.reshape(blocks * block_size, -1)

    message = shape(24, width)
    to_first, to_second = pl.pallas_call(
        edges_kernel, out_shape=(message, message), compiler_params=params(16), name="edges",
    )(right_sides, brinkman, east_faces, north_faces)
    from_first, from_second = pair_swaps(to_first, to_second)

    in_vmem = pl.BlockSpec(memory_space=pltpu.VMEM)
    block, own = pl.pallas_call(
        functools.partial(pack_kernel, owned),
        out_shape=(shape(owned * PIECE, 256), shape(PIECE, 256)),
        in_specs=[pl.BlockSpec(memory_space=pltpu.SMEM), in_vmem, in_vmem],
        compiler_params=params(16), name="pack",
    )(links, coarse_coupling, coarse_block_inverses)

    fetched = jnp.concatenate([swap(own, "wide", 2 * k) for k in range(1, zs)], axis=0)
    pieces = [block, fetched] + [swap(fetched, "narrow", k) for k in range(1, owned)]
    pieces = pieces + [swap(piece, "wide", 1) for piece in pieces]

    mine = lax.axis_index("wide") * owned + lax.rem(lax.axis_index("narrow"), owned)
    by_k = support.reshape(blocks // 4, 2, 2, 4).transpose(3, 0, 2, 1).reshape(4, blocks, 1)
    a_row = jnp.arange(adjoints, dtype=jnp.int32)
    sup = (by_k * 4 + a_row).reshape(4, blocks * adjoints)
    sup_rel = (jnp.bitwise_xor(by_k, mine) * 4 + a_row).reshape(4, blocks * adjoints).T

    rhs, x = pl.pallas_call(
        functools.partial(restrict_kernel, coarse_rows),
        out_shape=(shape(size // 2, 128), shape(adjoints, grid_rows, width)),
        scratch_shapes=fine_scratch(adjoints, width) + [
            pltpu.VMEM((4 * grid_rows, width), F32), pltpu.VMEM((4 * blocks, 256), F32)],
        compiler_params=params(24), name="restrict",
    )(right_sides, brinkman, east_faces, north_faces, from_first, from_second, basis, sup)

    rhs = sum_all(rhs)

    def coarse_body(*refs):
        coarse_kernel(owned, coarse_rows, zs, refs)

    y, coarse, y_first, y_second = pl.pallas_call(
        coarse_body,
        out_shape=(shape(adjoints, grid_rows, width), shape(owned, 256), shape(8, width), shape(8, width)),
        scratch_shapes=[
            pltpu.VMEM((64 * coarse_rows, 256), BF16), pltpu.VMEM((64 * coarse_rows, 256), BF16),
            pltpu.VMEM((64 * coarse_rows, 256), BF16), pltpu.VMEM((size, 128), F32),
            pltpu.VMEM((4 * size, size), BF16), pltpu.VMEM((size, 256), F32),
            pltpu.VMEM((4 * owned, 128), F32), pltpu.VMEM((4 * grid_rows, width), F32)],
        compiler_params=params(min(56, 16 + coarse_rows // 2)), name="coarse",
    )(rhs, *pieces, basis, sup_rel, x)

    y_first, y_second = pair_swaps(y_first, y_second)
    solution_field = pl.pallas_call(
        post_kernel,
        out_shape=shape(adjoints, grid_rows, width),
        scratch_shapes=fine_scratch(adjoints, width) + [pltpu.VMEM((adjoints, FIELD, width), F32)],
        compiler_params=params(16), name="post",
    )(right_sides, brinkman, east_faces, north_faces, from_first, from_second, y, y_first, y_second)
    return solution_field, coarse


def solution(mesh):
    return jax.shard_map(
        body,
        mesh=mesh,
        in_specs=(
            P(None, ("wide", "narrow"), None),
            P(("wide", "narrow"), None),
            P(("wide", "narrow"), None),
            P(("wide", "narrow"), None),
            P(("wide", "narrow"), None),
            P(("wide", "narrow"), None, None),
            P("wide", None),
            P("wide", None, None),
            P("wide", None, None),
        ),
        out_specs=(P(None, ("wide", "narrow"), None), P("wide", None)),
        check_vma=False,
    )
```

```python
import functools

import jax
import jax.numpy as jnp
from jax import lax
from jax.experimental import pallas as pl
from jax.experimental.pallas import tpu as pltpu
from jax.sharding import PartitionSpec as P

SWEEPS = 2
COARSE_SWEEPS = 3
relax_weight = 0.7

BOTH = ("wide", "narrow")
HALO = 3
FIELD = 24
PIECE = 88
F32 = jnp.float32
BF16 = jnp.bfloat16


def swap(value, axis, bits):
    size = lax.axis_size(axis)
    return lax.ppermute(value, axis, [(i, i ^ bits) for i in range(size)])


def pair_swaps(to_first, to_second):
    count = lax.axis_size(BOTH)
    first = lax.ppermute(to_first, BOTH, [(i, i ^ 1) for i in range(count)])
    odd = [(i, i + 1) for i in range(1, count - 1, 2)] + [(count - 1, 0)]
    second = lax.ppermute(to_second, BOTH, odd + [(target, source) for source, target in odd])
    return first, second


def tie(values, after):
    count = len(values)
    spec = pl.BlockSpec(memory_space=pl.ANY)
    return list(pl.pallas_call(
        lambda *refs: None, out_shape=[jax.ShapeDtypeStruct(v.shape, v.dtype) for v in values],
        in_specs=[spec] * (count + 1), out_specs=[spec] * count,
        input_output_aliases={i: i for i in range(count)}, cost_estimate=CHEAP, compiler_params=params(1), name="tie",
    )(*values, after))


def rounds_of(size):
    rounds, base = [], 1
    while base < size:
        span = 4 if base * 4 <= size else 2
        rounds.append([base * k for k in range(1, span)])
        base *= span
    return rounds


def bits_of(size):
    return [1 << i for i in range(size.bit_length() - 1)]


def place():
    wide, narrow = lax.axis_index("wide"), lax.axis_index("narrow")
    line = wide * lax.axis_size("narrow") + narrow
    count = lax.axis_size("wide") * lax.axis_size("narrow")
    return line, count


def lanes(shape):
    return lax.broadcasted_iota(jnp.int32, shape, len(shape) - 1)


def rows(shape):
    return lax.broadcasted_iota(jnp.int32, shape, len(shape) - 2)


def split(value):
    high = value.astype(BF16)
    return high, (value - high.astype(F32)).astype(BF16)


def dot(left, right):
    return lax.dot_general(left, right, (((1,), (0,)), ((), ())), preferred_element_type=F32)


def dot_t(left, right):
    return lax.dot_general(left, right, (((1,), (1,)), ((), ())), preferred_element_type=F32)


def half_turn(value):
    return pltpu.roll(value, 64, 1)


def copy_all(pairs, sems):
    copies = [pltpu.make_async_copy(source, target, sems.at[i]) for i, (source, target) in enumerate(pairs)]
    for copy in copies:
        copy.start()

    def wait():
        for copy in copies:
            copy.wait()

    return wait


def pack_row(matrix, inverse, links, j, put):
    packed = jnp.concatenate([inverse[16 * t:16 * t + 16, :] for t in range(4)], axis=1)
    lane = lanes((8, 256))
    tail = jnp.zeros((8, 256), F32)
    for l in range(links.shape[1]):
        tail = jnp.where(lane == l, links[j, l].astype(F32), tail)
    put(0, matrix)
    put(64, packed)
    put(80, tail)


def begin_kernel(r_in, b_in, e_in, n_in, first, second, r, b, e, n, sems):
    copy_all([(r_in, r), (b_in, b), (e_in, e), (n_in, n)], sems)()
    grid_rows = b.shape[0]
    line, _ = place()
    even = lax.rem(line, 2) == 0

    def message(start, north_start):
        parts = [r[a, start:start + HALO, :] for a in range(r.shape[0])]
        parts += [b[start:start + HALO, :], e[start:start + HALO, :]]
        parts += [n[north_start:north_start + HALO + 1, :], jnp.zeros((2, b.shape[1]), F32)]
        return parts

    top = message(0, 0)
    bottom = message(grid_rows - HALO, grid_rows - HALO - 1)
    at = 0
    for low, high in zip(top, bottom):
        size = low.shape[0]
        first[at:at + size, :] = jnp.where(even, high, low)
        second[at:at + size, :] = jnp.where(even, low, high)
        at += size


def pack_kernel(owned, links_in, coupling_in, inverses_in, after, own, block, links, coupling, inverses, sems):
    del after
    q = lax.rem(lax.axis_index("narrow"), owned)
    copy_all([(links_in, links), (coupling_in, coupling), (inverses_in, inverses)], sems)()
    for j_rel in range(owned):
        j = jnp.bitwise_xor(q, j_rel)

        def put(at, value, base=j_rel * PIECE):
            block[base + at:base + at + value.shape[0], :] = value
            if base == 0:
                own[at:at + value.shape[0], :] = value

        pack_row(coupling[j], inverses[j], links, j, put)


def prepare_kernel(owned, coarse_rows, r_in, b_in, e_in, n_in, support_in, basis_in,
                   r_out, b_out, e_out, n_out, basis_high, basis_low, hots, sup_hots,
                   support, basis, sems, basis_sems):
    q = lax.rem(lax.axis_index("narrow"), owned)
    mine = lax.axis_index("wide") * owned + q
    wait = copy_all([(r_in, r_out), (b_in, b_out), (e_in, e_out), (n_in, n_out), (support_in, support)], sems)
    parts = basis_sems.shape[0]
    part = basis.shape[0] // parts
    copies = [pltpu.make_async_copy(basis_in.at[pl.ds(part * i, part)], basis.at[pl.ds(part * i, part)],
                                    basis_sems.at[i]) for i in range(parts)]
    for copy in copies:
        copy.start()
    wait()

    blocks = support.shape[1]
    rows4 = 4 * blocks
    size = 4 * coarse_rows

    def chosen(which, index):
        g, h = lax.shift_right_logical(index, 4), jnp.bitwise_and(lax.shift_right_logical(index, 3), 1)
        p = jnp.bitwise_and(lax.shift_right_logical(index, 2), 1)
        return jnp.where(which == g * 4 + p * 2 + h, 1.0, 0.0).astype(BF16)

    value = support[...].astype(F32).astype(BF16)
    column = dot_t(chosen(lanes((rows4, blocks)), rows((rows4, blocks))), value)
    line = dot(value, chosen(rows((blocks, rows4)), lanes((blocks, rows4))))
    line = line.astype(jnp.int32) * 4 + jnp.bitwise_and(lanes((4, rows4)), 3)
    at = rows((size, rows4))
    for k in range(4):
        base, left = (k % 2) * size, (k // 2) * rows4
        hots[base:base + size, left:left + rows4] = jnp.where(at == line[k:k + 1, :], 1.0, 0.0).astype(BF16)
    column = jnp.bitwise_xor(column.astype(jnp.int32), mine) * 4 + jnp.bitwise_and(rows((rows4, 4)), 3)
    across = lanes((rows4, size))
    for k in range(4):
        sup_hots[rows4 * k:rows4 * k + rows4, :] = jnp.where(across == column[:, k:k + 1], 1.0, 0.0).astype(BF16)

    for i in range(parts):
        copies[i].wait()
        for at in range(part * i, part * i + part, 256):
            basis_high[at:at + 256, :], basis_low[at:at + 256, :] = split(basis[at:at + 256, :])


def stack_kernel(*refs):
    fetched, gathered = refs[:-4], refs[-1]
    for i, piece in enumerate(fetched):
        gathered[PIECE * i:PIECE * i + PIECE, :] = piece[...]


class Fine:
    def __init__(self, r, b, e, n, from_first, from_second, rx, bx, ex, nx, field):
        line, count = place()
        even = lax.rem(line, 2) == 0
        low_ok, high_ok = line > 0, line < count - 1
        one, two = from_first[...], from_second[...]
        low = jnp.where(low_ok, jnp.where(even, two, one), 0.0)
        high = jnp.where(high_ok, jnp.where(even, one, two), 0.0)
        self.even, self.low_ok, self.high_ok = even, low_ok, high_ok
        self.adjoints, self.grid_rows, width = r.shape
        top = HALO + self.grid_rows
        zeros = jnp.zeros((8, width), F32)
        for a in range(self.adjoints):
            rx[a, 16:24, :] = zeros
            rx[a, 0:HALO, :] = low[3 * a:3 * a + 3]
            rx[a, HALO:top, :] = r[a]
            rx[a, top:top + HALO, :] = high[3 * a:3 * a + 3]
            field[a, 0:8, :] = zeros
            field[a, 32:40, :] = zeros
        bx[16:24, :] = zeros
        bx[0:HALO, :] = low[12:15]
        bx[HALO:top, :] = b[...]
        bx[top:top + HALO, :] = high[12:15]
        ex[16:24, :] = zeros
        ex[0:HALO, :] = low[15:18]
        ex[HALO:top, :] = e[...]
        ex[top:top + HALO, :] = high[15:18]
        nx[16:24, :] = zeros
        nx[24:32, :] = zeros
        nx[0:HALO + 1, :] = low[18:22]
        nx[HALO + 1:top + 1, :] = n[...]
        nx[top + 1:top + 1 + HALO, :] = high[18:21]
        self.r = rx[...]
        self.east = ex[...]
        self.north = nx[1:1 + FIELD, :]
        self.south = nx[0:FIELD, :]
        self.west = pltpu.roll(self.east, 1, 1)
        self.diagonal = bx[...] + self.east + self.west + self.north + self.south
        t = rows((FIELD, width))
        valid = ((t >= HALO) | low_ok) & ((t < top) | high_ok) & (t < top + HALO)
        self.scale = jnp.where(valid, relax_weight / jnp.where(valid, self.diagonal, 1.0), 0.0)
        self.field = field
        self.width = width

    def apply(self, x):
        self.field[:, 8:32, :] = x
        above = self.field[:, 7:31, :]
        below = self.field[:, 9:33, :]
        east = pltpu.roll(x, self.width - 1, 2)
        west = pltpu.roll(x, 1, 2)
        return self.diagonal * x - self.north * below - self.south * above - self.east * east - self.west * west

    def sweep(self, x):
        return x + self.scale * (self.r - self.apply(x))


def fine_scratch(adjoints, width):
    return [
        pltpu.VMEM((adjoints, FIELD, width), F32),
        pltpu.VMEM((FIELD, width), F32),
        pltpu.VMEM((FIELD, width), F32),
        pltpu.VMEM((32, width), F32),
        pltpu.VMEM((adjoints, 40, width), F32),
    ]


def restrict_kernel(coarse_rows, r, b, e, n, from_first, from_second, basis_high, basis_low, hots, *refs):
    out, x_out, rx, bx, ex, nx, field, by_row, contrib = refs[-9:]
    fine = Fine(r, b, e, n, from_first, from_second, rx, bx, ex, nx, field)
    x = fine.scale * fine.r
    for step in range(SWEEPS - 1):
        x = fine.sweep(x)
    resid = fine.r - fine.apply(x)
    for a in range(fine.adjoints):
        x_out[a] = field[a, 8 + HALO:8 + HALO + fine.grid_rows, :]
    field[:, 8:32, :] = resid
    for a in range(fine.adjoints):
        by_row[pl.ds(a, fine.grid_rows, stride=4), :] = field[a, 8 + HALO:8 + HALO + fine.grid_rows, :]
    left = lanes((8, 128)) < 64
    upper = rows((8, 128)) < 4
    for g in range(fine.grid_rows // 2):
        z = by_row[8 * g:8 * g + 8, :]
        parts = []
        for here in (left, ~left):
            held = jnp.where(here, z, 0.0)
            parts.append(jnp.concatenate([jnp.where(upper, held, 0.0), jnp.where(upper, 0.0, held)], axis=1))
        high, low = split(jnp.concatenate(parts, axis=0))
        near = slice(256 * g, 256 * g + 256)
        both = dot(jnp.concatenate([high, low], axis=0), basis_high[near, :])
        contrib[16 * g:16 * g + 16, :] = both[0:16] + both[16:32] + dot(high, basis_low[near, :])
    c_high, c_low = split(contrib[...])
    weights = jnp.concatenate([
        jnp.concatenate([c_high[:, 0:128], c_low[:, 0:128]], axis=1),
        jnp.concatenate([c_high[:, 128:256], c_low[:, 128:256]], axis=1)], axis=0)
    size = 4 * coarse_rows
    total = dot(hots[...], weights)
    total = total[:, 0:128] + total[:, 128:256]
    here = lanes((size, 128)) < 64
    even = jnp.where(here, total[0:size], 0.0)
    odd = jnp.where(here, 0.0, total[size:2 * size])
    mid = size // 2
    out[...] = even[0:mid] + half_turn(odd[0:mid]) + half_turn(even[mid:size]) + odd[mid:size]


def coarse_kernel(owned, coarse_rows, zs, refs):
    refs = list(refs)

    def take(count):
        got = refs[:count]
        del refs[:count]
        return got

    (rhs_ref,) = take(1)
    pieces = take(2 * (1 + owned))
    basis_high, basis_low, sup_hots, x_ref = take(4)
    y_ref, coarse_ref, first, second = take(4)
    w_high, w_low, w_inv, link_rows, hots, product, u_ref, by_row = refs
    size = 4 * coarse_rows
    wide, narrow = lax.axis_index("wide"), lax.axis_index("narrow")
    q = lax.rem(narrow, owned)
    mine = wide * owned + q

    lane16 = lanes((16, 128)) < 64
    for z_rel in range(zs):
        for c_rel in range(2):
            for j_rel in range(owned):
                i = (z_rel * 2 + c_rel) * owned + j_rel
                if z_rel == 0:
                    piece, base = pieces[c_rel * (1 + owned)], j_rel * PIECE
                else:
                    piece, base = pieces[c_rel * (1 + owned) + 1 + j_rel], (z_rel - 1) * PIECE
                high, low = split(piece[base:base + 64, :])
                w_high[64 * i:64 * i + 64, :] = high
                w_low[64 * i:64 * i + 64, :] = low
                quarters = []
                for half in range(2):
                    packed = piece[base + 64:base + 80, 128 * half:128 * half + 128]
                    turned = half_turn(packed)
                    quarters += [jnp.where(lane16, packed, turned), jnp.where(lane16, turned, packed)]
                high, low = split(jnp.concatenate(quarters, axis=0))
                w_inv[64 * i:64 * i + 64, 0:128] = high
                w_inv[64 * i:64 * i + 64, 128:256] = low
                link_rows[4 * i:4 * i + 4, :] = piece[base + 80:base + 84, 0:128]

    lane = lanes((size, size))
    a_col = jnp.bitwise_and(rows((size, 1)), 3)
    for l in range(4):
        target = jnp.bitwise_xor(link_rows[:, l:l + 1].astype(jnp.int32), mine) * 4 + a_col
        hots[size * l:size * l + size, :] = jnp.where(lane == target, 1.0, 0.0).astype(BF16)

    here = lanes((size, 128)) < 64
    packed = rhs_ref[...]
    turned = half_turn(packed)
    here_mid = here[0:size // 2]
    rhs = jnp.concatenate([jnp.where(here_mid, packed, turned), jnp.where(here_mid, turned, packed)], axis=0)

    def hi_lo(value):
        high, low = split(value)
        return jnp.concatenate([high, low], axis=1)

    source = jnp.bitwise_xor(rows((size, 1)), mine * 4)
    order = jnp.where(lane == source, 1.0, 0.0).astype(BF16)
    rhs = dot(order, hi_lo(rhs))
    rhs = rhs[:, 0:128] + rhs[:, 128:256]

    own_block = jnp.bitwise_and(lax.shift_right_logical(rows((size, 256)), 2), 3) == lax.shift_right_logical(
        lanes((size, 256)), 6)

    def fold():
        value = jnp.where(own_block, product[...], 0.0)
        value = value[:, 0:128] + value[:, 128:256]
        return value + half_turn(value)

    def apply_inverse(value):
        high, low = split(value)
        mixed = jnp.where(here, high.astype(F32), low.astype(F32)).astype(BF16)
        mixed = jnp.concatenate([mixed, mixed], axis=1)
        for g in range(coarse_rows // 4):
            product[16 * g:16 * g + 16, :] = dot_t(mixed[16 * g:16 * g + 16], w_inv[256 * g:256 * g + 256, :])
        return fold()

    def pick(got, step):
        sel = lanes((step, 128)) < 64
        high = [jnp.where(sel, got[step * k:step * k + step, 0:128], got[step * k + step:step * k + 2 * step, 0:128])
                for k in (0, 2)]
        low = [jnp.where(sel, got[step * k:step * k + step, 128:256],
                         got[step * k + step:step * k + 2 * step, 128:256]) for k in (0, 2)]
        return jnp.concatenate(high, axis=1).astype(BF16), jnp.concatenate(low, axis=1).astype(BF16)

    u = apply_inverse(rhs)
    for step in range(COARSE_SWEEPS):
        high, low = pick(dot(hots[...], hi_lo(u)), size)
        for g in range(coarse_rows // 4):
            near = slice(16 * g, 16 * g + 16)
            block = slice(256 * g, 256 * g + 256)
            both = dot_t(jnp.concatenate([high[near], low[near]], axis=0), w_high[block, :])
            product[near, :] = both[0:16] + both[16:32] + dot_t(high[near], w_low[block, :])
        u = apply_inverse(rhs + fold())

    u_ref[...] = u[0:4 * owned]
    here1 = lanes((1, 128)) < 64
    for j in range(owned):
        got = u_ref[pl.ds(jnp.bitwise_xor(q, j) * 4, 4), :]
        coarse_ref[j:j + 1, 0:128] = jnp.where(here1, got[0:1], got[1:2])
        coarse_ref[j:j + 1, 128:256] = jnp.where(here1, got[2:3], got[3:4])

    blocks4 = sup_hots.shape[0] // 4
    high, low = pick(dot(sup_hots[...], hi_lo(u)), blocks4)
    left = lanes((8, 128)) < 64
    upper = rows((8, 128)) < 4
    for g in range(blocks4 // 16):
        near = slice(16 * g, 16 * g + 16)
        block = slice(256 * g, 256 * g + 256)
        both = dot_t(jnp.concatenate([high[near], low[near]], axis=0), basis_high[block, :])
        got = both[0:16] + both[16:32] + dot_t(high[near], basis_low[block, :])
        halves = [jnp.where(upper, got[8 * h:8 * h + 8, 0:128], got[8 * h:8 * h + 8, 128:256]) for h in range(2)]
        by_row[8 * g:8 * g + 8, :] = jnp.where(left, halves[0], halves[1])
    line, _ = place()
    even = lax.rem(line, 2) == 0
    adjoints, grid_rows, _ = x_ref.shape
    for a in range(adjoints):
        y = x_ref[a] + by_row[pl.ds(a, grid_rows, stride=4), :]
        y_ref[a] = y
        top, bottom = y[0:2], y[grid_rows - 2:grid_rows]
        first[2 * a:2 * a + 2, :] = jnp.where(even, bottom, top)
        second[2 * a:2 * a + 2, :] = jnp.where(even, top, bottom)


def post_kernel(r, b, e, n, from_first, from_second, y_ref, y_first, y_second, out, rx, bx, ex, nx, field, yx):
    fine = Fine(r, b, e, n, from_first, from_second, rx, bx, ex, nx, field)
    one, two = y_first[...], y_second[...]
    low = jnp.where(fine.low_ok, jnp.where(fine.even, two, one), 0.0)
    high = jnp.where(fine.high_ok, jnp.where(fine.even, one, two), 0.0)
    top = HALO + fine.grid_rows
    for a in range(fine.adjoints):
        yx[a, 0:8, :] = jnp.zeros((8, fine.width), F32)
        yx[a, 16:24, :] = jnp.zeros((8, fine.width), F32)
        yx[a, HALO - 2:HALO, :] = low[2 * a:2 * a + 2]
        yx[a, HALO:top, :] = y_ref[a]
        yx[a, top:top + 2, :] = high[2 * a:2 * a + 2]
    x = yx[...]
    for step in range(SWEEPS):
        x = fine.sweep(x)
    field[:, 8:32, :] = x
    for a in range(fine.adjoints):
        out[a] = field[a, 8 + HALO:8 + HALO + fine.grid_rows, :]


def shape(*dims, kind=F32):
    return jax.ShapeDtypeStruct(dims, kind)


def params(mebibytes):
    return pltpu.CompilerParams(vmem_limit_bytes=mebibytes * 2 ** 20)


def stay(array):
    return pltpu.with_memory_space_constraint(array, pltpu.HBM)


CHEAP = pl.CostEstimate(flops=1, bytes_accessed=1, transcendentals=0)


def body(right_sides, brinkman, east_faces, north_faces, support, basis, links, coarse_block_inverses, coarse_coupling):
    adjoints, grid_rows, width = right_sides.shape
    blocks, block_size, _ = basis.shape
    owned = coarse_block_inverses.shape[0]
    coarse_rows = owned * lax.axis_size("wide")
    zs = lax.axis_size("wide") // 2
    size = 4 * coarse_rows
    basis = basis.reshape(blocks * block_size, -1)

    in_hbm = pl.BlockSpec(memory_space=pltpu.HBM)
    anywhere = pl.BlockSpec(memory_space=pl.ANY)
    in_vmem = pl.BlockSpec(memory_space=pltpu.VMEM)
    row_dims = (grid_rows, width)
    message = shape(24, width)
    fine_inputs = tuple(map(stay, (right_sides, brinkman, east_faces, north_faces)))
    coarse_inputs = tuple(map(stay, (links, coarse_coupling, coarse_block_inverses)))
    to_first, to_second = pl.pallas_call(
        begin_kernel,
        out_shape=(message, message),
        in_specs=[in_hbm] * 4,
        scratch_shapes=[
            pltpu.VMEM((adjoints, *row_dims), F32), pltpu.VMEM(row_dims, F32), pltpu.VMEM(row_dims, F32),
            pltpu.VMEM(row_dims, F32), pltpu.SemaphoreType.DMA((4,))],
        cost_estimate=CHEAP, compiler_params=params(16), name="begin",
    )(*fine_inputs)
    from_first, from_second = pair_swaps(to_first, to_second)

    own, block = pl.pallas_call(
        functools.partial(pack_kernel, owned),
        out_shape=(shape(PIECE, 256), shape(owned * PIECE, 256)),
        in_specs=[in_hbm] * 3 + [anywhere],
        scratch_shapes=[
            pltpu.SMEM(links.shape, jnp.int32), pltpu.VMEM(coarse_coupling.shape, F32),
            pltpu.VMEM(coarse_block_inverses.shape, F32), pltpu.SemaphoreType.DMA((3,))],
        cost_estimate=CHEAP, compiler_params=params(16), name="pack",
    )(*coarse_inputs, to_first)
    fetched = [swap(own, "wide", 2 * k) for k in range(1, zs)]

    rows4 = adjoints * blocks
    r, b, e, n, basis_high, basis_low, hots, sup_hots = pl.pallas_call(
        functools.partial(prepare_kernel, owned, coarse_rows),
        out_shape=(shape(adjoints, *row_dims), shape(*row_dims), shape(*row_dims),
                   shape(*row_dims), shape(*basis.shape, kind=BF16), shape(*basis.shape, kind=BF16),
                   shape(2 * size, 2 * rows4, kind=BF16), shape(4 * rows4, size, kind=BF16)),
        in_specs=[in_hbm] * 6,
        scratch_shapes=[
            pltpu.VMEM((4, blocks), jnp.int32),
            pltpu.VMEM(basis.shape, F32), pltpu.SemaphoreType.DMA((5,)), pltpu.SemaphoreType.DMA((4,))],
        cost_estimate=CHEAP, compiler_params=params(24), name="prepare",
    )(*fine_inputs, stay(support.T), stay(basis))

    gathered = pl.pallas_call(
        stack_kernel, out_shape=shape((zs - 1) * PIECE, 256),
        in_specs=[in_vmem] * (zs - 1) + [anywhere] * 3,
        cost_estimate=CHEAP, compiler_params=params(4), name="stack",
    )(*fetched, from_first, from_second, hots)
    spread = [swap(gathered, "narrow", k) for k in range(1, owned)]

    rhs, x = pl.pallas_call(
        functools.partial(restrict_kernel, coarse_rows),
        out_shape=(shape(size // 2, 128), shape(adjoints, *row_dims)),
        scratch_shapes=fine_scratch(adjoints, width) + [
            pltpu.VMEM((4 * grid_rows, width), F32), pltpu.VMEM((rows4, 256), F32)],
        in_specs=[in_vmem] * 9 + [anywhere],
        cost_estimate=CHEAP, compiler_params=params(16), name="restrict",
    )(r, b, e, n, from_first, from_second, basis_high, basis_low, hots, gathered)

    rhs = rhs + swap(rhs, "wide", 1)
    for bit in bits_of(zs):
        rhs = rhs + swap(rhs, "wide", 2 * bit)
    block, gathered_late = tie([block, gathered], rhs)
    block_other = swap(block, "wide", 1)
    gathered_other = swap(gathered_late, "wide", 1)
    spread = tie(spread, rhs)
    for masks in rounds_of(lax.axis_size("narrow")):
        rhs = sum([swap(rhs, "narrow", k) for k in masks], rhs)
    pieces = [block, gathered_late] + spread + [block_other, gathered_other] + [swap(piece, "wide", 1) for piece in spread]

    def coarse_body(*refs):
        coarse_kernel(owned, coarse_rows, zs, refs)

    y, coarse, y_first, y_second = pl.pallas_call(
        coarse_body,
        out_shape=(shape(adjoints, *row_dims), shape(owned, 256), shape(8, width), shape(8, width)),
        scratch_shapes=[
            pltpu.VMEM((64 * coarse_rows, 256), BF16), pltpu.VMEM((64 * coarse_rows, 256), BF16),
            pltpu.VMEM((64 * coarse_rows, 256), BF16), pltpu.VMEM((size, 128), F32),
            pltpu.VMEM((4 * size, size), BF16), pltpu.VMEM((size, 256), F32),
            pltpu.VMEM((4 * owned, 128), F32), pltpu.VMEM((4 * grid_rows, width), F32)],
        cost_estimate=CHEAP, compiler_params=params(min(48, 8 + coarse_rows // 3)), name="coarse",
    )(rhs, *pieces, basis_high, basis_low, sup_hots, x)

    y_first, y_second = pair_swaps(y_first, y_second)
    solution_field = pl.pallas_call(
        post_kernel,
        out_shape=shape(adjoints, grid_rows, width),
        scratch_shapes=fine_scratch(adjoints, width) + [pltpu.VMEM((adjoints, FIELD, width), F32)],
        cost_estimate=CHEAP, compiler_params=params(16), name="post",
    )(r, b, e, n, from_first, from_second, y, y_first, y_second)
    return solution_field, coarse


def solution(mesh):
    return jax.shard_map(
        body,
        mesh=mesh,
        in_specs=(
            P(None, ("wide", "narrow"), None),
            P(("wide", "narrow"), None),
            P(("wide", "narrow"), None),
            P(("wide", "narrow"), None),
            P(("wide", "narrow"), None),
            P(("wide", "narrow"), None, None),
            P("wide", None),
            P("wide", None, None),
            P("wide", None, None),
        ),
        out_specs=(P(None, ("wide", "narrow"), None), P("wide", None)),
        check_vma=False,
    )
```

```python
import functools

import jax
import jax.numpy as jnp
from jax import lax
from jax.experimental import pallas as pl
from jax.experimental.pallas import tpu as pltpu
from jax.sharding import PartitionSpec as P

SWEEPS = 2
COARSE_SWEEPS = 3
relax_weight = 0.7

BOTH = ("wide", "narrow")
HALO = 3
FIELD = 24
PIECE = 80
F32 = jnp.float32
BF16 = jnp.bfloat16


def swap(value, axis, bits):
    size = lax.axis_size(axis)
    return lax.ppermute(value, axis, [(i, i ^ bits) for i in range(size)])


def pair_swaps(to_first, to_second):
    count = lax.axis_size(BOTH)
    first = lax.ppermute(to_first, BOTH, [(i, i ^ 1) for i in range(count)])
    odd = [(i, i + 1) for i in range(1, count - 1, 2)] + [(count - 1, 0)]
    second = lax.ppermute(to_second, BOTH, odd + [(target, source) for source, target in odd])
    return first, second


def pair_swaps_near(to_first, to_second):
    count = lax.axis_size(BOTH)
    first = lax.ppermute(to_first, BOTH, [(i, i ^ 1) for i in range(count)])
    inner = lax.ppermute(to_second, BOTH, [(i, i ^ 3) for i in range(count)])
    outer = [(i, i + 1) for i in range(3, count - 1, 4)]
    rest = sorted(set(range(count)) - {i for pair in outer for i in pair})
    outer += list(zip(rest[::2], rest[1::2]))
    outer = lax.ppermute(to_second, BOTH, outer + [(target, source) for source, target in outer])
    return first, inner, outer


def tie(values, after):
    count = len(values)
    spec = pl.BlockSpec(memory_space=pl.ANY)
    return list(pl.pallas_call(
        lambda *refs: None, out_shape=[jax.ShapeDtypeStruct(v.shape, v.dtype) for v in values],
        in_specs=[spec] * (count + 1), out_specs=[spec] * count,
        input_output_aliases={i: i for i in range(count)}, cost_estimate=CHEAP, compiler_params=params(1), name="tie",
    )(*values, after))


def rounds_of(size):
    rounds, base = [], 1
    while base < size:
        span = 4 if base * 4 <= size else 2
        rounds.append([base * k for k in range(1, span)])
        base *= span
    return rounds


def bits_of(size):
    return [1 << i for i in range(size.bit_length() - 1)]


def place():
    wide, narrow = lax.axis_index("wide"), lax.axis_index("narrow")
    line = wide * lax.axis_size("narrow") + narrow
    count = lax.axis_size("wide") * lax.axis_size("narrow")
    return line, count


def packed_rows(count):
    return count * PIECE + 8 * ((count + 7) // 8)


def lanes(shape):
    return lax.broadcasted_iota(jnp.int32, shape, len(shape) - 1)


def rows(shape):
    return lax.broadcasted_iota(jnp.int32, shape, len(shape) - 2)


def split(value):
    high = value.astype(BF16)
    return high, (value - high.astype(F32)).astype(BF16)


def dot(left, right):
    return lax.dot_general(left, right, (((1,), (0,)), ((), ())), preferred_element_type=F32)


def dot_t(left, right):
    return lax.dot_general(left, right, (((1,), (1,)), ((), ())), preferred_element_type=F32)


def half_turn(value):
    return pltpu.roll(value, 64, 1)


def copy_all(pairs, sems):
    copies = [pltpu.make_async_copy(source, target, sems.at[i]) for i, (source, target) in enumerate(pairs)]
    for copy in copies:
        copy.start()

    def wait():
        for copy in copies:
            copy.wait()

    return wait


def pack_row(matrix, inverse, put):
    put(0, matrix)
    put(64, jnp.concatenate([inverse[16 * t:16 * t + 16, :] for t in range(4)], axis=1))


def begin_kernel(owned, r_in, b_in, e_in, n_in, links_in, coupling_in, inverses_in, first, second, own, block,
                 r, b, e, n, links, coupling, inverses, sems):
    wait = copy_all([(r_in, r), (b_in, b), (e_in, e), (n_in, n), (links_in, links), (coupling_in, coupling),
                     (inverses_in, inverses)], sems)
    grid_rows = b.shape[0]
    line, _ = place()
    even = lax.rem(line, 2) == 0
    q = lax.rem(lax.axis_index("narrow"), owned)
    wait()

    def message(start, north_start):
        parts = [r[a, start:start + HALO, :] for a in range(r.shape[0])]
        parts += [b[start:start + HALO, :], e[start:start + HALO, :]]
        parts += [n[north_start:north_start + HALO + 1, :], jnp.zeros((2, b.shape[1]), F32)]
        return parts

    top = message(0, 0)
    bottom = message(grid_rows - HALO, grid_rows - HALO - 1)
    at = 0
    for low, high in zip(top, bottom):
        size = low.shape[0]
        first[at:at + size, :] = jnp.where(even, high, low)
        second[at:at + size, :] = jnp.where(even, low, high)
        at += size

    lane, row = lanes((8, 256)), rows((8, 256))
    tail = jnp.zeros((8, 256), F32)
    for j_rel in range(owned):
        j = jnp.bitwise_xor(q, j_rel)

        def put(at, value, base=j_rel * PIECE):
            block[base + at:base + at + value.shape[0], :] = value
            if base == 0:
                own[at:at + value.shape[0], :] = value

        pack_row(coupling[j], inverses[j], put)
        for l in range(links.shape[1]):
            tail = jnp.where((row == j_rel) & (lane == l), links[j, l].astype(F32), tail)
    block[owned * PIECE:owned * PIECE + 8, :] = tail
    own[PIECE:PIECE + 8, :] = tail


def prepare_kernel(owned, coarse_rows, r_in, b_in, e_in, n_in, support_in, basis_in,
                   r_out, b_out, e_out, n_out, basis, hots, sup_hots, support, sems):
    q = lax.rem(lax.axis_index("narrow"), owned)
    mine = lax.axis_index("wide") * owned + q
    wait_support = copy_all([(support_in, support)], sems.at[pl.ds(0, 1)])
    part = basis.shape[0] // 8
    parts = [pl.ds(part * i, part) for i in range(8)]
    wait = copy_all([(basis_in.at[at], basis.at[at]) for at in parts]
                    + [(r_in, r_out), (b_in, b_out), (e_in, e_out), (n_in, n_out)], sems.at[pl.ds(1, 12)])
    wait_support()

    blocks = support.shape[1]
    rows4 = 4 * blocks
    size = 4 * coarse_rows

    def chosen(which, index):
        g, h = lax.shift_right_logical(index, 4), jnp.bitwise_and(lax.shift_right_logical(index, 3), 1)
        p = jnp.bitwise_and(lax.shift_right_logical(index, 2), 1)
        return jnp.where(which == g * 4 + p * 2 + h, 1.0, 0.0).astype(BF16)

    value = support[...].astype(F32).astype(BF16)
    column = dot_t(chosen(lanes((rows4, blocks)), rows((rows4, blocks))), value)
    line = dot(value, chosen(rows((blocks, rows4)), lanes((blocks, rows4))))
    line = line.astype(jnp.int32) * 4 + jnp.bitwise_and(lanes((4, rows4)), 3)
    at = rows((size, rows4))
    for k in range(4):
        base, left = (k % 2) * size, (k // 2) * rows4
        hots[base:base + size, left:left + rows4] = jnp.where(at == line[k:k + 1, :], 1.0, 0.0).astype(BF16)
    column = jnp.bitwise_xor(column.astype(jnp.int32), mine) * 4 + jnp.bitwise_and(rows((rows4, 4)), 3)
    across = lanes((rows4, size))
    for k in range(4):
        sup_hots[rows4 * k:rows4 * k + rows4, :] = jnp.where(across == column[:, k:k + 1], 1.0, 0.0).astype(BF16)

    wait()


def stack_kernel(*refs):
    fetched, gathered = refs[:-4], refs[-1]
    count = len(fetched)
    gathered[count * PIECE:, :] = jnp.zeros((gathered.shape[0] - count * PIECE, gathered.shape[1]), F32)
    for i, piece in enumerate(fetched):
        gathered[PIECE * i:PIECE * i + PIECE, :] = piece[0:PIECE, :]
        gathered[PIECE * count + i:PIECE * count + i + 1, :] = piece[PIECE:PIECE + 1, :]


def add_kernel(one, two, out):
    half = out.shape[0] // 2
    for i in range(2):
        block = slice(128 * i, 128 * i + 128)
        out[half * i:half * i + half, :] = one[0:half, block] + two[0:half, block]


class Fine:
    def __init__(self, r, b, e, n, from_first, from_second, rx, bx, ex, nx, field):
        line, count = place()
        even = lax.rem(line, 2) == 0
        low_ok, high_ok = line > 0, line < count - 1
        one, two = from_first[...], from_second[...]
        low = jnp.where(low_ok, jnp.where(even, two, one), 0.0)
        high = jnp.where(high_ok, jnp.where(even, one, two), 0.0)
        self.even, self.low_ok, self.high_ok = even, low_ok, high_ok
        self.adjoints, self.grid_rows, width = r.shape
        top = HALO + self.grid_rows
        zeros = jnp.zeros((8, width), F32)
        for a in range(self.adjoints):
            rx[a, 16:24, :] = zeros
            rx[a, 0:HALO, :] = low[3 * a:3 * a + 3]
            rx[a, HALO:top, :] = r[a]
            rx[a, top:top + HALO, :] = high[3 * a:3 * a + 3]
            field[a, 0:8, :] = zeros
            field[a, 32:40, :] = zeros
        bx[16:24, :] = zeros
        bx[0:HALO, :] = low[12:15]
        bx[HALO:top, :] = b[...]
        bx[top:top + HALO, :] = high[12:15]
        ex[16:24, :] = zeros
        ex[0:HALO, :] = low[15:18]
        ex[HALO:top, :] = e[...]
        ex[top:top + HALO, :] = high[15:18]
        nx[16:24, :] = zeros
        nx[24:32, :] = zeros
        nx[0:HALO + 1, :] = low[18:22]
        nx[HALO + 1:top + 1, :] = n[...]
        nx[top + 1:top + 1 + HALO, :] = high[18:21]
        self.r = rx[...]
        self.east = ex[...]
        self.north = nx[1:1 + FIELD, :]
        self.south = nx[0:FIELD, :]
        self.west = pltpu.roll(self.east, 1, 1)
        self.diagonal = bx[...] + self.east + self.west + self.north + self.south
        t = rows((FIELD, width))
        valid = ((t >= HALO) | low_ok) & ((t < top) | high_ok) & (t < top + HALO)
        self.scale = jnp.where(valid, relax_weight / jnp.where(valid, self.diagonal, 1.0), 0.0)
        self.field = field
        self.width = width

    def apply(self, x):
        self.field[:, 8:32, :] = x
        above = self.field[:, 7:31, :]
        below = self.field[:, 9:33, :]
        east = pltpu.roll(x, self.width - 1, 2)
        west = pltpu.roll(x, 1, 2)
        return self.diagonal * x - self.north * below - self.south * above - self.east * east - self.west * west

    def sweep(self, x):
        return x + self.scale * (self.r - self.apply(x))


    def keep(self, r_out, coef_out):
        r_out[...] = self.r
        for i, value in enumerate((self.diagonal, self.scale, self.north, self.south, self.east, self.west)):
            coef_out[i] = value


class Kept(Fine):
    def __init__(self, r, coef, field):
        line, count = place()
        self.even, self.low_ok, self.high_ok = lax.rem(line, 2) == 0, line > 0, line < count - 1
        self.r, self.field = r[...], field
        self.diagonal, self.scale, self.north, self.south, self.east, self.west = [coef[i] for i in range(6)]
        self.adjoints, _, self.width = r.shape


def fine_scratch(adjoints, width):
    return [
        pltpu.VMEM((adjoints, FIELD, width), F32),
        pltpu.VMEM((FIELD, width), F32),
        pltpu.VMEM((FIELD, width), F32),
        pltpu.VMEM((32, width), F32),
        pltpu.VMEM((adjoints, 40, width), F32),
    ]


def restrict_kernel(coarse_rows, r, b, e, n, from_first, from_second, basis, hots,
                    block, gathered, out, x_out, rx, bx, ex, nx, field, by_row, contrib):
    fine = Fine(r, b, e, n, from_first, from_second, rx, bx, ex, nx, field)
    x = fine.scale * fine.r
    for step in range(SWEEPS - 1):
        x = fine.sweep(x)
    resid = fine.r - fine.apply(x)
    for a in range(fine.adjoints):
        x_out[a] = field[a, 8 + HALO:8 + HALO + fine.grid_rows, :]
    field[:, 8:32, :] = resid
    for a in range(fine.adjoints):
        by_row[pl.ds(a, fine.grid_rows, stride=4), :] = field[a, 8 + HALO:8 + HALO + fine.grid_rows, :]
    left = lanes((8, 128)) < 64
    upper = rows((8, 128)) < 4
    for g in range(fine.grid_rows // 2):
        z = by_row[8 * g:8 * g + 8, :]
        parts = []
        for here in (left, ~left):
            held = jnp.where(here, z, 0.0)
            parts.append(jnp.concatenate([jnp.where(upper, held, 0.0), jnp.where(upper, 0.0, held)], axis=1))
        high, low = split(jnp.concatenate(parts, axis=0))
        near = slice(256 * g, 256 * g + 256)
        w_high, w_low = split(basis[near, :])
        both = dot(jnp.concatenate([high, low], axis=0), w_high)
        contrib[16 * g:16 * g + 16, :] = both[0:16] + both[16:32] + dot(high, w_low)
    c_high, c_low = split(contrib[...])
    weights = jnp.concatenate([
        jnp.concatenate([c_high[:, 0:128], c_low[:, 0:128]], axis=1),
        jnp.concatenate([c_high[:, 128:256], c_low[:, 128:256]], axis=1)], axis=0)
    size = 4 * coarse_rows
    total = dot(hots[...], weights)
    total = total[:, 0:128] + total[:, 128:256]
    here = lanes((size, 128)) < 64
    even = jnp.where(here, total[0:size], 0.0)
    odd = jnp.where(here, 0.0, total[size:2 * size])
    mid = size // 2
    packed = even[0:mid] + half_turn(odd[0:mid]) + half_turn(even[mid:size]) + odd[mid:size]
    half = mid // 2
    out[0:half, 0:128] = packed[0:half]
    out[0:half, 128:256] = packed[half:mid]
    out[half:half + block.shape[0], :] = block[...]
    out[half + block.shape[0]:, :] = gathered[...]


def prolong(group, high, low, basis):
    near = slice(16 * group, 16 * group + 16)
    block = slice(256 * group, 256 * group + 256)
    high = high[near, :]
    w_high, w_low = split(basis[block, :])
    both = dot_t(jnp.concatenate([high, low[near, :]], axis=0), w_high)
    got = both[0:16] + both[16:32] + dot_t(high, w_low)
    upper = rows((8, 128)) < 4
    halves = [jnp.where(upper, got[8 * h:8 * h + 8, 0:128], got[8 * h:8 * h + 8, 128:256]) for h in range(2)]
    return jnp.where(lanes((8, 128)) < 64, halves[0], halves[1])


def coarse_kernel(owned, coarse_rows, zs, rhs_ref, message, message_other, *refs):
    spread, spread_other = refs[:owned - 1], refs[owned - 1:2 * owned - 2]
    (basis, sup_hots, x_ref, coarse_ref, high_out, low_out, first, second,
     w_high, w_low, w_inv, link_rows, hots, product, u_ref, by_row) = refs[2 * owned - 2:]
    size = 4 * coarse_rows
    wide, narrow = lax.axis_index("wide"), lax.axis_index("narrow")
    q = lax.rem(narrow, owned)
    mine = wide * owned + q

    lane16 = lanes((16, 128)) < 64
    at_own = coarse_rows
    at_fetched = at_own + packed_rows(owned)
    for z_rel in range(zs):
        for c_rel, (fetched, others) in enumerate(((message, spread), (message_other, spread_other))):
            for j_rel in range(owned):
                i = (z_rel * 2 + c_rel) * owned + j_rel
                if z_rel == 0:
                    piece, start, index, count = fetched, at_own, j_rel, owned
                elif j_rel == 0:
                    piece, start, index, count = fetched, at_fetched, z_rel - 1, zs - 1
                else:
                    piece, start, index, count = others[j_rel - 1], 0, z_rel - 1, zs - 1
                base = start + index * PIECE
                at_links = start + count * PIECE + index
                high, low = split(piece[base:base + 64, :])
                w_high[64 * i:64 * i + 64, :] = high
                w_low[64 * i:64 * i + 64, :] = low
                quarters = []
                for half in range(2):
                    packed = piece[base + 64:base + 80, 128 * half:128 * half + 128]
                    turned = half_turn(packed)
                    quarters += [jnp.where(lane16, packed, turned), jnp.where(lane16, turned, packed)]
                high, low = split(jnp.concatenate(quarters, axis=0))
                w_inv[64 * i:64 * i + 64, 0:128] = high
                w_inv[64 * i:64 * i + 64, 128:256] = low
                link_rows[4 * i:4 * i + 4, :] = jnp.broadcast_to(piece[at_links:at_links + 1, 0:128], (4, 128))

    lane = lanes((size, size))
    a_col = jnp.bitwise_and(rows((size, 1)), 3)
    for l in range(4):
        target = jnp.bitwise_xor(link_rows[:, l:l + 1].astype(jnp.int32), mine) * 4 + a_col
        hots[size * l:size * l + size, :] = jnp.where(lane == target, 1.0, 0.0).astype(BF16)

    here = lanes((size, 128)) < 64
    packed = rhs_ref[...]
    turned = half_turn(packed)
    here_mid = here[0:size // 2]
    rhs = jnp.concatenate([jnp.where(here_mid, packed, turned), jnp.where(here_mid, turned, packed)], axis=0)

    def hi_lo(value):
        high, low = split(value)
        return jnp.concatenate([high, low], axis=1)

    source = jnp.bitwise_xor(rows((size, 1)), mine * 4)
    order = jnp.where(lane == source, 1.0, 0.0).astype(BF16)
    rhs = dot(order, hi_lo(rhs))
    rhs = rhs[:, 0:128] + rhs[:, 128:256]

    own_block = jnp.bitwise_and(lax.shift_right_logical(rows((size, 256)), 2), 3) == lax.shift_right_logical(
        lanes((size, 256)), 6)

    def fold():
        value = jnp.where(own_block, product[...], 0.0)
        value = value[:, 0:128] + value[:, 128:256]
        return value + half_turn(value)

    def apply_inverse(value):
        high, low = split(value)
        mixed = jnp.where(here, high.astype(F32), low.astype(F32)).astype(BF16)
        mixed = jnp.concatenate([mixed, mixed], axis=1)
        for g in range(coarse_rows // 4):
            product[16 * g:16 * g + 16, :] = dot_t(mixed[16 * g:16 * g + 16], w_inv[256 * g:256 * g + 256, :])
        return fold()

    def pick(got, step):
        sel = lanes((step, 128)) < 64
        high = [jnp.where(sel, got[step * k:step * k + step, 0:128], got[step * k + step:step * k + 2 * step, 0:128])
                for k in (0, 2)]
        low = [jnp.where(sel, got[step * k:step * k + step, 128:256],
                         got[step * k + step:step * k + 2 * step, 128:256]) for k in (0, 2)]
        return jnp.concatenate(high, axis=1).astype(BF16), jnp.concatenate(low, axis=1).astype(BF16)

    u = apply_inverse(rhs)
    for step in range(COARSE_SWEEPS):
        high, low = pick(dot(hots[...], hi_lo(u)), size)
        for g in range(coarse_rows // 4):
            near = slice(16 * g, 16 * g + 16)
            block = slice(256 * g, 256 * g + 256)
            both = dot_t(jnp.concatenate([high[near], low[near]], axis=0), w_high[block, :])
            product[near, :] = both[0:16] + both[16:32] + dot_t(high[near], w_low[block, :])
        u = apply_inverse(rhs + fold())

    u_ref[...] = u[0:4 * owned]
    here1 = lanes((1, 128)) < 64
    for j in range(owned):
        got = u_ref[pl.ds(jnp.bitwise_xor(q, j) * 4, 4), :]
        coarse_ref[j:j + 1, 0:128] = jnp.where(here1, got[0:1], got[1:2])
        coarse_ref[j:j + 1, 128:256] = jnp.where(here1, got[2:3], got[3:4])

    blocks4 = sup_hots.shape[0] // 4
    high, low = pick(dot(sup_hots[...], hi_lo(u)), blocks4)
    high_out[...] = high
    low_out[...] = low
    line, _ = place()
    even = lax.rem(line, 2) == 0
    adjoints, grid_rows, _ = x_ref.shape
    by_row[0:8, :] = prolong(0, high, low, basis)
    by_row[8:16, :] = prolong(grid_rows // 2 - 1, high, low, basis)
    for a in range(adjoints):
        edge = by_row[pl.ds(a, 4, stride=4), :]
        top = x_ref[a, 0:2, :] + edge[0:2]
        bottom = x_ref[a, grid_rows - 2:grid_rows, :] + edge[2:4]
        first[2 * a:2 * a + 2, :] = jnp.where(even, bottom, top)
        second[2 * a:2 * a + 2, :] = jnp.where(even, top, bottom)


def correct_kernel(r, b, e, n, from_first, from_second, x_ref, high, low, basis,
                   r_out, coef_out, y_out, rx, bx, ex, nx, field, by_row):
    Fine(r, b, e, n, from_first, from_second, rx, bx, ex, nx, field).keep(r_out, coef_out)
    adjoints, grid_rows, width = x_ref.shape
    for g in range(grid_rows // 2):
        by_row[8 * g:8 * g + 8, :] = prolong(g, high, low, basis)
    for a in range(adjoints):
        y_out[a, 0:8, :] = jnp.zeros((8, width), F32)
        y_out[a, 16:24, :] = jnp.zeros((8, width), F32)
        y_out[a, HALO:HALO + grid_rows, :] = x_ref[a] + by_row[pl.ds(a, grid_rows, stride=4), :]


def post_kernel(r, coef, y_ref, y_first, y_inner, y_outer, out, field):
    fine = Kept(r, coef, field)
    in_line = lax.rem(place()[0], 4)
    one, two = y_first[...], jnp.where((in_line == 1) | (in_line == 2), y_inner[...], y_outer[...])
    low = jnp.where(fine.low_ok, jnp.where(fine.even, two, one), 0.0)
    high = jnp.where(fine.high_ok, jnp.where(fine.even, one, two), 0.0)
    grid_rows = out.shape[1]
    start, top = 8 + HALO, 8 + HALO + grid_rows
    field[:, 0:8, :] = jnp.zeros((fine.adjoints, 8, fine.width), F32)
    field[:, 32:40, :] = jnp.zeros((fine.adjoints, 8, fine.width), F32)
    field[:, 8:32, :] = y_ref[...]
    for a in range(fine.adjoints):
        field[a, start - 2:start, :] = low[2 * a:2 * a + 2]
        field[a, top:top + 2, :] = high[2 * a:2 * a + 2]
    x = field[:, 8:32, :]
    for step in range(SWEEPS):
        x = fine.sweep(x)
    field[:, 8:32, :] = x
    for a in range(fine.adjoints):
        out[a] = field[a, start:top, :]


def shape(*dims, kind=F32):
    return jax.ShapeDtypeStruct(dims, kind)


def params(mebibytes):
    return pltpu.CompilerParams(vmem_limit_bytes=mebibytes * 2 ** 20)


def stay(array):
    return pltpu.with_memory_space_constraint(array, pltpu.HBM)


CHEAP = pl.CostEstimate(flops=1, bytes_accessed=1, transcendentals=0)


def body(right_sides, brinkman, east_faces, north_faces, support, basis, links, coarse_block_inverses, coarse_coupling):
    adjoints, grid_rows, width = right_sides.shape
    blocks, block_size, _ = basis.shape
    owned = coarse_block_inverses.shape[0]
    coarse_rows = owned * lax.axis_size("wide")
    zs = lax.axis_size("wide") // 2
    size = 4 * coarse_rows
    basis = basis.reshape(blocks * block_size, -1)

    in_hbm = pl.BlockSpec(memory_space=pltpu.HBM)
    anywhere = pl.BlockSpec(memory_space=pl.ANY)
    in_vmem = pl.BlockSpec(memory_space=pltpu.VMEM)
    row_dims = (grid_rows, width)
    message = shape(24, width)
    fine_inputs = tuple(map(stay, (right_sides, brinkman, east_faces, north_faces)))
    coarse_inputs = tuple(map(stay, (links, coarse_coupling, coarse_block_inverses)))
    to_first, to_second, own, block = pl.pallas_call(
        functools.partial(begin_kernel, owned),
        out_shape=(message, message, shape(packed_rows(1), 256), shape(packed_rows(owned), 256)),
        in_specs=[in_hbm] * 7,
        scratch_shapes=[
            pltpu.VMEM((adjoints, *row_dims), F32), pltpu.VMEM(row_dims, F32), pltpu.VMEM(row_dims, F32),
            pltpu.VMEM(row_dims, F32), pltpu.SMEM(links.shape, jnp.int32), pltpu.VMEM(coarse_coupling.shape, F32),
            pltpu.VMEM(coarse_block_inverses.shape, F32), pltpu.SemaphoreType.DMA((7,))],
        cost_estimate=CHEAP, compiler_params=params(16), name="begin",
    )(*fine_inputs, *coarse_inputs)
    from_first, from_second = pair_swaps(to_first, to_second)
    fetched = [swap(own, "wide", 2 * k) for k in range(1, zs)]

    rows4 = adjoints * blocks
    r, b, e, n, basis, hots, sup_hots = pl.pallas_call(
        functools.partial(prepare_kernel, owned, coarse_rows),
        out_shape=(shape(adjoints, *row_dims), shape(*row_dims), shape(*row_dims), shape(*row_dims),
                   shape(*basis.shape), shape(2 * size, 2 * rows4, kind=BF16), shape(4 * rows4, size, kind=BF16)),
        in_specs=[in_hbm] * 6,
        scratch_shapes=[pltpu.VMEM((4, blocks), jnp.int32), pltpu.SemaphoreType.DMA((13,))],
        cost_estimate=CHEAP, compiler_params=params(16), name="prepare",
    )(*fine_inputs, stay(support.T), stay(basis))

    gathered = pl.pallas_call(
        stack_kernel, out_shape=shape(packed_rows(zs - 1), 256),
        in_specs=[in_vmem] * (zs - 1) + [anywhere] * 3,
        cost_estimate=CHEAP, compiler_params=params(4), name="stack",
    )(*fetched, from_first, from_second, hots)
    spread = [swap(gathered, "narrow", k) for k in range(1, owned)]

    half = coarse_rows
    message, x = pl.pallas_call(
        functools.partial(restrict_kernel, coarse_rows),
        out_shape=(shape(half + packed_rows(owned) + packed_rows(zs - 1), 256), shape(adjoints, *row_dims)),
        scratch_shapes=fine_scratch(adjoints, width) + [
            pltpu.VMEM((4 * grid_rows, width), F32), pltpu.VMEM((rows4, 256), F32)],
        cost_estimate=CHEAP, compiler_params=params(16), name="restrict",
    )(r, b, e, n, from_first, from_second, basis, hots, block, gathered)

    message_other = swap(message, "wide", 1)
    rhs = pl.pallas_call(
        add_kernel, out_shape=shape(2 * half, 128), cost_estimate=CHEAP, compiler_params=params(4), name="add",
    )(message, message_other)
    for bit in bits_of(zs):
        rhs = rhs + swap(rhs, "wide", 2 * bit)
    spread = tie(spread, rhs)
    spread_other = [swap(piece, "wide", 1) for piece in spread]
    for masks in rounds_of(lax.axis_size("narrow")):
        rhs = sum([swap(rhs, "narrow", k) for k in masks], rhs)

    near = shape(rows4, 256, kind=BF16)
    coarse, high, low, y_first, y_second = pl.pallas_call(
        functools.partial(coarse_kernel, owned, coarse_rows, zs),
        out_shape=(shape(owned, 256), near, near, shape(8, width), shape(8, width)),
        scratch_shapes=[
            pltpu.VMEM((64 * coarse_rows, 256), BF16), pltpu.VMEM((64 * coarse_rows, 256), BF16),
            pltpu.VMEM((64 * coarse_rows, 256), BF16), pltpu.VMEM((size, 128), F32),
            pltpu.VMEM((4 * size, size), BF16), pltpu.VMEM((size, 256), F32),
            pltpu.VMEM((4 * owned, 128), F32), pltpu.VMEM((16, width), F32)],
        cost_estimate=CHEAP, compiler_params=params(min(48, 8 + coarse_rows // 3)), name="coarse",
    )(rhs, message, message_other, *spread, *spread_other, basis, sup_hots, x)

    y_from = pair_swaps_near(y_first, y_second)
    extended = shape(adjoints, FIELD, width)
    r, coef, y = pl.pallas_call(
        correct_kernel,
        out_shape=(extended, shape(6, FIELD, width), extended),
        scratch_shapes=fine_scratch(adjoints, width) + [pltpu.VMEM((4 * grid_rows, width), F32)],
        cost_estimate=CHEAP, compiler_params=params(16), name="correct",
    )(r, b, e, n, from_first, from_second, x, high, low, basis)
    field = pl.pallas_call(
        post_kernel,
        out_shape=shape(adjoints, *row_dims),
        scratch_shapes=[pltpu.VMEM((adjoints, 40, width), F32)],
        cost_estimate=CHEAP, compiler_params=params(16), name="post",
    )(r, coef, y, *y_from)
    return field, coarse


def solution(mesh):
    return jax.shard_map(
        body,
        mesh=mesh,
        in_specs=(
            P(None, ("wide", "narrow"), None),
            P(("wide", "narrow"), None),
            P(("wide", "narrow"), None),
            P(("wide", "narrow"), None),
            P(("wide", "narrow"), None),
            P(("wide", "narrow"), None, None),
            P("wide", None),
            P("wide", None, None),
            P("wide", None, None),
        ),
        out_specs=(P(None, ("wide", "narrow"), None), P("wide", None)),
        check_vma=False,
    )
```

```python
import functools

import jax
import jax.numpy as jnp
from jax import lax
from jax.experimental import pallas as pl
from jax.experimental.pallas import tpu as pltpu
from jax.sharding import PartitionSpec as P

SWEEPS = 2
COARSE_SWEEPS = 3
relax_weight = 0.7

BOTH = ("wide", "narrow")
HALO = 3
FIELD = 24
PIECE = 80
F32 = jnp.float32
BF16 = jnp.bfloat16


def swap(value, axis, bits):
    size = lax.axis_size(axis)
    return lax.ppermute(value, axis, [(i, i ^ bits) for i in range(size)])


def pair_swaps(to_first, to_second):
    count = lax.axis_size(BOTH)
    first = lax.ppermute(to_first, BOTH, [(i, i ^ 1) for i in range(count)])
    odd = [(i, i + 1) for i in range(1, count - 1, 2)] + [(count - 1, 0)]
    second = lax.ppermute(to_second, BOTH, odd + [(target, source) for source, target in odd])
    return first, second


def pair_swaps_near(to_first, to_second):
    count, across = lax.axis_size(BOTH), lax.axis_size("narrow")
    first = lax.ppermute(to_first, BOTH, [(i, i ^ 1) for i in range(count)])
    inner = lax.ppermute(to_second, BOTH, [(i, i ^ (3 if i % 4 in (1, 2) else across)) for i in range(count)])
    outer = [(i, i + 1) for i in range(3, count - 1, 4)]
    outer += [(i, i ^ across) for i in range(2, count, 4) if i < i ^ across]
    rest = [0] + list(range(1, count, 4)) + [count - 1]
    outer += list(zip(rest[::2], rest[1::2]))
    outer = lax.ppermute(to_second, BOTH, outer + [(target, source) for source, target in outer])
    return first, inner, outer


def tie(values, after):
    count = len(values)
    spec = pl.BlockSpec(memory_space=pl.ANY)
    return list(pl.pallas_call(
        lambda *refs: None, out_shape=[jax.ShapeDtypeStruct(v.shape, v.dtype) for v in values],
        in_specs=[spec] * (count + 1), out_specs=[spec] * count,
        input_output_aliases={i: i for i in range(count)}, cost_estimate=CHEAP, compiler_params=params(1), name="tie",
    )(*values, after))


def rounds_of(size):
    rounds, base = [], 1
    while base < size:
        span = 4 if base * 4 <= size else 2
        rounds.append([base * k for k in range(1, span)])
        base *= span
    return rounds


def bits_of(size):
    return [1 << i for i in range(size.bit_length() - 1)]


def place():
    wide, narrow = lax.axis_index("wide"), lax.axis_index("narrow")
    line = wide * lax.axis_size("narrow") + narrow
    count = lax.axis_size("wide") * lax.axis_size("narrow")
    return line, count


def packed_rows(count):
    return count * PIECE + 8 * ((count + 7) // 8)


def lanes(shape):
    return lax.broadcasted_iota(jnp.int32, shape, len(shape) - 1)


def rows(shape):
    return lax.broadcasted_iota(jnp.int32, shape, len(shape) - 2)


def split(value):
    high = value.astype(BF16)
    return high, (value - high.astype(F32)).astype(BF16)


def dot(left, right):
    return lax.dot_general(left, right, (((1,), (0,)), ((), ())), preferred_element_type=F32)


def dot_t(left, right):
    return lax.dot_general(left, right, (((1,), (1,)), ((), ())), preferred_element_type=F32)


def half_turn(value):
    return pltpu.roll(value, 64, 1)


def copy_all(pairs, sems):
    copies = [pltpu.make_async_copy(source, target, sems.at[i]) for i, (source, target) in enumerate(pairs)]
    for copy in copies:
        copy.start()

    def wait():
        for copy in copies:
            copy.wait()

    return wait


def pack_row(matrix, inverse, put):
    put(0, matrix)
    put(64, jnp.concatenate([inverse[16 * t:16 * t + 16, :] for t in range(4)], axis=1))


def begin_kernel(owned, r_in, b_in, e_in, n_in, links_in, coupling_in, inverses_in, first, second, own, block,
                 r, b, e, n, links, coupling, inverses, sems):
    wait = copy_all([(r_in, r), (b_in, b), (e_in, e), (n_in, n), (links_in, links), (coupling_in, coupling),
                     (inverses_in, inverses)], sems)
    grid_rows = b.shape[0]
    line, _ = place()
    even = lax.rem(line, 2) == 0
    q = lax.rem(lax.axis_index("narrow"), owned)
    wait()

    def message(start, north_start):
        parts = [r[a, start:start + HALO, :] for a in range(r.shape[0])]
        parts += [b[start:start + HALO, :], e[start:start + HALO, :]]
        parts += [n[north_start:north_start + HALO + 1, :], jnp.zeros((2, b.shape[1]), F32)]
        return parts

    top = message(0, 0)
    bottom = message(grid_rows - HALO, grid_rows - HALO - 1)
    at = 0
    for low, high in zip(top, bottom):
        size = low.shape[0]
        first[at:at + size, :] = jnp.where(even, high, low)
        second[at:at + size, :] = jnp.where(even, low, high)
        at += size

    lane, row = lanes((8, 256)), rows((8, 256))
    tail = jnp.zeros((8, 256), F32)
    for j_rel in range(owned):
        j = jnp.bitwise_xor(q, j_rel)

        def put(at, value, base=j_rel * PIECE):
            block[base + at:base + at + value.shape[0], :] = value
            if base == 0:
                own[at:at + value.shape[0], :] = value

        pack_row(coupling[j], inverses[j], put)
        for l in range(links.shape[1]):
            tail = jnp.where((row == j_rel) & (lane == l), links[j, l].astype(F32), tail)
    block[owned * PIECE:owned * PIECE + 8, :] = tail
    own[PIECE:PIECE + 8, :] = tail


def prepare_kernel(owned, coarse_rows, r_in, b_in, e_in, n_in, support_in, basis_in,
                   r_out, b_out, e_out, n_out, basis, hots, sup_hots, support, sems):
    q = lax.rem(lax.axis_index("narrow"), owned)
    mine = lax.axis_index("wide") * owned + q
    wait_support = copy_all([(support_in, support)], sems.at[pl.ds(0, 1)])
    part = basis.shape[0] // 8
    parts = [pl.ds(part * i, part) for i in range(8)]
    wait = copy_all([(basis_in.at[at], basis.at[at]) for at in parts]
                    + [(r_in, r_out), (b_in, b_out), (e_in, e_out), (n_in, n_out)], sems.at[pl.ds(1, 12)])
    wait_support()

    blocks = support.shape[1]
    rows4 = 4 * blocks
    size = 4 * coarse_rows

    def chosen(which, index):
        g, h = lax.shift_right_logical(index, 4), jnp.bitwise_and(lax.shift_right_logical(index, 3), 1)
        p = jnp.bitwise_and(lax.shift_right_logical(index, 2), 1)
        return jnp.where(which == g * 4 + p * 2 + h, 1.0, 0.0).astype(BF16)

    value = support[...].astype(F32).astype(BF16)
    column = dot_t(chosen(lanes((rows4, blocks)), rows((rows4, blocks))), value)
    line = dot(value, chosen(rows((blocks, rows4)), lanes((blocks, rows4))))
    line = line.astype(jnp.int32) * 4 + jnp.bitwise_and(lanes((4, rows4)), 3)
    at = rows((size, rows4))
    for k in range(4):
        base, left = (k % 2) * size, (k // 2) * rows4
        hots[base:base + size, left:left + rows4] = jnp.where(at == line[k:k + 1, :], 1.0, 0.0).astype(BF16)
    column = jnp.bitwise_xor(column.astype(jnp.int32), mine) * 4 + jnp.bitwise_and(rows((rows4, 4)), 3)
    across = lanes((rows4, size))
    for k in range(4):
        sup_hots[rows4 * k:rows4 * k + rows4, :] = jnp.where(across == column[:, k:k + 1], 1.0, 0.0).astype(BF16)

    wait()


def stack_kernel(*refs):
    fetched, gathered = refs[:-4], refs[-1]
    count = len(fetched)
    gathered[count * PIECE:, :] = jnp.zeros((gathered.shape[0] - count * PIECE, gathered.shape[1]), F32)
    for i, piece in enumerate(fetched):
        gathered[PIECE * i:PIECE * i + PIECE, :] = piece[0:PIECE, :]
        gathered[PIECE * count + i:PIECE * count + i + 1, :] = piece[PIECE:PIECE + 1, :]


def add_kernel(one, two, out):
    half = out.shape[0] // 2
    for i in range(2):
        block = slice(128 * i, 128 * i + 128)
        out[half * i:half * i + half, :] = one[0:half, block] + two[0:half, block]


class Fine:
    def __init__(self, r, b, e, n, from_first, from_second, rx, bx, ex, nx, field):
        line, count = place()
        even = lax.rem(line, 2) == 0
        low_ok, high_ok = line > 0, line < count - 1
        one, two = from_first[...], from_second[...]
        low = jnp.where(low_ok, jnp.where(even, two, one), 0.0)
        high = jnp.where(high_ok, jnp.where(even, one, two), 0.0)
        self.even, self.low_ok, self.high_ok = even, low_ok, high_ok
        self.adjoints, self.grid_rows, width = r.shape
        top = HALO + self.grid_rows
        zeros = jnp.zeros((8, width), F32)
        for a in range(self.adjoints):
            rx[a, 16:24, :] = zeros
            rx[a, 0:HALO, :] = low[3 * a:3 * a + 3]
            rx[a, HALO:top, :] = r[a]
            rx[a, top:top + HALO, :] = high[3 * a:3 * a + 3]
            field[a, 0:8, :] = zeros
            field[a, 32:40, :] = zeros
        bx[16:24, :] = zeros
        bx[0:HALO, :] = low[12:15]
        bx[HALO:top, :] = b[...]
        bx[top:top + HALO, :] = high[12:15]
        ex[16:24, :] = zeros
        ex[0:HALO, :] = low[15:18]
        ex[HALO:top, :] = e[...]
        ex[top:top + HALO, :] = high[15:18]
        nx[16:24, :] = zeros
        nx[24:32, :] = zeros
        nx[0:HALO + 1, :] = low[18:22]
        nx[HALO + 1:top + 1, :] = n[...]
        nx[top + 1:top + 1 + HALO, :] = high[18:21]
        self.r = rx[...]
        self.east = ex[...]
        self.north = nx[1:1 + FIELD, :]
        self.south = nx[0:FIELD, :]
        self.west = pltpu.roll(self.east, 1, 1)
        self.diagonal = bx[...] + self.east + self.west + self.north + self.south
        t = rows((FIELD, width))
        valid = ((t >= HALO) | low_ok) & ((t < top) | high_ok) & (t < top + HALO)
        self.scale = jnp.where(valid, relax_weight / jnp.where(valid, self.diagonal, 1.0), 0.0)
        self.field = field
        self.width = width

    def apply(self, x):
        self.field[:, 8:32, :] = x
        above = self.field[:, 7:31, :]
        below = self.field[:, 9:33, :]
        east = pltpu.roll(x, self.width - 1, 2)
        west = pltpu.roll(x, 1, 2)
        return self.diagonal * x - self.north * below - self.south * above - self.east * east - self.west * west

    def sweep(self, x):
        return x + self.scale * (self.r - self.apply(x))


    def keep(self, r_out, coef_out):
        r_out[...] = self.r
        for i, value in enumerate((self.diagonal, self.scale, self.north, self.south, self.east, self.west)):
            coef_out[i] = value


class Kept(Fine):
    def __init__(self, r, coef, field):
        line, count = place()
        self.even, self.low_ok, self.high_ok = lax.rem(line, 2) == 0, line > 0, line < count - 1
        self.r, self.field = r[...], field
        self.diagonal, self.scale, self.north, self.south, self.east, self.west = [coef[i] for i in range(6)]
        self.adjoints, _, self.width = r.shape


def fine_scratch(adjoints, width):
    return [
        pltpu.VMEM((adjoints, FIELD, width), F32),
        pltpu.VMEM((FIELD, width), F32),
        pltpu.VMEM((FIELD, width), F32),
        pltpu.VMEM((32, width), F32),
        pltpu.VMEM((adjoints, 40, width), F32),
    ]


def restrict_kernel(coarse_rows, r, b, e, n, from_first, from_second, basis, hots,
                    block, gathered, out, x_out, rx, bx, ex, nx, field, by_row, contrib):
    fine = Fine(r, b, e, n, from_first, from_second, rx, bx, ex, nx, field)
    x = fine.scale * fine.r
    for step in range(SWEEPS - 1):
        x = fine.sweep(x)
    resid = fine.r - fine.apply(x)
    for a in range(fine.adjoints):
        x_out[a] = field[a, 8 + HALO:8 + HALO + fine.grid_rows, :]
    field[:, 8:32, :] = resid
    for a in range(fine.adjoints):
        by_row[pl.ds(a, fine.grid_rows, stride=4), :] = field[a, 8 + HALO:8 + HALO + fine.grid_rows, :]
    left = lanes((8, 128)) < 64
    upper = rows((8, 128)) < 4
    for g in range(fine.grid_rows // 2):
        z = by_row[8 * g:8 * g + 8, :]
        parts = []
        for here in (left, ~left):
            held = jnp.where(here, z, 0.0)
            parts.append(jnp.concatenate([jnp.where(upper, held, 0.0), jnp.where(upper, 0.0, held)], axis=1))
        high, low = split(jnp.concatenate(parts, axis=0))
        near = slice(256 * g, 256 * g + 256)
        w_high, w_low = split(basis[near, :])
        both = dot(jnp.concatenate([high, low], axis=0), w_high)
        contrib[16 * g:16 * g + 16, :] = both[0:16] + both[16:32] + dot(high, w_low)
    c_high, c_low = split(contrib[...])
    weights = jnp.concatenate([
        jnp.concatenate([c_high[:, 0:128], c_low[:, 0:128]], axis=1),
        jnp.concatenate([c_high[:, 128:256], c_low[:, 128:256]], axis=1)], axis=0)
    size = 4 * coarse_rows
    total = dot(hots[...], weights)
    total = total[:, 0:128] + total[:, 128:256]
    here = lanes((size, 128)) < 64
    even = jnp.where(here, total[0:size], 0.0)
    odd = jnp.where(here, 0.0, total[size:2 * size])
    mid = size // 2
    packed = even[0:mid] + half_turn(odd[0:mid]) + half_turn(even[mid:size]) + odd[mid:size]
    half = mid // 2
    out[0:half, 0:128] = packed[0:half]
    out[0:half, 128:256] = packed[half:mid]
    out[half:half + block.shape[0], :] = block[...]
    out[half + block.shape[0]:, :] = gathered[...]


def prolong(group, high, low, basis):
    near = slice(16 * group, 16 * group + 16)
    block = slice(256 * group, 256 * group + 256)
    high = high[near, :]
    w_high, w_low = split(basis[block, :])
    both = dot_t(jnp.concatenate([high, low[near, :]], axis=0), w_high)
    got = both[0:16] + both[16:32] + dot_t(high, w_low)
    upper = rows((8, 128)) < 4
    halves = [jnp.where(upper, got[8 * h:8 * h + 8, 0:128], got[8 * h:8 * h + 8, 128:256]) for h in range(2)]
    return jnp.where(lanes((8, 128)) < 64, halves[0], halves[1])


def coarse_kernel(owned, coarse_rows, zs, rhs_ref, message, message_other, *refs):
    spread, spread_other = refs[:owned - 1], refs[owned - 1:2 * owned - 2]
    (basis, sup_hots, x_ref, coarse_ref, high_out, low_out, first, second,
     w_high, w_low, w_inv, link_rows, hots, product, u_ref, by_row) = refs[2 * owned - 2:]
    size = 4 * coarse_rows
    wide, narrow = lax.axis_index("wide"), lax.axis_index("narrow")
    q = lax.rem(narrow, owned)
    mine = wide * owned + q

    lane16 = lanes((16, 128)) < 64
    lane64 = lanes((64, 128)) < 64
    at_own = coarse_rows
    at_fetched = at_own + packed_rows(owned)
    for z_rel in range(zs):
        for c_rel, (fetched, others) in enumerate(((message, spread), (message_other, spread_other))):
            for j_rel in range(owned):
                i = (z_rel * 2 + c_rel) * owned + j_rel
                if z_rel == 0:
                    piece, start, index, count = fetched, at_own, j_rel, owned
                elif j_rel == 0:
                    piece, start, index, count = fetched, at_fetched, z_rel - 1, zs - 1
                else:
                    piece, start, index, count = others[j_rel - 1], 0, z_rel - 1, zs - 1
                base = start + index * PIECE
                at_links = start + count * PIECE + index
                high, low = split(piece[base:base + 64, :])
                w_high[64 * i:64 * i + 64, :] = high
                w_low[64 * i:64 * i + 64, :] = low
                quarters = []
                for half in range(2):
                    packed = piece[base + 64:base + 80, 128 * half:128 * half + 128]
                    turned = half_turn(packed)
                    quarters += [jnp.where(lane16, packed, turned), jnp.where(lane16, turned, packed)]
                high, low = split(jnp.concatenate(quarters, axis=0))
                w_inv[64 * i:64 * i + 64, :] = jnp.where(lane64, high.astype(F32), low.astype(F32)).astype(BF16)
                link_rows[4 * i:4 * i + 4, :] = jnp.broadcast_to(piece[at_links:at_links + 1, 0:128], (4, 128))

    lane = lanes((size, size))
    a_col = jnp.bitwise_and(rows((size, 1)), 3)
    for l in range(4):
        target = jnp.bitwise_xor(link_rows[:, l:l + 1].astype(jnp.int32), mine) * 4 + a_col
        hots[size * l:size * l + size, :] = jnp.where(lane == target, 1.0, 0.0).astype(BF16)

    here = lanes((size, 128)) < 64
    packed = rhs_ref[...]
    turned = half_turn(packed)
    here_mid = here[0:size // 2]
    rhs = jnp.concatenate([jnp.where(here_mid, packed, turned), jnp.where(here_mid, turned, packed)], axis=0)

    def hi_lo(value):
        high, low = split(value)
        return jnp.concatenate([high, low], axis=1)

    u_ref[...] = rhs
    for i in range(coarse_rows):
        link_rows[4 * i:4 * i + 4, :] = u_ref[pl.ds(jnp.bitwise_xor(mine, i) * 4, 4), :]
    rhs = link_rows[...]

    own_block = jnp.bitwise_and(lax.shift_right_logical(rows((size, 256)), 2), 3) == lax.shift_right_logical(
        lanes((size, 256)), 6)

    def fold():
        value = jnp.where(own_block, product[...], 0.0)
        value = value[:, 0:128] + value[:, 128:256]
        return value + half_turn(value)

    def apply_inverse(value):
        high, low = split(value)
        low = jnp.where(here, low.astype(F32), 0.0).astype(BF16)
        for g in range(coarse_rows // 4):
            near = slice(16 * g, 16 * g + 16)
            both = dot_t(jnp.concatenate([high[near], low[near]], axis=0), w_inv[256 * g:256 * g + 256, :])
            product[near, :] = both[0:16] + both[16:32]
        return fold()

    def pick(got, step):
        sel = lanes((step, 128)) < 64
        high = [jnp.where(sel, got[step * k:step * k + step, 0:128], got[step * k + step:step * k + 2 * step, 0:128])
                for k in (0, 2)]
        low = [jnp.where(sel, got[step * k:step * k + step, 128:256],
                         got[step * k + step:step * k + 2 * step, 128:256]) for k in (0, 2)]
        return jnp.concatenate(high, axis=1).astype(BF16), jnp.concatenate(low, axis=1).astype(BF16)

    u = apply_inverse(rhs)
    for step in range(COARSE_SWEEPS):
        high, low = pick(dot(hots[...], hi_lo(u)), size)
        for g in range(coarse_rows // 4):
            near = slice(16 * g, 16 * g + 16)
            block = slice(256 * g, 256 * g + 256)
            both = dot_t(jnp.concatenate([high[near], low[near]], axis=0), w_high[block, :])
            product[near, :] = both[0:16] + both[16:32] + dot_t(high[near], w_low[block, :])
        u = apply_inverse(rhs + fold())

    u_ref[0:4 * owned, :] = u[0:4 * owned]
    here1 = lanes((1, 128)) < 64
    for j in range(owned):
        got = u_ref[pl.ds(jnp.bitwise_xor(q, j) * 4, 4), :]
        coarse_ref[j:j + 1, 0:128] = jnp.where(here1, got[0:1], got[1:2])
        coarse_ref[j:j + 1, 128:256] = jnp.where(here1, got[2:3], got[3:4])

    blocks4 = sup_hots.shape[0] // 4
    high, low = pick(dot(sup_hots[...], hi_lo(u)), blocks4)
    high_out[...] = high
    low_out[...] = low
    line, _ = place()
    even = lax.rem(line, 2) == 0
    adjoints, grid_rows, _ = x_ref.shape
    by_row[0:8, :] = prolong(0, high, low, basis)
    by_row[8:16, :] = prolong(grid_rows // 2 - 1, high, low, basis)
    for a in range(adjoints):
        edge = by_row[pl.ds(a, 4, stride=4), :]
        top = x_ref[a, 0:2, :] + edge[0:2]
        bottom = x_ref[a, grid_rows - 2:grid_rows, :] + edge[2:4]
        first[2 * a:2 * a + 2, :] = jnp.where(even, bottom, top)
        second[2 * a:2 * a + 2, :] = jnp.where(even, top, bottom)


def correct_kernel(r, b, e, n, from_first, from_second, x_ref, high, low, basis,
                   r_out, coef_out, y_out, rx, bx, ex, nx, field, by_row):
    Fine(r, b, e, n, from_first, from_second, rx, bx, ex, nx, field).keep(r_out, coef_out)
    adjoints, grid_rows, width = x_ref.shape
    for g in range(grid_rows // 2):
        by_row[8 * g:8 * g + 8, :] = prolong(g, high, low, basis)
    for a in range(adjoints):
        y_out[a, 0:8, :] = jnp.zeros((8, width), F32)
        y_out[a, 16:24, :] = jnp.zeros((8, width), F32)
        y_out[a, HALO:HALO + grid_rows, :] = x_ref[a] + by_row[pl.ds(a, grid_rows, stride=4), :]


def post_kernel(r, coef, y_ref, y_first, y_inner, y_outer, out, field):
    fine = Kept(r, coef, field)
    in_line = lax.rem(place()[0], 4)
    one, two = y_first[...], jnp.where((in_line == 1) | (in_line == 2), y_inner[...], y_outer[...])
    low = jnp.where(fine.low_ok, jnp.where(fine.even, two, one), 0.0)
    high = jnp.where(fine.high_ok, jnp.where(fine.even, one, two), 0.0)
    grid_rows = out.shape[1]
    start, top = 8 + HALO, 8 + HALO + grid_rows
    field[:, 0:8, :] = jnp.zeros((fine.adjoints, 8, fine.width), F32)
    field[:, 32:40, :] = jnp.zeros((fine.adjoints, 8, fine.width), F32)
    field[:, 8:32, :] = y_ref[...]
    for a in range(fine.adjoints):
        field[a, start - 2:start, :] = low[2 * a:2 * a + 2]
        field[a, top:top + 2, :] = high[2 * a:2 * a + 2]
    x = field[:, 8:32, :]
    for step in range(SWEEPS):
        x = fine.sweep(x)
    field[:, 8:32, :] = x
    for a in range(fine.adjoints):
        out[a] = field[a, start:top, :]


def shape(*dims, kind=F32):
    return jax.ShapeDtypeStruct(dims, kind)


def params(mebibytes):
    return pltpu.CompilerParams(vmem_limit_bytes=mebibytes * 2 ** 20)


def stay(array):
    return pltpu.with_memory_space_constraint(array, pltpu.HBM)


CHEAP = pl.CostEstimate(flops=1, bytes_accessed=1, transcendentals=0)


def body(right_sides, brinkman, east_faces, north_faces, support, basis, links, coarse_block_inverses, coarse_coupling):
    adjoints, grid_rows, width = right_sides.shape
    blocks, block_size, _ = basis.shape
    owned = coarse_block_inverses.shape[0]
    coarse_rows = owned * lax.axis_size("wide")
    zs = lax.axis_size("wide") // 2
    size = 4 * coarse_rows
    basis = basis.reshape(blocks * block_size, -1)

    in_hbm = pl.BlockSpec(memory_space=pltpu.HBM)
    anywhere = pl.BlockSpec(memory_space=pl.ANY)
    in_vmem = pl.BlockSpec(memory_space=pltpu.VMEM)
    row_dims = (grid_rows, width)
    message = shape(24, width)
    fine_inputs = tuple(map(stay, (right_sides, brinkman, east_faces, north_faces)))
    coarse_inputs = tuple(map(stay, (links, coarse_coupling, coarse_block_inverses)))
    to_first, to_second, own, block = pl.pallas_call(
        functools.partial(begin_kernel, owned),
        out_shape=(message, message, shape(packed_rows(1), 256), shape(packed_rows(owned), 256)),
        in_specs=[in_hbm] * 7,
        scratch_shapes=[
            pltpu.VMEM((adjoints, *row_dims), F32), pltpu.VMEM(row_dims, F32), pltpu.VMEM(row_dims, F32),
            pltpu.VMEM(row_dims, F32), pltpu.SMEM(links.shape, jnp.int32), pltpu.VMEM(coarse_coupling.shape, F32),
            pltpu.VMEM(coarse_block_inverses.shape, F32), pltpu.SemaphoreType.DMA((7,))],
        cost_estimate=CHEAP, compiler_params=params(16), name="begin",
    )(*fine_inputs, *coarse_inputs)
    from_first, from_second = pair_swaps(to_first, to_second)
    fetched = [swap(own, "wide", 2 * k) for k in range(1, zs)]

    rows4 = adjoints * blocks
    r, b, e, n, basis, hots, sup_hots = pl.pallas_call(
        functools.partial(prepare_kernel, owned, coarse_rows),
        out_shape=(shape(adjoints, *row_dims), shape(*row_dims), shape(*row_dims), shape(*row_dims),
                   shape(*basis.shape), shape(2 * size, 2 * rows4, kind=BF16), shape(4 * rows4, size, kind=BF16)),
        in_specs=[in_hbm] * 6,
        scratch_shapes=[pltpu.VMEM((4, blocks), jnp.int32), pltpu.SemaphoreType.DMA((13,))],
        cost_estimate=CHEAP, compiler_params=params(16), name="prepare",
    )(*fine_inputs, stay(support.T), stay(basis))

    gathered = pl.pallas_call(
        stack_kernel, out_shape=shape(packed_rows(zs - 1), 256),
        in_specs=[in_vmem] * (zs - 1) + [anywhere] * 3,
        cost_estimate=CHEAP, compiler_params=params(4), name="stack",
    )(*fetched, from_first, from_second, hots)
    spread = [swap(gathered, "narrow", k) for k in range(1, owned)]

    half = coarse_rows
    message, x = pl.pallas_call(
        functools.partial(restrict_kernel, coarse_rows),
        out_shape=(shape(half + packed_rows(owned) + packed_rows(zs - 1), 256), shape(adjoints, *row_dims)),
        scratch_shapes=fine_scratch(adjoints, width) + [
            pltpu.VMEM((4 * grid_rows, width), F32), pltpu.VMEM((rows4, 256), F32)],
        cost_estimate=CHEAP, compiler_params=params(16), name="restrict",
    )(r, b, e, n, from_first, from_second, basis, hots, block, gathered)

    message_other = swap(message, "wide", 1)
    rhs = pl.pallas_call(
        add_kernel, out_shape=shape(2 * half, 128), cost_estimate=CHEAP, compiler_params=params(4), name="add",
    )(message, message_other)
    for bit in bits_of(zs):
        rhs = rhs + swap(rhs, "wide", 2 * bit)
    spread = tie(spread, rhs)
    spread_other = [swap(piece, "wide", 1) for piece in spread]
    for masks in rounds_of(lax.axis_size("narrow")):
        rhs = sum([swap(rhs, "narrow", k) for k in masks], rhs)

    near = shape(rows4, 256, kind=BF16)
    coarse, high, low, y_first, y_second = pl.pallas_call(
        functools.partial(coarse_kernel, owned, coarse_rows, zs),
        out_shape=(shape(owned, 256), near, near, shape(8, width), shape(8, width)),
        scratch_shapes=[
            pltpu.VMEM((64 * coarse_rows, 256), BF16), pltpu.VMEM((64 * coarse_rows, 256), BF16),
            pltpu.VMEM((64 * coarse_rows, 128), BF16), pltpu.VMEM((size, 128), F32),
            pltpu.VMEM((4 * size, size), BF16), pltpu.VMEM((size, 256), F32),
            pltpu.VMEM((size, 128), F32), pltpu.VMEM((16, width), F32)],
        cost_estimate=CHEAP, compiler_params=params(min(48, 8 + coarse_rows // 3)), name="coarse",
    )(rhs, message, message_other, *spread, *spread_other, basis, sup_hots, x)

    y_from = pair_swaps_near(y_first, y_second)
    extended = shape(adjoints, FIELD, width)
    r, coef, y = pl.pallas_call(
        correct_kernel,
        out_shape=(extended, shape(6, FIELD, width), extended),
        scratch_shapes=fine_scratch(adjoints, width) + [pltpu.VMEM((4 * grid_rows, width), F32)],
        cost_estimate=CHEAP, compiler_params=params(16), name="correct",
    )(r, b, e, n, from_first, from_second, x, high, low, basis)
    field = pl.pallas_call(
        post_kernel,
        out_shape=shape(adjoints, *row_dims),
        scratch_shapes=[pltpu.VMEM((adjoints, 40, width), F32)],
        cost_estimate=CHEAP, compiler_params=params(16), name="post",
    )(r, coef, y, *y_from)
    return field, coarse


def solution(mesh):
    return jax.shard_map(
        body,
        mesh=mesh,
        in_specs=(
            P(None, ("wide", "narrow"), None),
            P(("wide", "narrow"), None),
            P(("wide", "narrow"), None),
            P(("wide", "narrow"), None),
            P(("wide", "narrow"), None),
            P(("wide", "narrow"), None, None),
            P("wide", None),
            P("wide", None, None),
            P("wide", None, None),
        ),
        out_specs=(P(None, ("wide", "narrow"), None), P("wide", None)),
        check_vma=False,
    )
```

```python
import functools

import jax
import jax.numpy as jnp
from jax import lax
from jax.experimental import pallas as pl
from jax.experimental.pallas import tpu as pltpu
from jax.sharding import PartitionSpec as P

SWEEPS = 2
COARSE_SWEEPS = 3
relax_weight = 0.7

BOTH = ("wide", "narrow")
HALO = 3
FIELD = 24
PIECE = 80
F32 = jnp.float32
BF16 = jnp.bfloat16


def swap(value, axis, bits):
    size = lax.axis_size(axis)
    return lax.ppermute(value, axis, [(i, i ^ bits) for i in range(size)])


def pair_swaps(to_first, to_second):
    count = lax.axis_size(BOTH)
    first = lax.ppermute(to_first, BOTH, [(i, i ^ 1) for i in range(count)])
    odd = [(i, i + 1) for i in range(1, count - 1, 2)] + [(count - 1, 0)]
    second = lax.ppermute(to_second, BOTH, odd + [(target, source) for source, target in odd])
    return first, second


def pair_swaps_near(to_first, to_second):
    count, across = lax.axis_size(BOTH), lax.axis_size("narrow")
    first = lax.ppermute(to_first, BOTH, [(i, i ^ 1) for i in range(count)])
    inner = lax.ppermute(to_second, BOTH, [(i, i ^ (3 if i % 4 in (1, 2) else across)) for i in range(count)])
    outer = [(i, i + 1) for i in range(3, count - 1, 4)]
    outer += [(i, i ^ across) for i in range(2, count, 4) if i < i ^ across]
    rest = [0] + list(range(1, count, 4)) + [count - 1]
    outer += list(zip(rest[::2], rest[1::2]))
    outer = lax.ppermute(to_second, BOTH, outer + [(target, source) for source, target in outer])
    return first, inner, outer


def tie(values, after):
    count = len(values)
    spec = pl.BlockSpec(memory_space=pl.ANY)
    return list(pl.pallas_call(
        lambda *refs: None, out_shape=[jax.ShapeDtypeStruct(v.shape, v.dtype) for v in values],
        in_specs=[spec] * (count + 1), out_specs=[spec] * count,
        input_output_aliases={i: i for i in range(count)}, cost_estimate=CHEAP, compiler_params=params(1), name="tie",
    )(*values, after))


def rounds_of(size):
    rounds, base = [], 1
    while base < size:
        span = 4 if base * 4 <= size else 2
        rounds.append([base * k for k in range(1, span)])
        base *= span
    return rounds


def share_kernel(value, one, two, out):
    second = lax.rem(lax.axis_index("wide"), 2) == 1
    out[...] = one[...] + jnp.where(second, two[...], value[...])


def sum_shared(value, axis, masks):
    if len(masks) == 1:
        return value + swap(value, axis, masks[0])
    count, across = lax.axis_size(BOTH), lax.axis_size("narrow")
    unit = across if axis == "wide" else 1
    near, far, farthest = [unit * mask for mask in masks]
    one = lax.ppermute(value, BOTH, [(i, i ^ (far if i & across else near)) for i in range(count)])
    two = lax.ppermute(value, BOTH, [(i, i ^ (farthest if i & across else near)) for i in range(count)])
    value = pl.pallas_call(
        share_kernel, out_shape=jax.ShapeDtypeStruct(value.shape, value.dtype),
        cost_estimate=CHEAP, compiler_params=params(1), name="share",
    )(value, one, two)
    return value + swap(value, "wide", 1)


def bits_of(size):
    return [1 << i for i in range(size.bit_length() - 1)]


def place():
    wide, narrow = lax.axis_index("wide"), lax.axis_index("narrow")
    line = wide * lax.axis_size("narrow") + narrow
    count = lax.axis_size("wide") * lax.axis_size("narrow")
    return line, count


def packed_rows(count):
    return count * PIECE + 8 * ((count + 7) // 8)


def lanes(shape):
    return lax.broadcasted_iota(jnp.int32, shape, len(shape) - 1)


def rows(shape):
    return lax.broadcasted_iota(jnp.int32, shape, len(shape) - 2)


def split(value):
    high = value.astype(BF16)
    return high, (value - high.astype(F32)).astype(BF16)


def dot(left, right):
    return lax.dot_general(left, right, (((1,), (0,)), ((), ())), preferred_element_type=F32)


def dot_t(left, right):
    return lax.dot_general(left, right, (((1,), (1,)), ((), ())), preferred_element_type=F32)


def half_turn(value):
    return pltpu.roll(value, 64, 1)


def copy_all(pairs, sems):
    copies = [pltpu.make_async_copy(source, target, sems.at[i]) for i, (source, target) in enumerate(pairs)]
    for copy in copies:
        copy.start()

    def wait():
        for copy in copies:
            copy.wait()

    return wait


def pack_row(matrix, inverse, put):
    put(0, matrix)
    put(64, jnp.concatenate([inverse[16 * t:16 * t + 16, :] for t in range(4)], axis=1))


def begin_kernel(owned, r_in, b_in, e_in, n_in, links_in, coupling_in, inverses_in, first, second, own, block,
                 r, b, e, n, links, coupling, inverses, sems):
    wait = copy_all([(r_in, r), (b_in, b), (e_in, e), (n_in, n), (links_in, links), (coupling_in, coupling),
                     (inverses_in, inverses)], sems)
    grid_rows = b.shape[0]
    line, _ = place()
    even = lax.rem(line, 2) == 0
    q = lax.rem(lax.axis_index("narrow"), owned)
    wait()

    def message(start, north_start):
        parts = [r[a, start:start + HALO, :] for a in range(r.shape[0])]
        parts += [b[start:start + HALO, :], e[start:start + HALO, :]]
        parts += [n[north_start:north_start + HALO + 1, :], jnp.zeros((2, b.shape[1]), F32)]
        return parts

    top = message(0, 0)
    bottom = message(grid_rows - HALO, grid_rows - HALO - 1)
    at = 0
    for low, high in zip(top, bottom):
        size = low.shape[0]
        first[at:at + size, :] = jnp.where(even, high, low)
        second[at:at + size, :] = jnp.where(even, low, high)
        at += size

    lane, row = lanes((8, 256)), rows((8, 256))
    tail = jnp.zeros((8, 256), F32)
    for j_rel in range(owned):
        j = jnp.bitwise_xor(q, j_rel)

        def put(at, value, base=j_rel * PIECE):
            block[base + at:base + at + value.shape[0], :] = value
            if base == 0:
                own[at:at + value.shape[0], :] = value

        pack_row(coupling[j], inverses[j], put)
        for l in range(links.shape[1]):
            tail = jnp.where((row == j_rel) & (lane == l), links[j, l].astype(F32), tail)
    block[owned * PIECE:owned * PIECE + 8, :] = tail
    own[PIECE:PIECE + 8, :] = tail


def prepare_kernel(owned, coarse_rows, r_in, b_in, e_in, n_in, support_in, basis_in,
                   r_out, b_out, e_out, n_out, basis, hots, sup_hots, support, sems):
    q = lax.rem(lax.axis_index("narrow"), owned)
    mine = lax.axis_index("wide") * owned + q
    wait_support = copy_all([(support_in, support)], sems.at[pl.ds(0, 1)])
    part = basis.shape[0] // 8
    parts = [pl.ds(part * i, part) for i in range(8)]
    wait = copy_all([(basis_in.at[at], basis.at[at]) for at in parts]
                    + [(r_in, r_out), (b_in, b_out), (e_in, e_out), (n_in, n_out)], sems.at[pl.ds(1, 12)])
    wait_support()

    blocks = support.shape[1]
    rows4 = 4 * blocks
    size = 4 * coarse_rows

    def chosen(which, index):
        g, h = lax.shift_right_logical(index, 4), jnp.bitwise_and(lax.shift_right_logical(index, 3), 1)
        p = jnp.bitwise_and(lax.shift_right_logical(index, 2), 1)
        return jnp.where(which == g * 4 + p * 2 + h, 1.0, 0.0).astype(BF16)

    value = support[...].astype(F32).astype(BF16)
    column = dot_t(chosen(lanes((rows4, blocks)), rows((rows4, blocks))), value)
    line = dot(value, chosen(rows((blocks, rows4)), lanes((blocks, rows4))))
    line = line.astype(jnp.int32) * 4 + jnp.bitwise_and(lanes((4, rows4)), 3)
    at = rows((size, rows4))
    for k in range(4):
        base, left = (k % 2) * size, (k // 2) * rows4
        hots[base:base + size, left:left + rows4] = jnp.where(at == line[k:k + 1, :], 1.0, 0.0).astype(BF16)
    column = jnp.bitwise_xor(column.astype(jnp.int32), mine) * 4 + jnp.bitwise_and(rows((rows4, 4)), 3)
    across = lanes((rows4, size))
    for k in range(4):
        sup_hots[rows4 * k:rows4 * k + rows4, :] = jnp.where(across == column[:, k:k + 1], 1.0, 0.0).astype(BF16)

    wait()


def stack_kernel(*refs):
    fetched, gathered = refs[:-4], refs[-1]
    count = len(fetched)
    gathered[count * PIECE:, :] = jnp.zeros((gathered.shape[0] - count * PIECE, gathered.shape[1]), F32)
    for i, piece in enumerate(fetched):
        gathered[PIECE * i:PIECE * i + PIECE, :] = piece[0:PIECE, :]
        gathered[PIECE * count + i:PIECE * count + i + 1, :] = piece[PIECE:PIECE + 1, :]


def add_kernel(one, two, out):
    half = out.shape[0] // 2
    for i in range(2):
        block = slice(128 * i, 128 * i + 128)
        out[half * i:half * i + half, :] = one[0:half, block] + two[0:half, block]


class Fine:
    def __init__(self, r, b, e, n, from_first, from_second, rx, bx, ex, nx, field):
        line, count = place()
        even = lax.rem(line, 2) == 0
        low_ok, high_ok = line > 0, line < count - 1
        one, two = from_first[...], from_second[...]
        low = jnp.where(low_ok, jnp.where(even, two, one), 0.0)
        high = jnp.where(high_ok, jnp.where(even, one, two), 0.0)
        self.even, self.low_ok, self.high_ok = even, low_ok, high_ok
        self.adjoints, self.grid_rows, width = r.shape
        top = HALO + self.grid_rows
        zeros = jnp.zeros((8, width), F32)
        for a in range(self.adjoints):
            rx[a, 16:24, :] = zeros
            rx[a, 0:HALO, :] = low[3 * a:3 * a + 3]
            rx[a, HALO:top, :] = r[a]
            rx[a, top:top + HALO, :] = high[3 * a:3 * a + 3]
            field[a, 0:8, :] = zeros
            field[a, 32:40, :] = zeros
        bx[16:24, :] = zeros
        bx[0:HALO, :] = low[12:15]
        bx[HALO:top, :] = b[...]
        bx[top:top + HALO, :] = high[12:15]
        ex[16:24, :] = zeros
        ex[0:HALO, :] = low[15:18]
        ex[HALO:top, :] = e[...]
        ex[top:top + HALO, :] = high[15:18]
        nx[16:24, :] = zeros
        nx[24:32, :] = zeros
        nx[0:HALO + 1, :] = low[18:22]
        nx[HALO + 1:top + 1, :] = n[...]
        nx[top + 1:top + 1 + HALO, :] = high[18:21]
        self.r = rx[...]
        self.east = ex[...]
        self.north = nx[1:1 + FIELD, :]
        self.south = nx[0:FIELD, :]
        self.west = pltpu.roll(self.east, 1, 1)
        self.diagonal = bx[...] + self.east + self.west + self.north + self.south
        t = rows((FIELD, width))
        valid = ((t >= HALO) | low_ok) & ((t < top) | high_ok) & (t < top + HALO)
        self.scale = jnp.where(valid, relax_weight / jnp.where(valid, self.diagonal, 1.0), 0.0)
        self.field = field
        self.width = width

    def apply(self, x):
        self.field[:, 8:32, :] = x
        above = self.field[:, 7:31, :]
        below = self.field[:, 9:33, :]
        east = pltpu.roll(x, self.width - 1, 2)
        west = pltpu.roll(x, 1, 2)
        return self.diagonal * x - self.north * below - self.south * above - self.east * east - self.west * west

    def sweep(self, x):
        return x + self.scale * (self.r - self.apply(x))


    def keep(self, r_out, coef_out):
        r_out[...] = self.r
        for i, value in enumerate((self.diagonal, self.scale, self.north, self.south, self.east, self.west)):
            coef_out[i] = value


class Kept(Fine):
    def __init__(self, r, coef, field):
        line, count = place()
        self.even, self.low_ok, self.high_ok = lax.rem(line, 2) == 0, line > 0, line < count - 1
        self.r, self.field = r[...], field
        self.diagonal, self.scale, self.north, self.south, self.east, self.west = [coef[i] for i in range(6)]
        self.adjoints, _, self.width = r.shape


def fine_scratch(adjoints, width):
    return [
        pltpu.VMEM((adjoints, FIELD, width), F32),
        pltpu.VMEM((FIELD, width), F32),
        pltpu.VMEM((FIELD, width), F32),
        pltpu.VMEM((32, width), F32),
        pltpu.VMEM((adjoints, 40, width), F32),
    ]


def restrict_kernel(coarse_rows, r, b, e, n, from_second, from_first, basis, hots,
                    block, gathered, out, x_out, rx, bx, ex, nx, field, by_row, contrib):
    fine = Fine(r, b, e, n, from_first, from_second, rx, bx, ex, nx, field)
    x = fine.scale * fine.r
    for step in range(SWEEPS - 1):
        x = fine.sweep(x)
    resid = fine.r - fine.apply(x)
    for a in range(fine.adjoints):
        x_out[a] = field[a, 8 + HALO:8 + HALO + fine.grid_rows, :]
    field[:, 8:32, :] = resid
    for a in range(fine.adjoints):
        by_row[pl.ds(a, fine.grid_rows, stride=4), :] = field[a, 8 + HALO:8 + HALO + fine.grid_rows, :]
    left = lanes((8, 128)) < 64
    upper = rows((8, 128)) < 4
    for g in range(fine.grid_rows // 2):
        z = by_row[8 * g:8 * g + 8, :]
        parts = []
        for here in (left, ~left):
            held = jnp.where(here, z, 0.0)
            parts.append(jnp.concatenate([jnp.where(upper, held, 0.0), jnp.where(upper, 0.0, held)], axis=1))
        high, low = split(jnp.concatenate(parts, axis=0))
        near = slice(256 * g, 256 * g + 256)
        w_high, w_low = split(basis[near, :])
        both = dot(jnp.concatenate([high, low], axis=0), w_high)
        contrib[16 * g:16 * g + 16, :] = both[0:16] + both[16:32] + dot(high, w_low)
    c_high, c_low = split(contrib[...])
    weights = jnp.concatenate([
        jnp.concatenate([c_high[:, 0:128], c_low[:, 0:128]], axis=1),
        jnp.concatenate([c_high[:, 128:256], c_low[:, 128:256]], axis=1)], axis=0)
    size = 4 * coarse_rows
    total = dot(hots[...], weights)
    total = total[:, 0:128] + total[:, 128:256]
    here = lanes((size, 128)) < 64
    even = jnp.where(here, total[0:size], 0.0)
    odd = jnp.where(here, 0.0, total[size:2 * size])
    mid = size // 2
    packed = even[0:mid] + half_turn(odd[0:mid]) + half_turn(even[mid:size]) + odd[mid:size]
    half = mid // 2
    out[0:half, 0:128] = packed[0:half]
    out[0:half, 128:256] = packed[half:mid]
    out[half:half + block.shape[0], :] = block[...]
    out[half + block.shape[0]:, :] = gathered[...]


def prolong(group, high, low, basis):
    near = slice(16 * group, 16 * group + 16)
    block = slice(256 * group, 256 * group + 256)
    high = high[near, :]
    w_high, w_low = split(basis[block, :])
    both = dot_t(jnp.concatenate([high, low[near, :]], axis=0), w_high)
    got = both[0:16] + both[16:32] + dot_t(high, w_low)
    upper = rows((8, 128)) < 4
    halves = [jnp.where(upper, got[8 * h:8 * h + 8, 0:128], got[8 * h:8 * h + 8, 128:256]) for h in range(2)]
    return jnp.where(lanes((8, 128)) < 64, halves[0], halves[1])


def coarse_kernel(owned, coarse_rows, zs, rhs_ref, message, message_other, *refs):
    spread, spread_other = refs[:owned - 1], refs[owned - 1:2 * owned - 2]
    (basis, sup_hots, x_ref, coarse_ref, high_out, low_out, first, second,
     w_high, w_low, w_inv, link_rows, hots, product, u_ref, by_row) = refs[2 * owned - 2:]
    size = 4 * coarse_rows
    wide, narrow = lax.axis_index("wide"), lax.axis_index("narrow")
    q = lax.rem(narrow, owned)
    mine = wide * owned + q

    lane16 = lanes((16, 128)) < 64
    lane64 = lanes((64, 128)) < 64
    at_own = coarse_rows
    at_fetched = at_own + packed_rows(owned)
    for z_rel in range(zs):
        for c_rel, (fetched, others) in enumerate(((message, spread), (message_other, spread_other))):
            for j_rel in range(owned):
                i = (z_rel * 2 + c_rel) * owned + j_rel
                if z_rel == 0:
                    piece, start, index, count = fetched, at_own, j_rel, owned
                elif j_rel == 0:
                    piece, start, index, count = fetched, at_fetched, z_rel - 1, zs - 1
                else:
                    piece, start, index, count = others[j_rel - 1], 0, z_rel - 1, zs - 1
                base = start + index * PIECE
                at_links = start + count * PIECE + index
                high, low = split(piece[base:base + 64, :])
                w_high[64 * i:64 * i + 64, :] = high
                w_low[64 * i:64 * i + 64, :] = low
                quarters = []
                for half in range(2):
                    packed = piece[base + 64:base + 80, 128 * half:128 * half + 128]
                    turned = half_turn(packed)
                    quarters += [jnp.where(lane16, packed, turned), jnp.where(lane16, turned, packed)]
                high, low = split(jnp.concatenate(quarters, axis=0))
                w_inv[64 * i:64 * i + 64, :] = jnp.where(lane64, high.astype(F32), low.astype(F32)).astype(BF16)
                link_rows[4 * i:4 * i + 4, :] = jnp.broadcast_to(piece[at_links:at_links + 1, 0:128], (4, 128))

    lane = lanes((size, size))
    a_col = jnp.bitwise_and(rows((size, 1)), 3)
    for l in range(4):
        target = jnp.bitwise_xor(link_rows[:, l:l + 1].astype(jnp.int32), mine) * 4 + a_col
        hots[size * l:size * l + size, :] = jnp.where(lane == target, 1.0, 0.0).astype(BF16)

    here = lanes((size, 128)) < 64
    packed = rhs_ref[...]
    turned = half_turn(packed)
    here_mid = here[0:size // 2]
    rhs = jnp.concatenate([jnp.where(here_mid, packed, turned), jnp.where(here_mid, turned, packed)], axis=0)

    def hi_lo(value):
        high, low = split(value)
        return jnp.concatenate([high, low], axis=1)

    u_ref[...] = rhs
    for i in range(coarse_rows):
        link_rows[4 * i:4 * i + 4, :] = u_ref[pl.ds(jnp.bitwise_xor(mine, i) * 4, 4), :]
    rhs = link_rows[...]

    own_block = jnp.bitwise_and(lax.shift_right_logical(rows((size, 256)), 2), 3) == lax.shift_right_logical(
        lanes((size, 256)), 6)

    def fold():
        value = jnp.where(own_block, product[...], 0.0)
        value = value[:, 0:128] + value[:, 128:256]
        return value + half_turn(value)

    def apply_inverse(value):
        high, low = split(value)
        low = jnp.where(here, low.astype(F32), 0.0).astype(BF16)
        for g in range(coarse_rows // 4):
            near = slice(16 * g, 16 * g + 16)
            both = dot_t(jnp.concatenate([high[near], low[near]], axis=0), w_inv[256 * g:256 * g + 256, :])
            product[near, :] = both[0:16] + both[16:32]
        return fold()

    def pick(got, step):
        sel = lanes((step, 128)) < 64
        high = [jnp.where(sel, got[step * k:step * k + step, 0:128], got[step * k + step:step * k + 2 * step, 0:128])
                for k in (0, 2)]
        low = [jnp.where(sel, got[step * k:step * k + step, 128:256],
                         got[step * k + step:step * k + 2 * step, 128:256]) for k in (0, 2)]
        return jnp.concatenate(high, axis=1).astype(BF16), jnp.concatenate(low, axis=1).astype(BF16)

    u = apply_inverse(rhs)
    for step in range(COARSE_SWEEPS):
        high, low = pick(dot(hots[...], hi_lo(u)), size)
        for g in range(coarse_rows // 4):
            near = slice(16 * g, 16 * g + 16)
            block = slice(256 * g, 256 * g + 256)
            both = dot_t(jnp.concatenate([high[near], low[near]], axis=0), w_high[block, :])
            product[near, :] = both[0:16] + both[16:32] + dot_t(high[near], w_low[block, :])
        u = apply_inverse(rhs + fold())

    u_ref[0:4 * owned, :] = u[0:4 * owned]
    here1 = lanes((1, 128)) < 64
    for j in range(owned):
        got = u_ref[pl.ds(jnp.bitwise_xor(q, j) * 4, 4), :]
        coarse_ref[j:j + 1, 0:128] = jnp.where(here1, got[0:1], got[1:2])
        coarse_ref[j:j + 1, 128:256] = jnp.where(here1, got[2:3], got[3:4])

    blocks4 = sup_hots.shape[0] // 4
    high, low = pick(dot(sup_hots[...], hi_lo(u)), blocks4)
    high_out[...] = high
    low_out[...] = low
    line, _ = place()
    even = lax.rem(line, 2) == 0
    adjoints, grid_rows, _ = x_ref.shape
    by_row[0:8, :] = prolong(0, high, low, basis)
    by_row[8:16, :] = prolong(grid_rows // 2 - 1, high, low, basis)
    for a in range(adjoints):
        edge = by_row[pl.ds(a, 4, stride=4), :]
        top = x_ref[a, 0:2, :] + edge[0:2]
        bottom = x_ref[a, grid_rows - 2:grid_rows, :] + edge[2:4]
        first[2 * a:2 * a + 2, :] = jnp.where(even, bottom, top)
        second[2 * a:2 * a + 2, :] = jnp.where(even, top, bottom)


def correct_kernel(r, b, e, n, from_second, from_first, x_ref, high, low, basis,
                   r_out, coef_out, y_out, rx, bx, ex, nx, field, by_row):
    Fine(r, b, e, n, from_first, from_second, rx, bx, ex, nx, field).keep(r_out, coef_out)
    adjoints, grid_rows, width = x_ref.shape
    for g in range(grid_rows // 2):
        by_row[8 * g:8 * g + 8, :] = prolong(g, high, low, basis)
    for a in range(adjoints):
        y_out[a, 0:8, :] = jnp.zeros((8, width), F32)
        y_out[a, 16:24, :] = jnp.zeros((8, width), F32)
        y_out[a, HALO:HALO + grid_rows, :] = x_ref[a] + by_row[pl.ds(a, grid_rows, stride=4), :]


def post_kernel(r, coef, y_ref, y_first, y_inner, y_outer, out, field):
    fine = Kept(r, coef, field)
    in_line = lax.rem(place()[0], 4)
    one, two = y_first[...], jnp.where((in_line == 1) | (in_line == 2), y_inner[...], y_outer[...])
    low = jnp.where(fine.low_ok, jnp.where(fine.even, two, one), 0.0)
    high = jnp.where(fine.high_ok, jnp.where(fine.even, one, two), 0.0)
    grid_rows = out.shape[1]
    start, top = 8 + HALO, 8 + HALO + grid_rows
    field[:, 0:8, :] = jnp.zeros((fine.adjoints, 8, fine.width), F32)
    field[:, 32:40, :] = jnp.zeros((fine.adjoints, 8, fine.width), F32)
    field[:, 8:32, :] = y_ref[...]
    for a in range(fine.adjoints):
        field[a, start - 2:start, :] = low[2 * a:2 * a + 2]
        field[a, top:top + 2, :] = high[2 * a:2 * a + 2]
    x = field[:, 8:32, :]
    for step in range(SWEEPS):
        x = fine.sweep(x)
    field[:, 8:32, :] = x
    for a in range(fine.adjoints):
        out[a] = field[a, start:top, :]


def shape(*dims, kind=F32):
    return jax.ShapeDtypeStruct(dims, kind)


def params(mebibytes):
    return pltpu.CompilerParams(vmem_limit_bytes=mebibytes * 2 ** 20)


def stay(array):
    return pltpu.with_memory_space_constraint(array, pltpu.HBM)


CHEAP = pl.CostEstimate(flops=1, bytes_accessed=1, transcendentals=0)


def body(right_sides, brinkman, east_faces, north_faces, support, basis, links, coarse_block_inverses, coarse_coupling):
    adjoints, grid_rows, width = right_sides.shape
    blocks, block_size, _ = basis.shape
    owned = coarse_block_inverses.shape[0]
    coarse_rows = owned * lax.axis_size("wide")
    zs = lax.axis_size("wide") // 2
    size = 4 * coarse_rows
    basis = basis.reshape(blocks * block_size, -1)

    in_hbm = pl.BlockSpec(memory_space=pltpu.HBM)
    anywhere = pl.BlockSpec(memory_space=pl.ANY)
    in_vmem = pl.BlockSpec(memory_space=pltpu.VMEM)
    row_dims = (grid_rows, width)
    message = shape(24, width)
    fine_inputs = tuple(map(stay, (right_sides, brinkman, east_faces, north_faces)))
    coarse_inputs = tuple(map(stay, (links, coarse_coupling, coarse_block_inverses)))
    to_first, to_second, own, block = pl.pallas_call(
        functools.partial(begin_kernel, owned),
        out_shape=(message, message, shape(packed_rows(1), 256), shape(packed_rows(owned), 256)),
        in_specs=[in_hbm] * 7,
        scratch_shapes=[
            pltpu.VMEM((adjoints, *row_dims), F32), pltpu.VMEM(row_dims, F32), pltpu.VMEM(row_dims, F32),
            pltpu.VMEM(row_dims, F32), pltpu.SMEM(links.shape, jnp.int32), pltpu.VMEM(coarse_coupling.shape, F32),
            pltpu.VMEM(coarse_block_inverses.shape, F32), pltpu.SemaphoreType.DMA((7,))],
        cost_estimate=CHEAP, compiler_params=params(16), name="begin",
    )(*fine_inputs, *coarse_inputs)
    from_first, from_second = pair_swaps(to_first, to_second)
    fetched = [swap(own, "wide", 2 * k) for k in range(1, zs)]

    rows4 = adjoints * blocks
    r, b, e, n, basis, hots, sup_hots = pl.pallas_call(
        functools.partial(prepare_kernel, owned, coarse_rows),
        out_shape=(shape(adjoints, *row_dims), shape(*row_dims), shape(*row_dims), shape(*row_dims),
                   shape(*basis.shape), shape(2 * size, 2 * rows4, kind=BF16), shape(4 * rows4, size, kind=BF16)),
        in_specs=[in_hbm] * 6,
        scratch_shapes=[pltpu.VMEM((4, blocks), jnp.int32), pltpu.SemaphoreType.DMA((13,))],
        cost_estimate=CHEAP, compiler_params=params(16), name="prepare",
    )(*fine_inputs, stay(support.T), stay(basis))

    gathered = pl.pallas_call(
        stack_kernel, out_shape=shape(packed_rows(zs - 1), 256),
        in_specs=[in_vmem] * (zs - 1) + [anywhere] * 3,
        cost_estimate=CHEAP, compiler_params=params(4), name="stack",
    )(*fetched, from_second, from_first, hots)
    spread = [swap(gathered, "narrow", k) for k in range(1, owned)]

    half = coarse_rows
    message, x = pl.pallas_call(
        functools.partial(restrict_kernel, coarse_rows),
        out_shape=(shape(half + packed_rows(owned) + packed_rows(zs - 1), 256), shape(adjoints, *row_dims)),
        scratch_shapes=fine_scratch(adjoints, width) + [
            pltpu.VMEM((4 * grid_rows, width), F32), pltpu.VMEM((rows4, 256), F32)],
        cost_estimate=CHEAP, compiler_params=params(16), name="restrict",
    )(r, b, e, n, from_second, from_first, basis, hots, block, gathered)

    message_other = swap(message, "wide", 1)
    rhs = pl.pallas_call(
        add_kernel, out_shape=shape(2 * half, 128), cost_estimate=CHEAP, compiler_params=params(4), name="add",
    )(message, message_other)
    for masks in rounds_of(zs):
        rhs = sum_shared(rhs, "wide", [2 * k for k in masks])
    spread = tie(spread, rhs)
    spread_other = [swap(piece, "wide", 1) for piece in spread]
    for masks in rounds_of(lax.axis_size("narrow")):
        rhs = sum([swap(rhs, "narrow", k) for k in masks], rhs)

    near = shape(rows4, 256, kind=BF16)
    coarse, high, low, y_first, y_second = pl.pallas_call(
        functools.partial(coarse_kernel, owned, coarse_rows, zs),
        out_shape=(shape(owned, 256), near, near, shape(8, width), shape(8, width)),
        scratch_shapes=[
            pltpu.VMEM((64 * coarse_rows, 256), BF16), pltpu.VMEM((64 * coarse_rows, 256), BF16),
            pltpu.VMEM((64 * coarse_rows, 128), BF16), pltpu.VMEM((size, 128), F32),
            pltpu.VMEM((4 * size, size), BF16), pltpu.VMEM((size, 256), F32),
            pltpu.VMEM((size, 128), F32), pltpu.VMEM((16, width), F32)],
        cost_estimate=CHEAP, compiler_params=params(min(48, 8 + coarse_rows // 3)), name="coarse",
    )(rhs, message, message_other, *spread, *spread_other, basis, sup_hots, x)

    y_from = pair_swaps_near(y_first, y_second)
    extended = shape(adjoints, FIELD, width)
    r, coef, y = pl.pallas_call(
        correct_kernel,
        out_shape=(extended, shape(6, FIELD, width), extended),
        scratch_shapes=fine_scratch(adjoints, width) + [pltpu.VMEM((4 * grid_rows, width), F32)],
        cost_estimate=CHEAP, compiler_params=params(16), name="correct",
    )(r, b, e, n, from_second, from_first, x, high, low, basis)
    field = pl.pallas_call(
        post_kernel,
        out_shape=shape(adjoints, *row_dims),
        scratch_shapes=[pltpu.VMEM((adjoints, 40, width), F32)],
        cost_estimate=CHEAP, compiler_params=params(16), name="post",
    )(r, coef, y, *y_from)
    return field, coarse


def solution(mesh):
    return jax.shard_map(
        body,
        mesh=mesh,
        in_specs=(
            P(None, ("wide", "narrow"), None),
            P(("wide", "narrow"), None),
            P(("wide", "narrow"), None),
            P(("wide", "narrow"), None),
            P(("wide", "narrow"), None),
            P(("wide", "narrow"), None, None),
            P("wide", None),
            P("wide", None, None),
            P("wide", None, None),
        ),
        out_specs=(P(None, ("wide", "narrow"), None), P("wide", None)),
        check_vma=False,
    )
```

```python
import functools

import jax
import jax.numpy as jnp
from jax import lax
from jax.experimental import pallas as pl
from jax.experimental.pallas import tpu as pltpu
from jax.sharding import PartitionSpec as P

SWEEPS = 2
COARSE_SWEEPS = 3
relax_weight = 0.7

BOTH = ("wide", "narrow")
HALO = 3
FIELD = 24
PIECE = 80
F32 = jnp.float32
BF16 = jnp.bfloat16


def swap(value, axis, bits):
    size = lax.axis_size(axis)
    return lax.ppermute(value, axis, [(i, i ^ bits) for i in range(size)])


def pair_swaps(to_first, to_second):
    count = lax.axis_size(BOTH)
    first = lax.ppermute(to_first, BOTH, [(i, i ^ 1) for i in range(count)])
    odd = [(i, i + 1) for i in range(1, count - 1, 2)] + [(count - 1, 0)]
    second = lax.ppermute(to_second, BOTH, odd + [(target, source) for source, target in odd])
    return first, second


def pair_swaps_near(to_first, to_second):
    count, across = lax.axis_size(BOTH), lax.axis_size("narrow")
    first = lax.ppermute(to_first, BOTH, [(i, i ^ 1) for i in range(count)])
    inner = lax.ppermute(to_second, BOTH, [(i, i ^ (3 if i % 4 in (1, 2) else across)) for i in range(count)])
    outer = [(i, i + 1) for i in range(3, count - 1, 4)]
    outer += [(i, i ^ across) for i in range(2, count, 4) if i < i ^ across]
    rest = [0] + list(range(1, count, 4)) + [count - 1]
    outer += list(zip(rest[::2], rest[1::2]))
    outer = lax.ppermute(to_second, BOTH, outer + [(target, source) for source, target in outer])
    return first, inner, outer


def tie(values, after):
    count = len(values)
    spec = pl.BlockSpec(memory_space=pl.ANY)
    return list(pl.pallas_call(
        lambda *refs: None, out_shape=[jax.ShapeDtypeStruct(v.shape, v.dtype) for v in values],
        in_specs=[spec] * (count + 1), out_specs=[spec] * count,
        input_output_aliases={i: i for i in range(count)}, cost_estimate=CHEAP, compiler_params=params(1), name="tie",
    )(*values, after))


def rounds_of(size):
    rounds, base = [], 1
    while base < size:
        span = 4 if base * 4 <= size else 2
        rounds.append([base * k for k in range(1, span)])
        base *= span
    return rounds


def share_kernel(value, one, two, out):
    second = lax.rem(lax.axis_index("wide"), 2) == 1
    out[...] = one[...] + jnp.where(second, two[...], value[...])


def sum_shared(value, axis, masks):
    if len(masks) == 1:
        return value + swap(value, axis, masks[0])
    count, across = lax.axis_size(BOTH), lax.axis_size("narrow")
    unit = across if axis == "wide" else 1
    near, far, farthest = [unit * mask for mask in masks]
    one = lax.ppermute(value, BOTH, [(i, i ^ (far if i & across else near)) for i in range(count)])
    two = lax.ppermute(value, BOTH, [(i, i ^ (farthest if i & across else near)) for i in range(count)])
    value = pl.pallas_call(
        share_kernel, out_shape=jax.ShapeDtypeStruct(value.shape, value.dtype),
        cost_estimate=CHEAP, compiler_params=params(1), name="share",
    )(value, one, two)
    return value + swap(value, "wide", 1)


def bits_of(size):
    return [1 << i for i in range(size.bit_length() - 1)]


def place():
    wide, narrow = lax.axis_index("wide"), lax.axis_index("narrow")
    line = wide * lax.axis_size("narrow") + narrow
    count = lax.axis_size("wide") * lax.axis_size("narrow")
    return line, count


def packed_rows(count):
    return count * PIECE + 8 * ((count + 7) // 8)


def lanes(shape):
    return lax.broadcasted_iota(jnp.int32, shape, len(shape) - 1)


def rows(shape):
    return lax.broadcasted_iota(jnp.int32, shape, len(shape) - 2)


def split(value):
    high = value.astype(BF16)
    return high, (value - high.astype(F32)).astype(BF16)


def dot(left, right):
    return lax.dot_general(left, right, (((1,), (0,)), ((), ())), preferred_element_type=F32)


def dot_t(left, right):
    return lax.dot_general(left, right, (((1,), (1,)), ((), ())), preferred_element_type=F32)


def half_turn(value):
    return pltpu.roll(value, 64, 1)


def copy_all(pairs, sems):
    copies = [pltpu.make_async_copy(source, target, sems.at[i]) for i, (source, target) in enumerate(pairs)]
    for copy in copies:
        copy.start()

    def wait():
        for copy in copies:
            copy.wait()

    return wait


def pack_row(matrix, inverse, put):
    put(0, matrix)
    put(64, jnp.concatenate([inverse[16 * t:16 * t + 16, :] for t in range(4)], axis=1))


def begin_kernel(owned, r_in, b_in, e_in, n_in, links_in, coupling_in, inverses_in, first, second, own, block,
                 r, b, e, n, links, coupling, inverses, sems):
    wait = copy_all([(r_in, r), (b_in, b), (e_in, e), (n_in, n), (links_in, links), (coupling_in, coupling),
                     (inverses_in, inverses)], sems)
    grid_rows = b.shape[0]
    line, _ = place()
    even = lax.rem(line, 2) == 0
    q = lax.rem(lax.axis_index("narrow"), owned)
    wait()

    def message(start, north_start):
        parts = [r[a, start:start + HALO, :] for a in range(r.shape[0])]
        parts += [b[start:start + HALO, :], e[start:start + HALO, :]]
        parts += [n[north_start:north_start + HALO + 1, :], jnp.zeros((2, b.shape[1]), F32)]
        return parts

    top = message(0, 0)
    bottom = message(grid_rows - HALO, grid_rows - HALO - 1)
    at = 0
    for low, high in zip(top, bottom):
        size = low.shape[0]
        first[at:at + size, :] = jnp.where(even, high, low)
        second[at:at + size, :] = jnp.where(even, low, high)
        at += size

    lane, row = lanes((8, 256)), rows((8, 256))
    tail = jnp.zeros((8, 256), F32)
    for j_rel in range(owned):
        j = jnp.bitwise_xor(q, j_rel)

        def put(at, value, base=j_rel * PIECE):
            block[base + at:base + at + value.shape[0], :] = value
            if base == 0:
                own[at:at + value.shape[0], :] = value

        pack_row(coupling[j], inverses[j], put)
        for l in range(links.shape[1]):
            tail = jnp.where((row == j_rel) & (lane == l), links[j, l].astype(F32), tail)
    block[owned * PIECE:owned * PIECE + 8, :] = tail
    own[PIECE:PIECE + 8, :] = tail


def prepare_kernel(owned, coarse_rows, r_in, b_in, e_in, n_in, support_in, basis_in,
                   r_out, b_out, e_out, n_out, basis, hots, sup_hots, support, sems):
    q = lax.rem(lax.axis_index("narrow"), owned)
    mine = lax.axis_index("wide") * owned + q
    wait_support = copy_all([(support_in, support)], sems.at[pl.ds(0, 1)])
    part = basis.shape[0] // 8
    parts = [pl.ds(part * i, part) for i in range(8)]
    wait = copy_all([(basis_in.at[at], basis.at[at]) for at in parts]
                    + [(r_in, r_out), (b_in, b_out), (e_in, e_out), (n_in, n_out)], sems.at[pl.ds(1, 12)])
    wait_support()

    blocks = support.shape[1]
    rows4 = 4 * blocks
    size = 4 * coarse_rows

    def chosen(which, index):
        g, h = lax.shift_right_logical(index, 4), jnp.bitwise_and(lax.shift_right_logical(index, 3), 1)
        p = jnp.bitwise_and(lax.shift_right_logical(index, 2), 1)
        return jnp.where(which == g * 4 + p * 2 + h, 1.0, 0.0).astype(BF16)

    value = support[...].astype(F32).astype(BF16)
    column = dot_t(chosen(lanes((rows4, blocks)), rows((rows4, blocks))), value)
    line = dot(value, chosen(rows((blocks, rows4)), lanes((blocks, rows4))))
    line = line.astype(jnp.int32) * 4 + jnp.bitwise_and(lanes((4, rows4)), 3)
    at = rows((size, rows4))
    for k in range(4):
        base, left = (k % 2) * size, (k // 2) * rows4
        hots[base:base + size, left:left + rows4] = jnp.where(at == line[k:k + 1, :], 1.0, 0.0).astype(BF16)
    column = jnp.bitwise_xor(column.astype(jnp.int32), mine) * 4 + jnp.bitwise_and(rows((rows4, 4)), 3)
    across = lanes((rows4, size))
    for k in range(4):
        sup_hots[rows4 * k:rows4 * k + rows4, :] = jnp.where(across == column[:, k:k + 1], 1.0, 0.0).astype(BF16)

    wait()


def stack_kernel(*refs):
    fetched, gathered, far = refs[:-5], refs[-2], refs[-1]
    owned = far.shape[0] // len(fetched)
    for i, piece in enumerate(fetched):
        gathered[PIECE * i:PIECE * i + PIECE, :] = piece[0:PIECE, :]
        far[owned * i:owned * i + owned, :] = piece[PIECE:PIECE + owned, :]


def add_kernel(one, two, out):
    half = out.shape[0] // 2
    for i in range(2):
        block = slice(128 * i, 128 * i + 128)
        out[half * i:half * i + half, :] = one[0:half, block] + two[0:half, block]


class Fine:
    def __init__(self, r, b, e, n, from_first, from_second, rx, bx, ex, nx, field):
        line, count = place()
        even = lax.rem(line, 2) == 0
        low_ok, high_ok = line > 0, line < count - 1
        one, two = from_first[...], from_second[...]
        low = jnp.where(low_ok, jnp.where(even, two, one), 0.0)
        high = jnp.where(high_ok, jnp.where(even, one, two), 0.0)
        self.even, self.low_ok, self.high_ok = even, low_ok, high_ok
        self.adjoints, self.grid_rows, width = r.shape
        top = HALO + self.grid_rows
        zeros = jnp.zeros((8, width), F32)
        for a in range(self.adjoints):
            rx[a, 16:24, :] = zeros
            rx[a, 0:HALO, :] = low[3 * a:3 * a + 3]
            rx[a, HALO:top, :] = r[a]
            rx[a, top:top + HALO, :] = high[3 * a:3 * a + 3]
            field[a, 0:8, :] = zeros
            field[a, 32:40, :] = zeros
        bx[16:24, :] = zeros
        bx[0:HALO, :] = low[12:15]
        bx[HALO:top, :] = b[...]
        bx[top:top + HALO, :] = high[12:15]
        ex[16:24, :] = zeros
        ex[0:HALO, :] = low[15:18]
        ex[HALO:top, :] = e[...]
        ex[top:top + HALO, :] = high[15:18]
        nx[16:24, :] = zeros
        nx[24:32, :] = zeros
        nx[0:HALO + 1, :] = low[18:22]
        nx[HALO + 1:top + 1, :] = n[...]
        nx[top + 1:top + 1 + HALO, :] = high[18:21]
        self.r = rx[...]
        self.east = ex[...]
        self.north = nx[1:1 + FIELD, :]
        self.south = nx[0:FIELD, :]
        self.west = pltpu.roll(self.east, 1, 1)
        self.diagonal = bx[...] + self.east + self.west + self.north + self.south
        t = rows((FIELD, width))
        valid = ((t >= HALO) | low_ok) & ((t < top) | high_ok) & (t < top + HALO)
        self.scale = jnp.where(valid, relax_weight / jnp.where(valid, self.diagonal, 1.0), 0.0)
        self.field = field
        self.width = width

    def apply(self, x):
        self.field[:, 8:32, :] = x
        above = self.field[:, 7:31, :]
        below = self.field[:, 9:33, :]
        east = pltpu.roll(x, self.width - 1, 2)
        west = pltpu.roll(x, 1, 2)
        return self.diagonal * x - self.north * below - self.south * above - self.east * east - self.west * west

    def sweep(self, x):
        return x + self.scale * (self.r - self.apply(x))


    def keep(self, r_out, coef_out):
        r_out[...] = self.r
        for i, value in enumerate((self.diagonal, self.scale, self.north, self.south, self.east, self.west)):
            coef_out[i] = value


class Kept(Fine):
    def __init__(self, r, coef, field):
        line, count = place()
        self.even, self.low_ok, self.high_ok = lax.rem(line, 2) == 0, line > 0, line < count - 1
        self.r, self.field = r[...], field
        self.diagonal, self.scale, self.north, self.south, self.east, self.west = [coef[i] for i in range(6)]
        self.adjoints, _, self.width = r.shape


def fine_scratch(adjoints, width):
    return [
        pltpu.VMEM((adjoints, FIELD, width), F32),
        pltpu.VMEM((FIELD, width), F32),
        pltpu.VMEM((FIELD, width), F32),
        pltpu.VMEM((32, width), F32),
        pltpu.VMEM((adjoints, 40, width), F32),
    ]


def restrict_kernel(coarse_rows, r, b, e, n, from_second, from_first, basis, hots,
                    block, gathered, far, out, x_out, rx, bx, ex, nx, field, by_row, contrib):
    fine = Fine(r, b, e, n, from_first, from_second, rx, bx, ex, nx, field)
    x = fine.scale * fine.r
    for step in range(SWEEPS - 1):
        x = fine.sweep(x)
    resid = fine.r - fine.apply(x)
    for a in range(fine.adjoints):
        x_out[a] = field[a, 8 + HALO:8 + HALO + fine.grid_rows, :]
    field[:, 8:32, :] = resid
    for a in range(fine.adjoints):
        by_row[pl.ds(a, fine.grid_rows, stride=4), :] = field[a, 8 + HALO:8 + HALO + fine.grid_rows, :]
    left = lanes((8, 128)) < 64
    upper = rows((8, 128)) < 4
    for g in range(fine.grid_rows // 2):
        z = by_row[8 * g:8 * g + 8, :]
        parts = []
        for here in (left, ~left):
            held = jnp.where(here, z, 0.0)
            parts.append(jnp.concatenate([jnp.where(upper, held, 0.0), jnp.where(upper, 0.0, held)], axis=1))
        high, low = split(jnp.concatenate(parts, axis=0))
        near = slice(256 * g, 256 * g + 256)
        w_high, w_low = split(basis[near, :])
        both = dot(jnp.concatenate([high, low], axis=0), w_high)
        contrib[16 * g:16 * g + 16, :] = both[0:16] + both[16:32] + dot(high, w_low)
    c_high, c_low = split(contrib[...])
    weights = jnp.concatenate([
        jnp.concatenate([c_high[:, 0:128], c_low[:, 0:128]], axis=1),
        jnp.concatenate([c_high[:, 128:256], c_low[:, 128:256]], axis=1)], axis=0)
    size = 4 * coarse_rows
    total = dot(hots[...], weights)
    total = total[:, 0:128] + total[:, 128:256]
    here = lanes((size, 128)) < 64
    even = jnp.where(here, total[0:size], 0.0)
    odd = jnp.where(here, 0.0, total[size:2 * size])
    mid = size // 2
    packed = even[0:mid] + half_turn(odd[0:mid]) + half_turn(even[mid:size]) + odd[mid:size]
    half = mid // 2
    out[0:half, 0:128] = packed[0:half]
    out[0:half, 128:256] = packed[half:mid]
    out[half:half + block.shape[0], :] = block[...]
    at = half + block.shape[0]
    out[at:at + gathered.shape[0], :] = gathered[...]
    at += gathered.shape[0]
    out[at:at + far.shape[0], :] = far[...]


def prolong(group, high, low, basis):
    near = slice(16 * group, 16 * group + 16)
    block = slice(256 * group, 256 * group + 256)
    high = high[near, :]
    w_high, w_low = split(basis[block, :])
    both = dot_t(jnp.concatenate([high, low[near, :]], axis=0), w_high)
    got = both[0:16] + both[16:32] + dot_t(high, w_low)
    upper = rows((8, 128)) < 4
    halves = [jnp.where(upper, got[8 * h:8 * h + 8, 0:128], got[8 * h:8 * h + 8, 128:256]) for h in range(2)]
    return jnp.where(lanes((8, 128)) < 64, halves[0], halves[1])


def coarse_kernel(owned, coarse_rows, zs, rhs_ref, message, message_other, *refs):
    spread, spread_other = refs[:owned - 1], refs[owned - 1:2 * owned - 2]
    (basis, sup_hots, x_ref, coarse_ref, high_out, low_out, first, second,
     w_high, w_low, w_inv, link_rows, hots, product, u_ref, by_row) = refs[2 * owned - 2:]
    size = 4 * coarse_rows
    wide, narrow = lax.axis_index("wide"), lax.axis_index("narrow")
    q = lax.rem(narrow, owned)
    mine = wide * owned + q

    lane16 = lanes((16, 128)) < 64
    lane64 = lanes((64, 128)) < 64
    at_own = coarse_rows
    at_fetched = at_own + packed_rows(owned)
    for z_rel in range(zs):
        for c_rel, (fetched, others) in enumerate(((message, spread), (message_other, spread_other))):
            for j_rel in range(owned):
                i = (z_rel * 2 + c_rel) * owned + j_rel
                at_links = at_own + owned * PIECE + j_rel
                if z_rel > 0:
                    at_links = at_fetched + (zs - 1) * PIECE + (z_rel - 1) * owned + j_rel
                if z_rel == 0:
                    piece, base = fetched, at_own + j_rel * PIECE
                elif j_rel == 0:
                    piece, base = fetched, at_fetched + (z_rel - 1) * PIECE
                else:
                    piece, base = others[j_rel - 1], (z_rel - 1) * PIECE
                high, low = split(piece[base:base + 64, :])
                w_high[64 * i:64 * i + 64, :] = high
                w_low[64 * i:64 * i + 64, :] = low
                quarters = []
                for half in range(2):
                    packed = piece[base + 64:base + 80, 128 * half:128 * half + 128]
                    turned = half_turn(packed)
                    quarters += [jnp.where(lane16, packed, turned), jnp.where(lane16, turned, packed)]
                high, low = split(jnp.concatenate(quarters, axis=0))
                w_inv[64 * i:64 * i + 64, :] = jnp.where(lane64, high.astype(F32), low.astype(F32)).astype(BF16)
                link_rows[4 * i:4 * i + 4, :] = jnp.broadcast_to(fetched[at_links:at_links + 1, 0:128], (4, 128))

    lane = lanes((size, size))
    a_col = jnp.bitwise_and(rows((size, 1)), 3)
    for l in range(4):
        target = jnp.bitwise_xor(link_rows[:, l:l + 1].astype(jnp.int32), mine) * 4 + a_col
        hots[size * l:size * l + size, :] = jnp.where(lane == target, 1.0, 0.0).astype(BF16)

    here = lanes((size, 128)) < 64
    packed = rhs_ref[...]
    turned = half_turn(packed)
    here_mid = here[0:size // 2]
    rhs = jnp.concatenate([jnp.where(here_mid, packed, turned), jnp.where(here_mid, turned, packed)], axis=0)

    def hi_lo(value):
        high, low = split(value)
        return jnp.concatenate([high, low], axis=1)

    u_ref[...] = rhs
    for i in range(coarse_rows):
        link_rows[4 * i:4 * i + 4, :] = u_ref[pl.ds(jnp.bitwise_xor(mine, i) * 4, 4), :]
    rhs = link_rows[...]

    own_block = jnp.bitwise_and(lax.shift_right_logical(rows((size, 256)), 2), 3) == lax.shift_right_logical(
        lanes((size, 256)), 6)

    def fold():
        value = jnp.where(own_block, product[...], 0.0)
        value = value[:, 0:128] + value[:, 128:256]
        return value + half_turn(value)

    def apply_inverse(value):
        high, low = split(value)
        low = jnp.where(here, low.astype(F32), 0.0).astype(BF16)
        for g in range(coarse_rows // 4):
            near = slice(16 * g, 16 * g + 16)
            both = dot_t(jnp.concatenate([high[near], low[near]], axis=0), w_inv[256 * g:256 * g + 256, :])
            product[near, :] = both[0:16] + both[16:32]
        return fold()

    def pick(got, step):
        sel = lanes((step, 128)) < 64
        high = [jnp.where(sel, got[step * k:step * k + step, 0:128], got[step * k + step:step * k + 2 * step, 0:128])
                for k in (0, 2)]
        low = [jnp.where(sel, got[step * k:step * k + step, 128:256],
                         got[step * k + step:step * k + 2 * step, 128:256]) for k in (0, 2)]
        return jnp.concatenate(high, axis=1).astype(BF16), jnp.concatenate(low, axis=1).astype(BF16)

    u = apply_inverse(rhs)
    for step in range(COARSE_SWEEPS):
        high, low = pick(dot(hots[...], hi_lo(u)), size)
        for g in range(coarse_rows // 4):
            near = slice(16 * g, 16 * g + 16)
            block = slice(256 * g, 256 * g + 256)
            both = dot_t(jnp.concatenate([high[near], low[near]], axis=0), w_high[block, :])
            product[near, :] = both[0:16] + both[16:32] + dot_t(high[near], w_low[block, :])
        u = apply_inverse(rhs + fold())

    u_ref[0:4 * owned, :] = u[0:4 * owned]
    here1 = lanes((1, 128)) < 64
    for j in range(owned):
        got = u_ref[pl.ds(jnp.bitwise_xor(q, j) * 4, 4), :]
        coarse_ref[j:j + 1, 0:128] = jnp.where(here1, got[0:1], got[1:2])
        coarse_ref[j:j + 1, 128:256] = jnp.where(here1, got[2:3], got[3:4])

    blocks4 = sup_hots.shape[0] // 4
    high, low = pick(dot(sup_hots[...], hi_lo(u)), blocks4)
    high_out[...] = high
    low_out[...] = low
    line, _ = place()
    even = lax.rem(line, 2) == 0
    adjoints, grid_rows, _ = x_ref.shape
    by_row[0:8, :] = prolong(0, high, low, basis)
    by_row[8:16, :] = prolong(grid_rows // 2 - 1, high, low, basis)
    for a in range(adjoints):
        edge = by_row[pl.ds(a, 4, stride=4), :]
        top = x_ref[a, 0:2, :] + edge[0:2]
        bottom = x_ref[a, grid_rows - 2:grid_rows, :] + edge[2:4]
        first[2 * a:2 * a + 2, :] = jnp.where(even, bottom, top)
        second[2 * a:2 * a + 2, :] = jnp.where(even, top, bottom)


def correct_kernel(r, b, e, n, from_second, from_first, x_ref, high, low, basis,
                   r_out, coef_out, y_out, rx, bx, ex, nx, field, by_row):
    Fine(r, b, e, n, from_first, from_second, rx, bx, ex, nx, field).keep(r_out, coef_out)
    adjoints, grid_rows, width = x_ref.shape
    for g in range(grid_rows // 2):
        by_row[8 * g:8 * g + 8, :] = prolong(g, high, low, basis)
    for a in range(adjoints):
        y_out[a, 0:8, :] = jnp.zeros((8, width), F32)
        y_out[a, 16:24, :] = jnp.zeros((8, width), F32)
        y_out[a, HALO:HALO + grid_rows, :] = x_ref[a] + by_row[pl.ds(a, grid_rows, stride=4), :]


def post_kernel(r, coef, y_ref, y_first, y_inner, y_outer, out, field):
    fine = Kept(r, coef, field)
    in_line = lax.rem(place()[0], 4)
    one, two = y_first[...], jnp.where((in_line == 1) | (in_line == 2), y_inner[...], y_outer[...])
    low = jnp.where(fine.low_ok, jnp.where(fine.even, two, one), 0.0)
    high = jnp.where(fine.high_ok, jnp.where(fine.even, one, two), 0.0)
    grid_rows = out.shape[1]
    start, top = 8 + HALO, 8 + HALO + grid_rows
    field[:, 0:8, :] = jnp.zeros((fine.adjoints, 8, fine.width), F32)
    field[:, 32:40, :] = jnp.zeros((fine.adjoints, 8, fine.width), F32)
    field[:, 8:32, :] = y_ref[...]
    for a in range(fine.adjoints):
        field[a, start - 2:start, :] = low[2 * a:2 * a + 2]
        field[a, top:top + 2, :] = high[2 * a:2 * a + 2]
    x = field[:, 8:32, :]
    for step in range(SWEEPS):
        x = fine.sweep(x)
    field[:, 8:32, :] = x
    for a in range(fine.adjoints):
        out[a] = field[a, start:top, :]


def shape(*dims, kind=F32):
    return jax.ShapeDtypeStruct(dims, kind)


def params(mebibytes):
    return pltpu.CompilerParams(vmem_limit_bytes=mebibytes * 2 ** 20)


def stay(array):
    return pltpu.with_memory_space_constraint(array, pltpu.HBM)


CHEAP = pl.CostEstimate(flops=1, bytes_accessed=1, transcendentals=0)


def body(right_sides, brinkman, east_faces, north_faces, support, basis, links, coarse_block_inverses, coarse_coupling):
    adjoints, grid_rows, width = right_sides.shape
    blocks, block_size, _ = basis.shape
    owned = coarse_block_inverses.shape[0]
    coarse_rows = owned * lax.axis_size("wide")
    zs = lax.axis_size("wide") // 2
    size = 4 * coarse_rows
    basis = basis.reshape(blocks * block_size, -1)

    in_hbm = pl.BlockSpec(memory_space=pltpu.HBM)
    anywhere = pl.BlockSpec(memory_space=pl.ANY)
    in_vmem = pl.BlockSpec(memory_space=pltpu.VMEM)
    row_dims = (grid_rows, width)
    message = shape(24, width)
    fine_inputs = tuple(map(stay, (right_sides, brinkman, east_faces, north_faces)))
    coarse_inputs = tuple(map(stay, (links, coarse_coupling, coarse_block_inverses)))
    to_first, to_second, own, block = pl.pallas_call(
        functools.partial(begin_kernel, owned),
        out_shape=(message, message, shape(packed_rows(1), 256), shape(packed_rows(owned), 256)),
        in_specs=[in_hbm] * 7,
        scratch_shapes=[
            pltpu.VMEM((adjoints, *row_dims), F32), pltpu.VMEM(row_dims, F32), pltpu.VMEM(row_dims, F32),
            pltpu.VMEM(row_dims, F32), pltpu.SMEM(links.shape, jnp.int32), pltpu.VMEM(coarse_coupling.shape, F32),
            pltpu.VMEM(coarse_block_inverses.shape, F32), pltpu.SemaphoreType.DMA((7,))],
        cost_estimate=CHEAP, compiler_params=params(16), name="begin",
    )(*fine_inputs, *coarse_inputs)
    from_first, from_second = pair_swaps(to_first, to_second)
    fetched = [swap(own, "wide", 2 * k) for k in range(1, zs)]

    rows4 = adjoints * blocks
    r, b, e, n, basis, hots, sup_hots = pl.pallas_call(
        functools.partial(prepare_kernel, owned, coarse_rows),
        out_shape=(shape(adjoints, *row_dims), shape(*row_dims), shape(*row_dims), shape(*row_dims),
                   shape(*basis.shape), shape(2 * size, 2 * rows4, kind=BF16), shape(4 * rows4, size, kind=BF16)),
        in_specs=[in_hbm] * 6,
        scratch_shapes=[pltpu.VMEM((4, blocks), jnp.int32), pltpu.SemaphoreType.DMA((13,))],
        cost_estimate=CHEAP, compiler_params=params(16), name="prepare",
    )(*fine_inputs, stay(support.T), stay(basis))

    height = (zs - 1) * PIECE
    far_rows = (zs - 1) * owned
    gathered, far = pl.pallas_call(
        stack_kernel, out_shape=(shape(height, 256), shape(far_rows, 256)),
        in_specs=[in_vmem] * (zs - 1) + [anywhere] * 3,
        cost_estimate=CHEAP, compiler_params=params(4), name="stack",
    )(*fetched, from_second, from_first, hots)
    spread = [swap(gathered, "narrow", k) for k in range(1, owned)]

    half = coarse_rows
    message, x = pl.pallas_call(
        functools.partial(restrict_kernel, coarse_rows),
        out_shape=(shape(half + packed_rows(owned) + height + far_rows, 256), shape(adjoints, *row_dims)),
        scratch_shapes=fine_scratch(adjoints, width) + [
            pltpu.VMEM((4 * grid_rows, width), F32), pltpu.VMEM((rows4, 256), F32)],
        cost_estimate=CHEAP, compiler_params=params(16), name="restrict",
    )(r, b, e, n, from_second, from_first, basis, hots, block, gathered, far)

    message_other = swap(message, "wide", 1)
    rhs = pl.pallas_call(
        add_kernel, out_shape=shape(2 * half, 128), cost_estimate=CHEAP, compiler_params=params(4), name="add",
    )(message, message_other)
    for masks in rounds_of(zs):
        rhs = sum_shared(rhs, "wide", [2 * k for k in masks])
    spread = tie(spread, rhs)
    spread_other = [swap(piece, "wide", 1) for piece in spread]
    for masks in rounds_of(lax.axis_size("narrow")):
        rhs = sum([swap(rhs, "narrow", k) for k in masks], rhs)

    near = shape(rows4, 256, kind=BF16)
    coarse, high, low, y_first, y_second = pl.pallas_call(
        functools.partial(coarse_kernel, owned, coarse_rows, zs),
        out_shape=(shape(owned, 256), near, near, shape(8, width), shape(8, width)),
        scratch_shapes=[
            pltpu.VMEM((64 * coarse_rows, 256), BF16), pltpu.VMEM((64 * coarse_rows, 256), BF16),
            pltpu.VMEM((64 * coarse_rows, 128), BF16), pltpu.VMEM((size, 128), F32),
            pltpu.VMEM((4 * size, size), BF16), pltpu.VMEM((size, 256), F32),
            pltpu.VMEM((size, 128), F32), pltpu.VMEM((16, width), F32)],
        cost_estimate=CHEAP, compiler_params=params(min(48, 8 + coarse_rows // 3)), name="coarse",
    )(rhs, message, message_other, *spread, *spread_other, basis, sup_hots, x)

    y_from = pair_swaps_near(y_first, y_second)
    extended = shape(adjoints, FIELD, width)
    r, coef, y = pl.pallas_call(
        correct_kernel,
        out_shape=(extended, shape(6, FIELD, width), extended),
        scratch_shapes=fine_scratch(adjoints, width) + [pltpu.VMEM((4 * grid_rows, width), F32)],
        cost_estimate=CHEAP, compiler_params=params(16), name="correct",
    )(r, b, e, n, from_second, from_first, x, high, low, basis)
    field = pl.pallas_call(
        post_kernel,
        out_shape=shape(adjoints, *row_dims),
        scratch_shapes=[pltpu.VMEM((adjoints, 40, width), F32)],
        cost_estimate=CHEAP, compiler_params=params(16), name="post",
    )(r, coef, y, *y_from)
    return field, coarse


def solution(mesh):
    return jax.shard_map(
        body,
        mesh=mesh,
        in_specs=(
            P(None, ("wide", "narrow"), None),
            P(("wide", "narrow"), None),
            P(("wide", "narrow"), None),
            P(("wide", "narrow"), None),
            P(("wide", "narrow"), None),
            P(("wide", "narrow"), None, None),
            P("wide", None),
            P("wide", None, None),
            P("wide", None, None),
        ),
        out_specs=(P(None, ("wide", "narrow"), None), P("wide", None)),
        check_vma=False,
    )
```

```python
import functools

import jax
import jax.numpy as jnp
from jax import lax
from jax.experimental import pallas as pl
from jax.experimental.pallas import tpu as pltpu
from jax.sharding import PartitionSpec as P

SWEEPS = 2
COARSE_SWEEPS = 3
relax_weight = 0.7

BOTH = ("wide", "narrow")
HALO = 3
FIELD = 24
PIECE = 80
F32 = jnp.float32
BF16 = jnp.bfloat16


def swap(value, axis, bits):
    size = lax.axis_size(axis)
    return lax.ppermute(value, axis, [(i, i ^ bits) for i in range(size)])


def pair_swaps(to_first, to_second):
    count = lax.axis_size(BOTH)
    first = lax.ppermute(to_first, BOTH, [(i, i ^ 1) for i in range(count)])
    odd = [(i, i + 1) for i in range(1, count - 1, 2)] + [(count - 1, 0)]
    second = lax.ppermute(to_second, BOTH, odd + [(target, source) for source, target in odd])
    return first, second


def pair_swaps_near(to_first, to_second):
    count, across = lax.axis_size(BOTH), lax.axis_size("narrow")
    first = lax.ppermute(to_first, BOTH, [(i, i ^ 1) for i in range(count)])
    inner = lax.ppermute(to_second, BOTH, [(i, i ^ (3 if i % 4 in (1, 2) else across)) for i in range(count)])
    outer = [(i, i + 1) for i in range(3, count - 1, 4)]
    outer += [(i, i ^ across) for i in range(2, count, 4) if i < i ^ across]
    rest = [0] + list(range(1, count, 4)) + [count - 1]
    outer += list(zip(rest[::2], rest[1::2]))
    outer = lax.ppermute(to_second, BOTH, outer + [(target, source) for source, target in outer])
    return first, inner, outer


def tie(values, after):
    count = len(values)
    spec = pl.BlockSpec(memory_space=pl.ANY)
    return list(pl.pallas_call(
        lambda *refs: None, out_shape=[jax.ShapeDtypeStruct(v.shape, v.dtype) for v in values],
        in_specs=[spec] * (count + 1), out_specs=[spec] * count,
        input_output_aliases={i: i for i in range(count)}, cost_estimate=CHEAP, compiler_params=params(1), name="tie",
    )(*values, after))


def rounds_of(size):
    rounds, base = [], 1
    while base < size:
        span = 4 if base * 4 <= size else 2
        rounds.append([base * k for k in range(1, span)])
        base *= span
    return rounds


def share_kernel(value, one, two, out):
    second = lax.rem(lax.axis_index("wide"), 2) == 1
    out[...] = one[...] + jnp.where(second, two[...], value[...])


def sum_shared(value, axis, masks):
    if len(masks) == 1:
        return value + swap(value, axis, masks[0])
    count, across = lax.axis_size(BOTH), lax.axis_size("narrow")
    unit = across if axis == "wide" else 1
    near, far, farthest = [unit * mask for mask in masks]
    one = lax.ppermute(value, BOTH, [(i, i ^ (far if i & across else near)) for i in range(count)])
    two = lax.ppermute(value, BOTH, [(i, i ^ (farthest if i & across else near)) for i in range(count)])
    value = pl.pallas_call(
        share_kernel, out_shape=jax.ShapeDtypeStruct(value.shape, value.dtype),
        cost_estimate=CHEAP, compiler_params=params(1), name="share",
    )(value, one, two)
    return value + swap(value, "wide", 1)


def bits_of(size):
    return [1 << i for i in range(size.bit_length() - 1)]


def place():
    wide, narrow = lax.axis_index("wide"), lax.axis_index("narrow")
    line = wide * lax.axis_size("narrow") + narrow
    count = lax.axis_size("wide") * lax.axis_size("narrow")
    return line, count


def packed_rows(count):
    return count * PIECE + 8 * ((count + 7) // 8)


def lanes(shape):
    return lax.broadcasted_iota(jnp.int32, shape, len(shape) - 1)


def rows(shape):
    return lax.broadcasted_iota(jnp.int32, shape, len(shape) - 2)


def split(value):
    high = value.astype(BF16)
    return high, (value - high.astype(F32)).astype(BF16)


def dot(left, right):
    return lax.dot_general(left, right, (((1,), (0,)), ((), ())), preferred_element_type=F32)


def dot_t(left, right):
    return lax.dot_general(left, right, (((1,), (1,)), ((), ())), preferred_element_type=F32)


def half_turn(value):
    return pltpu.roll(value, 64, 1)


def copy_all(pairs, sems):
    copies = [pltpu.make_async_copy(source, target, sems.at[i]) for i, (source, target) in enumerate(pairs)]
    for copy in copies:
        copy.start()

    def wait():
        for copy in copies:
            copy.wait()

    return wait


def packed_inverse(inverse):
    return jnp.concatenate([inverse[16 * t:16 * t + 16, :] for t in range(4)], axis=1)


def link_rows_of(owned, links, q):
    lane, row = lanes((8, 256)), rows((8, 256))
    tail = jnp.zeros((8, 256), F32)
    for j_rel in range(owned):
        for l in range(links.shape[1]):
            link = links[jnp.bitwise_xor(q, j_rel), l].astype(F32)
            tail = jnp.where((row == j_rel) & (lane == l), link, tail)
    return tail


def begin_kernel(owned, r_in, b_in, e_in, n_in, links_in, coupling_in, inverses_in, first, second, own,
                 r, b, e, n, links, inverse, sems):
    q = lax.rem(lax.axis_index("narrow"), owned)
    wait = copy_all([(r_in, r), (b_in, b), (e_in, e), (n_in, n), (links_in, links),
                     (coupling_in.at[q], own.at[pl.ds(0, 64)]), (inverses_in.at[q], inverse)], sems)
    grid_rows = b.shape[0]
    line, _ = place()
    even = lax.rem(line, 2) == 0
    wait()

    def message(start, north_start):
        parts = [r[a, start:start + HALO, :] for a in range(r.shape[0])]
        parts += [b[start:start + HALO, :], e[start:start + HALO, :]]
        parts += [n[north_start:north_start + HALO + 1, :], jnp.zeros((2, b.shape[1]), F32)]
        return parts

    top = message(0, 0)
    bottom = message(grid_rows - HALO, grid_rows - HALO - 1)
    at = 0
    for low, high in zip(top, bottom):
        size = low.shape[0]
        first[at:at + size, :] = jnp.where(even, high, low)
        second[at:at + size, :] = jnp.where(even, low, high)
        at += size

    own[64:PIECE, :] = packed_inverse(inverse[...])
    own[PIECE:PIECE + 8, :] = link_rows_of(owned, links, q)


def prepare_kernel(owned, coarse_rows, r_in, b_in, e_in, n_in, links_in, coupling_in, inverses_in, support_in, basis_in,
                   block, r_out, b_out, e_out, n_out, basis, hots, sup_hots, support, links, inverses, sems):
    q = lax.rem(lax.axis_index("narrow"), owned)
    mine = lax.axis_index("wide") * owned + q
    wait_support = copy_all([(support_in, support)], sems.at[pl.ds(0, 1)])
    wait_rows = copy_all([(coupling_in.at[jnp.bitwise_xor(q, j)], block.at[pl.ds(j * PIECE, 64)]) for j in range(owned)]
                         + [(links_in, links), (inverses_in, inverses)], sems.at[pl.ds(13, owned + 2)])
    part = basis.shape[0] // 8
    parts = [pl.ds(part * i, part) for i in range(8)]
    wait = copy_all([(basis_in.at[at], basis.at[at]) for at in parts]
                    + [(r_in, r_out), (b_in, b_out), (e_in, e_out), (n_in, n_out)], sems.at[pl.ds(1, 12)])
    wait_rows()
    for j in range(owned):
        block[j * PIECE + 64:j * PIECE + PIECE, :] = packed_inverse(inverses[jnp.bitwise_xor(q, j)])
    block[owned * PIECE:owned * PIECE + 8, :] = link_rows_of(owned, links, q)
    wait_support()

    blocks = support.shape[1]
    rows4 = 4 * blocks
    size = 4 * coarse_rows

    def chosen(which, index):
        g, h = lax.shift_right_logical(index, 4), jnp.bitwise_and(lax.shift_right_logical(index, 3), 1)
        p = jnp.bitwise_and(lax.shift_right_logical(index, 2), 1)
        return jnp.where(which == g * 4 + p * 2 + h, 1.0, 0.0).astype(BF16)

    value = support[...].astype(F32).astype(BF16)
    column = dot_t(chosen(lanes((rows4, blocks)), rows((rows4, blocks))), value)
    line = dot(value, chosen(rows((blocks, rows4)), lanes((blocks, rows4))))
    line = line.astype(jnp.int32) * 4 + jnp.bitwise_and(lanes((4, rows4)), 3)
    at = rows((size, rows4))
    for k in range(4):
        base, left = (k % 2) * size, (k // 2) * rows4
        hots[base:base + size, left:left + rows4] = jnp.where(at == line[k:k + 1, :], 1.0, 0.0).astype(BF16)
    column = jnp.bitwise_xor(column.astype(jnp.int32), mine) * 4 + jnp.bitwise_and(rows((rows4, 4)), 3)
    across = lanes((rows4, size))
    for k in range(4):
        sup_hots[rows4 * k:rows4 * k + rows4, :] = jnp.where(across == column[:, k:k + 1], 1.0, 0.0).astype(BF16)

    wait()


def stack_kernel(*refs):
    fetched, gathered, far = refs[:-5], refs[-2], refs[-1]
    owned = far.shape[0] // len(fetched)
    for i, piece in enumerate(fetched):
        gathered[PIECE * i:PIECE * i + PIECE, :] = piece[0:PIECE, :]
        far[owned * i:owned * i + owned, :] = piece[PIECE:PIECE + owned, :]


def add_kernel(one, two, out):
    half = out.shape[0] // 2
    for i in range(2):
        block = slice(128 * i, 128 * i + 128)
        out[half * i:half * i + half, :] = one[0:half, block] + two[0:half, block]


class Fine:
    def __init__(self, r, b, e, n, from_first, from_second, rx, bx, ex, nx, field):
        line, count = place()
        even = lax.rem(line, 2) == 0
        low_ok, high_ok = line > 0, line < count - 1
        one, two = from_first[...], from_second[...]
        low = jnp.where(low_ok, jnp.where(even, two, one), 0.0)
        high = jnp.where(high_ok, jnp.where(even, one, two), 0.0)
        self.even, self.low_ok, self.high_ok = even, low_ok, high_ok
        self.adjoints, self.grid_rows, width = r.shape
        top = HALO + self.grid_rows
        zeros = jnp.zeros((8, width), F32)
        for a in range(self.adjoints):
            rx[a, 16:24, :] = zeros
            rx[a, 0:HALO, :] = low[3 * a:3 * a + 3]
            rx[a, HALO:top, :] = r[a]
            rx[a, top:top + HALO, :] = high[3 * a:3 * a + 3]
            field[a, 0:8, :] = zeros
            field[a, 32:40, :] = zeros
        bx[16:24, :] = zeros
        bx[0:HALO, :] = low[12:15]
        bx[HALO:top, :] = b[...]
        bx[top:top + HALO, :] = high[12:15]
        ex[16:24, :] = zeros
        ex[0:HALO, :] = low[15:18]
        ex[HALO:top, :] = e[...]
        ex[top:top + HALO, :] = high[15:18]
        nx[16:24, :] = zeros
        nx[24:32, :] = zeros
        nx[0:HALO + 1, :] = low[18:22]
        nx[HALO + 1:top + 1, :] = n[...]
        nx[top + 1:top + 1 + HALO, :] = high[18:21]
        self.r = rx[...]
        self.east = ex[...]
        self.north = nx[1:1 + FIELD, :]
        self.south = nx[0:FIELD, :]
        self.west = pltpu.roll(self.east, 1, 1)
        self.diagonal = bx[...] + self.east + self.west + self.north + self.south
        t = rows((FIELD, width))
        valid = ((t >= HALO) | low_ok) & ((t < top) | high_ok) & (t < top + HALO)
        self.scale = jnp.where(valid, relax_weight / jnp.where(valid, self.diagonal, 1.0), 0.0)
        self.field = field
        self.width = width

    def apply(self, x):
        self.field[:, 8:32, :] = x
        above = self.field[:, 7:31, :]
        below = self.field[:, 9:33, :]
        east = pltpu.roll(x, self.width - 1, 2)
        west = pltpu.roll(x, 1, 2)
        return self.diagonal * x - self.north * below - self.south * above - self.east * east - self.west * west

    def sweep(self, x):
        return x + self.scale * (self.r - self.apply(x))


    def keep(self, r_out, coef_out):
        r_out[...] = self.r
        for i, value in enumerate((self.diagonal, self.scale, self.north, self.south, self.east, self.west)):
            coef_out[i] = value


class Kept(Fine):
    def __init__(self, r, coef, field):
        line, count = place()
        self.even, self.low_ok, self.high_ok = lax.rem(line, 2) == 0, line > 0, line < count - 1
        self.r, self.field = r[...], field
        self.diagonal, self.scale, self.north, self.south, self.east, self.west = [coef[i] for i in range(6)]
        self.adjoints, _, self.width = r.shape


def fine_scratch(adjoints, width):
    return [
        pltpu.VMEM((adjoints, FIELD, width), F32),
        pltpu.VMEM((FIELD, width), F32),
        pltpu.VMEM((FIELD, width), F32),
        pltpu.VMEM((32, width), F32),
        pltpu.VMEM((adjoints, 40, width), F32),
    ]


def restrict_kernel(coarse_rows, r, b, e, n, from_second, from_first, basis, hots,
                    block, gathered, far, out, x_out, rx, bx, ex, nx, field, by_row, contrib):
    fine = Fine(r, b, e, n, from_first, from_second, rx, bx, ex, nx, field)
    x = fine.scale * fine.r
    for step in range(SWEEPS - 1):
        x = fine.sweep(x)
    resid = fine.r - fine.apply(x)
    for a in range(fine.adjoints):
        x_out[a] = field[a, 8 + HALO:8 + HALO + fine.grid_rows, :]
    field[:, 8:32, :] = resid
    for a in range(fine.adjoints):
        by_row[pl.ds(a, fine.grid_rows, stride=4), :] = field[a, 8 + HALO:8 + HALO + fine.grid_rows, :]
    left = lanes((8, 128)) < 64
    upper = rows((8, 128)) < 4
    for g in range(fine.grid_rows // 2):
        z = by_row[8 * g:8 * g + 8, :]
        parts = []
        for here in (left, ~left):
            held = jnp.where(here, z, 0.0)
            parts.append(jnp.concatenate([jnp.where(upper, held, 0.0), jnp.where(upper, 0.0, held)], axis=1))
        high, low = split(jnp.concatenate(parts, axis=0))
        near = slice(256 * g, 256 * g + 256)
        w_high, w_low = split(basis[near, :])
        both = dot(jnp.concatenate([high, low], axis=0), w_high)
        contrib[16 * g:16 * g + 16, :] = both[0:16] + both[16:32] + dot(high, w_low)
    c_high, c_low = split(contrib[...])
    weights = jnp.concatenate([
        jnp.concatenate([c_high[:, 0:128], c_low[:, 0:128]], axis=1),
        jnp.concatenate([c_high[:, 128:256], c_low[:, 128:256]], axis=1)], axis=0)
    size = 4 * coarse_rows
    total = dot(hots[...], weights)
    total = total[:, 0:128] + total[:, 128:256]
    here = lanes((size, 128)) < 64
    even = jnp.where(here, total[0:size], 0.0)
    odd = jnp.where(here, 0.0, total[size:2 * size])
    mid = size // 2
    packed = even[0:mid] + half_turn(odd[0:mid]) + half_turn(even[mid:size]) + odd[mid:size]
    half = mid // 2
    out[0:half, 0:128] = packed[0:half]
    out[0:half, 128:256] = packed[half:mid]
    out[half:half + block.shape[0], :] = block[...]
    at = half + block.shape[0]
    out[at:at + gathered.shape[0], :] = gathered[...]
    at += gathered.shape[0]
    out[at:at + far.shape[0], :] = far[...]


def prolong(group, high, low, basis):
    near = slice(16 * group, 16 * group + 16)
    block = slice(256 * group, 256 * group + 256)
    high = high[near, :]
    w_high, w_low = split(basis[block, :])
    both = dot_t(jnp.concatenate([high, low[near, :]], axis=0), w_high)
    got = both[0:16] + both[16:32] + dot_t(high, w_low)
    upper = rows((8, 128)) < 4
    halves = [jnp.where(upper, got[8 * h:8 * h + 8, 0:128], got[8 * h:8 * h + 8, 128:256]) for h in range(2)]
    return jnp.where(lanes((8, 128)) < 64, halves[0], halves[1])


def coarse_kernel(owned, coarse_rows, zs, rhs_ref, message, message_other, *refs):
    spread, spread_other = refs[:owned - 1], refs[owned - 1:2 * owned - 2]
    (basis, sup_hots, x_ref, coarse_ref, high_out, low_out, first, second,
     w_high, w_low, w_inv, link_rows, hots, product, u_ref, by_row) = refs[2 * owned - 2:]
    size = 4 * coarse_rows
    wide, narrow = lax.axis_index("wide"), lax.axis_index("narrow")
    q = lax.rem(narrow, owned)
    mine = wide * owned + q

    lane16 = lanes((16, 128)) < 64
    lane64 = lanes((64, 128)) < 64
    at_own = coarse_rows
    at_fetched = at_own + packed_rows(owned)
    for z_rel in range(zs):
        for c_rel, (fetched, others) in enumerate(((message, spread), (message_other, spread_other))):
            for j_rel in range(owned):
                i = (z_rel * 2 + c_rel) * owned + j_rel
                at_links = at_own + owned * PIECE + j_rel
                if z_rel > 0:
                    at_links = at_fetched + (zs - 1) * PIECE + (z_rel - 1) * owned + j_rel
                if z_rel == 0:
                    piece, base = fetched, at_own + j_rel * PIECE
                elif j_rel == 0:
                    piece, base = fetched, at_fetched + (z_rel - 1) * PIECE
                else:
                    piece, base = others[j_rel - 1], (z_rel - 1) * PIECE
                high, low = split(piece[base:base + 64, :])
                w_high[64 * i:64 * i + 64, :] = high
                w_low[64 * i:64 * i + 64, :] = low
                quarters = []
                for half in range(2):
                    packed = piece[base + 64:base + 80, 128 * half:128 * half + 128]
                    turned = half_turn(packed)
                    quarters += [jnp.where(lane16, packed, turned), jnp.where(lane16, turned, packed)]
                high, low = split(jnp.concatenate(quarters, axis=0))
                w_inv[64 * i:64 * i + 64, :] = jnp.where(lane64, high.astype(F32), low.astype(F32)).astype(BF16)
                link_rows[4 * i:4 * i + 4, :] = jnp.broadcast_to(fetched[at_links:at_links + 1, 0:128], (4, 128))

    lane = lanes((size, size))
    a_col = jnp.bitwise_and(rows((size, 1)), 3)
    for l in range(4):
        target = jnp.bitwise_xor(link_rows[:, l:l + 1].astype(jnp.int32), mine) * 4 + a_col
        hots[size * l:size * l + size, :] = jnp.where(lane == target, 1.0, 0.0).astype(BF16)

    here = lanes((size, 128)) < 64
    packed = rhs_ref[...]
    turned = half_turn(packed)
    here_mid = here[0:size // 2]
    rhs = jnp.concatenate([jnp.where(here_mid, packed, turned), jnp.where(here_mid, turned, packed)], axis=0)

    def hi_lo(value):
        high, low = split(value)
        return jnp.concatenate([high, low], axis=1)

    u_ref[...] = rhs
    for i in range(coarse_rows):
        link_rows[4 * i:4 * i + 4, :] = u_ref[pl.ds(jnp.bitwise_xor(mine, i) * 4, 4), :]
    rhs = link_rows[...]

    own_block = jnp.bitwise_and(lax.shift_right_logical(rows((size, 256)), 2), 3) == lax.shift_right_logical(
        lanes((size, 256)), 6)

    def fold():
        value = jnp.where(own_block, product[...], 0.0)
        value = value[:, 0:128] + value[:, 128:256]
        return value + half_turn(value)

    def apply_inverse(value):
        high, low = split(value)
        low = jnp.where(here, low.astype(F32), 0.0).astype(BF16)
        for g in range(coarse_rows // 4):
            near = slice(16 * g, 16 * g + 16)
            both = dot_t(jnp.concatenate([high[near], low[near]], axis=0), w_inv[256 * g:256 * g + 256, :])
            product[near, :] = both[0:16] + both[16:32]
        return fold()

    def pick(got, step):
        sel = lanes((step, 128)) < 64
        high = [jnp.where(sel, got[step * k:step * k + step, 0:128], got[step * k + step:step * k + 2 * step, 0:128])
                for k in (0, 2)]
        low = [jnp.where(sel, got[step * k:step * k + step, 128:256],
                         got[step * k + step:step * k + 2 * step, 128:256]) for k in (0, 2)]
        return jnp.concatenate(high, axis=1).astype(BF16), jnp.concatenate(low, axis=1).astype(BF16)

    u = apply_inverse(rhs)
    for step in range(COARSE_SWEEPS):
        high, low = pick(dot(hots[...], hi_lo(u)), size)
        for g in range(coarse_rows // 4):
            near = slice(16 * g, 16 * g + 16)
            block = slice(256 * g, 256 * g + 256)
            both = dot_t(jnp.concatenate([high[near], low[near]], axis=0), w_high[block, :])
            product[near, :] = both[0:16] + both[16:32] + dot_t(high[near], w_low[block, :])
        u = apply_inverse(rhs + fold())

    u_ref[0:4 * owned, :] = u[0:4 * owned]
    here1 = lanes((1, 128)) < 64
    for j in range(owned):
        got = u_ref[pl.ds(jnp.bitwise_xor(q, j) * 4, 4), :]
        coarse_ref[j:j + 1, 0:128] = jnp.where(here1, got[0:1], got[1:2])
        coarse_ref[j:j + 1, 128:256] = jnp.where(here1, got[2:3], got[3:4])

    blocks4 = sup_hots.shape[0] // 4
    high, low = pick(dot(sup_hots[...], hi_lo(u)), blocks4)
    high_out[...] = high
    low_out[...] = low
    line, _ = place()
    even = lax.rem(line, 2) == 0
    adjoints, grid_rows, _ = x_ref.shape
    by_row[0:8, :] = prolong(0, high, low, basis)
    by_row[8:16, :] = prolong(grid_rows // 2 - 1, high, low, basis)
    for a in range(adjoints):
        edge = by_row[pl.ds(a, 4, stride=4), :]
        top = x_ref[a, 0:2, :] + edge[0:2]
        bottom = x_ref[a, grid_rows - 2:grid_rows, :] + edge[2:4]
        first[2 * a:2 * a + 2, :] = jnp.where(even, bottom, top)
        second[2 * a:2 * a + 2, :] = jnp.where(even, top, bottom)


def correct_kernel(r, b, e, n, from_second, from_first, x_ref, high, low, basis,
                   r_out, coef_out, y_out, rx, bx, ex, nx, field, by_row):
    Fine(r, b, e, n, from_first, from_second, rx, bx, ex, nx, field).keep(r_out, coef_out)
    adjoints, grid_rows, width = x_ref.shape
    for g in range(grid_rows // 2):
        by_row[8 * g:8 * g + 8, :] = prolong(g, high, low, basis)
    for a in range(adjoints):
        y_out[a, 0:8, :] = jnp.zeros((8, width), F32)
        y_out[a, 16:24, :] = jnp.zeros((8, width), F32)
        y_out[a, HALO:HALO + grid_rows, :] = x_ref[a] + by_row[pl.ds(a, grid_rows, stride=4), :]


def post_kernel(r, coef, y_ref, y_first, y_inner, y_outer, out, field):
    fine = Kept(r, coef, field)
    in_line = lax.rem(place()[0], 4)
    one, two = y_first[...], jnp.where((in_line == 1) | (in_line == 2), y_inner[...], y_outer[...])
    low = jnp.where(fine.low_ok, jnp.where(fine.even, two, one), 0.0)
    high = jnp.where(fine.high_ok, jnp.where(fine.even, one, two), 0.0)
    grid_rows = out.shape[1]
    start, top = 8 + HALO, 8 + HALO + grid_rows
    field[:, 0:8, :] = jnp.zeros((fine.adjoints, 8, fine.width), F32)
    field[:, 32:40, :] = jnp.zeros((fine.adjoints, 8, fine.width), F32)
    field[:, 8:32, :] = y_ref[...]
    for a in range(fine.adjoints):
        field[a, start - 2:start, :] = low[2 * a:2 * a + 2]
        field[a, top:top + 2, :] = high[2 * a:2 * a + 2]
    x = field[:, 8:32, :]
    for step in range(SWEEPS):
        x = fine.sweep(x)
    field[:, 8:32, :] = x
    for a in range(fine.adjoints):
        out[a] = field[a, start:top, :]


def shape(*dims, kind=F32):
    return jax.ShapeDtypeStruct(dims, kind)


def params(mebibytes):
    return pltpu.CompilerParams(vmem_limit_bytes=mebibytes * 2 ** 20)


def stay(array):
    return pltpu.with_memory_space_constraint(array, pltpu.HBM)


CHEAP = pl.CostEstimate(flops=1, bytes_accessed=1, transcendentals=0)


def body(right_sides, brinkman, east_faces, north_faces, support, basis, links, coarse_block_inverses, coarse_coupling):
    adjoints, grid_rows, width = right_sides.shape
    blocks, block_size, _ = basis.shape
    owned = coarse_block_inverses.shape[0]
    coarse_rows = owned * lax.axis_size("wide")
    zs = lax.axis_size("wide") // 2
    size = 4 * coarse_rows
    basis = basis.reshape(blocks * block_size, -1)

    in_hbm = pl.BlockSpec(memory_space=pltpu.HBM)
    anywhere = pl.BlockSpec(memory_space=pl.ANY)
    in_vmem = pl.BlockSpec(memory_space=pltpu.VMEM)
    row_dims = (grid_rows, width)
    message = shape(24, width)
    fine_inputs = tuple(map(stay, (right_sides, brinkman, east_faces, north_faces)))
    coarse_inputs = tuple(map(stay, (links, coarse_coupling, coarse_block_inverses)))
    to_first, to_second, own = pl.pallas_call(
        functools.partial(begin_kernel, owned),
        out_shape=(message, message, shape(packed_rows(1), 256)),
        in_specs=[in_hbm] * 7,
        scratch_shapes=[
            pltpu.VMEM((adjoints, *row_dims), F32), pltpu.VMEM(row_dims, F32), pltpu.VMEM(row_dims, F32),
            pltpu.VMEM(row_dims, F32), pltpu.SMEM(links.shape, jnp.int32),
            pltpu.VMEM(coarse_block_inverses.shape[1:], F32), pltpu.SemaphoreType.DMA((7,))],
        cost_estimate=CHEAP, compiler_params=params(16), name="begin",
    )(*fine_inputs, *coarse_inputs)
    from_first, from_second = pair_swaps(to_first, to_second)
    fetched = [swap(own, "wide", 2 * k) for k in range(1, zs)]

    rows4 = adjoints * blocks
    block, r, b, e, n, basis, hots, sup_hots = pl.pallas_call(
        functools.partial(prepare_kernel, owned, coarse_rows),
        out_shape=(shape(packed_rows(owned), 256), shape(adjoints, *row_dims), shape(*row_dims), shape(*row_dims),
                   shape(*row_dims), shape(*basis.shape), shape(2 * size, 2 * rows4, kind=BF16),
                   shape(4 * rows4, size, kind=BF16)),
        in_specs=[in_hbm] * 9,
        scratch_shapes=[
            pltpu.VMEM((4, blocks), jnp.int32), pltpu.SMEM(links.shape, jnp.int32),
            pltpu.VMEM(coarse_block_inverses.shape, F32), pltpu.SemaphoreType.DMA((13 + owned + 2,))],
        cost_estimate=CHEAP, compiler_params=params(16), name="prepare",
    )(*fine_inputs, *coarse_inputs, stay(support.T), stay(basis))

    height = (zs - 1) * PIECE
    far_rows = (zs - 1) * owned
    gathered, far = pl.pallas_call(
        stack_kernel, out_shape=(shape(height, 256), shape(far_rows, 256)),
        in_specs=[in_vmem] * (zs - 1) + [anywhere] * 3,
        cost_estimate=CHEAP, compiler_params=params(4), name="stack",
    )(*fetched, from_second, from_first, hots)
    spread = [swap(gathered, "narrow", k) for k in range(1, owned)]

    half = coarse_rows
    message, x = pl.pallas_call(
        functools.partial(restrict_kernel, coarse_rows),
        out_shape=(shape(half + packed_rows(owned) + height + far_rows, 256), shape(adjoints, *row_dims)),
        scratch_shapes=fine_scratch(adjoints, width) + [
            pltpu.VMEM((4 * grid_rows, width), F32), pltpu.VMEM((rows4, 256), F32)],
        cost_estimate=CHEAP, compiler_params=params(16), name="restrict",
    )(r, b, e, n, from_second, from_first, basis, hots, block, gathered, far)

    message_other = swap(message, "wide", 1)
    rhs = pl.pallas_call(
        add_kernel, out_shape=shape(2 * half, 128), cost_estimate=CHEAP, compiler_params=params(4), name="add",
    )(message, message_other)
    for masks in rounds_of(zs):
        rhs = sum_shared(rhs, "wide", [2 * k for k in masks])
    spread = tie(spread, rhs)
    spread_other = [swap(piece, "wide", 1) for piece in spread]
    for masks in rounds_of(lax.axis_size("narrow")):
        rhs = sum([swap(rhs, "narrow", k) for k in masks], rhs)

    near = shape(rows4, 256, kind=BF16)
    coarse, high, low, y_first, y_second = pl.pallas_call(
        functools.partial(coarse_kernel, owned, coarse_rows, zs),
        out_shape=(shape(owned, 256), near, near, shape(8, width), shape(8, width)),
        scratch_shapes=[
            pltpu.VMEM((64 * coarse_rows, 256), BF16), pltpu.VMEM((64 * coarse_rows, 256), BF16),
            pltpu.VMEM((64 * coarse_rows, 128), BF16), pltpu.VMEM((size, 128), F32),
            pltpu.VMEM((4 * size, size), BF16), pltpu.VMEM((size, 256), F32),
            pltpu.VMEM((size, 128), F32), pltpu.VMEM((16, width), F32)],
        cost_estimate=CHEAP, compiler_params=params(min(48, 8 + coarse_rows // 3)), name="coarse",
    )(rhs, message, message_other, *spread, *spread_other, basis, sup_hots, x)

    y_from = pair_swaps_near(y_first, y_second)
    extended = shape(adjoints, FIELD, width)
    r, coef, y = pl.pallas_call(
        correct_kernel,
        out_shape=(extended, shape(6, FIELD, width), extended),
        scratch_shapes=fine_scratch(adjoints, width) + [pltpu.VMEM((4 * grid_rows, width), F32)],
        cost_estimate=CHEAP, compiler_params=params(16), name="correct",
    )(r, b, e, n, from_second, from_first, x, high, low, basis)
    field = pl.pallas_call(
        post_kernel,
        out_shape=shape(adjoints, *row_dims),
        scratch_shapes=[pltpu.VMEM((adjoints, 40, width), F32)],
        cost_estimate=CHEAP, compiler_params=params(16), name="post",
    )(r, coef, y, *y_from)
    return field, coarse


def solution(mesh):
    return jax.shard_map(
        body,
        mesh=mesh,
        in_specs=(
            P(None, ("wide", "narrow"), None),
            P(("wide", "narrow"), None),
            P(("wide", "narrow"), None),
            P(("wide", "narrow"), None),
            P(("wide", "narrow"), None),
            P(("wide", "narrow"), None, None),
            P("wide", None),
            P("wide", None, None),
            P("wide", None, None),
        ),
        out_specs=(P(None, ("wide", "narrow"), None), P("wide", None)),
        check_vma=False,
    )
```

```python
import functools

import jax
import jax.numpy as jnp
from jax import lax
from jax.experimental import pallas as pl
from jax.experimental.pallas import tpu as pltpu
from jax.sharding import PartitionSpec as P

SWEEPS = 2
COARSE_SWEEPS = 3
relax_weight = 0.7

BOTH = ("wide", "narrow")
HALO = 3
FIELD = 24
PIECE = 80
F32 = jnp.float32
BF16 = jnp.bfloat16


def swap(value, axis, bits):
    size = lax.axis_size(axis)
    return lax.ppermute(value, axis, [(i, i ^ bits) for i in range(size)])


def pair_swaps(to_first, to_second):
    count = lax.axis_size(BOTH)
    first = lax.ppermute(to_first, BOTH, [(i, i ^ 1) for i in range(count)])
    odd = [(i, i + 1) for i in range(1, count - 1, 2)] + [(count - 1, 0)]
    second = lax.ppermute(to_second, BOTH, odd + [(target, source) for source, target in odd])
    return first, second


def pair_swaps_near(to_first, to_second):
    count, across = lax.axis_size(BOTH), lax.axis_size("narrow")
    first = lax.ppermute(to_first, BOTH, [(i, i ^ 1) for i in range(count)])
    inner = lax.ppermute(to_second, BOTH, [(i, i ^ (3 if i % 4 in (1, 2) else across)) for i in range(count)])
    outer = [(i, i + 1) for i in range(3, count - 1, 4)]
    outer += [(i, i ^ across) for i in range(2, count, 4) if i < i ^ across]
    rest = [0] + list(range(1, count, 4)) + [count - 1]
    outer += list(zip(rest[::2], rest[1::2]))
    outer = lax.ppermute(to_second, BOTH, outer + [(target, source) for source, target in outer])
    return first, inner, outer


def tie(values, after):
    count = len(values)
    spec = pl.BlockSpec(memory_space=pl.ANY)
    return list(pl.pallas_call(
        lambda *refs: None, out_shape=[jax.ShapeDtypeStruct(v.shape, v.dtype) for v in values],
        in_specs=[spec] * (count + 1), out_specs=[spec] * count,
        input_output_aliases={i: i for i in range(count)}, cost_estimate=CHEAP, compiler_params=params(1), name="tie",
    )(*values, after))


def rounds_of(size):
    rounds, base = [], 1
    while base < size:
        span = 4 if base * 4 <= size else 2
        rounds.append([base * k for k in range(1, span)])
        base *= span
    return rounds


def share_kernel(value, one, two, out):
    second = lax.rem(lax.axis_index("wide"), 2) == 1
    out[...] = one[...] + jnp.where(second, two[...], value[...])


def sum_shared(value, axis, masks):
    if len(masks) == 1:
        return value + swap(value, axis, masks[0])
    count, across = lax.axis_size(BOTH), lax.axis_size("narrow")
    unit = across if axis == "wide" else 1
    near, far, farthest = [unit * mask for mask in masks]
    one = lax.ppermute(value, BOTH, [(i, i ^ (far if i & across else near)) for i in range(count)])
    two = lax.ppermute(value, BOTH, [(i, i ^ (farthest if i & across else near)) for i in range(count)])
    value = pl.pallas_call(
        share_kernel, out_shape=jax.ShapeDtypeStruct(value.shape, value.dtype),
        cost_estimate=CHEAP, compiler_params=params(1), name="share",
    )(value, one, two)
    return value + swap(value, "wide", 1)


def bits_of(size):
    return [1 << i for i in range(size.bit_length() - 1)]


def place():
    wide, narrow = lax.axis_index("wide"), lax.axis_index("narrow")
    line = wide * lax.axis_size("narrow") + narrow
    count = lax.axis_size("wide") * lax.axis_size("narrow")
    return line, count


def packed_rows(count):
    return count * PIECE + 8 * ((count + 7) // 8)


def lanes(shape):
    return lax.broadcasted_iota(jnp.int32, shape, len(shape) - 1)


def rows(shape):
    return lax.broadcasted_iota(jnp.int32, shape, len(shape) - 2)


def split(value):
    high = value.astype(BF16)
    return high, (value - high.astype(F32)).astype(BF16)


def dot(left, right):
    return lax.dot_general(left, right, (((1,), (0,)), ((), ())), preferred_element_type=F32)


def dot_t(left, right):
    return lax.dot_general(left, right, (((1,), (1,)), ((), ())), preferred_element_type=F32)


def half_turn(value):
    return pltpu.roll(value, 64, 1)


def copy_all(pairs, sems):
    copies = [pltpu.make_async_copy(source, target, sems.at[i]) for i, (source, target) in enumerate(pairs)]
    for copy in copies:
        copy.start()

    def wait():
        for copy in copies:
            copy.wait()

    return wait


def packed_inverse(inverse):
    inverse = inverse.T
    return jnp.concatenate([inverse[16 * t:16 * t + 16, :] for t in range(4)], axis=1)


def link_rows_of(owned, links, q):
    lane, row = lanes((8, 256)), rows((8, 256))
    tail = jnp.zeros((8, 256), F32)
    for j_rel in range(owned):
        for l in range(links.shape[1]):
            link = links[jnp.bitwise_xor(q, j_rel), l].astype(F32)
            tail = jnp.where((row == j_rel) & (lane == l), link, tail)
    return tail


def begin_kernel(owned, r_in, b_in, e_in, n_in, links_in, coupling_in, inverses_in, first, second, own,
                 r, b, e, n, links, inverse, sems):
    q = lax.rem(lax.axis_index("narrow"), owned)
    wait = copy_all([(r_in, r), (b_in, b), (e_in, e), (n_in, n), (links_in, links),
                     (coupling_in.at[q], own.at[pl.ds(0, 64)]), (inverses_in.at[q], inverse)], sems)
    grid_rows = b.shape[0]
    line, _ = place()
    even = lax.rem(line, 2) == 0
    wait()

    def message(start, north_start):
        parts = [r[a, start:start + HALO, :] for a in range(r.shape[0])]
        parts += [b[start:start + HALO, :], e[start:start + HALO, :]]
        parts += [n[north_start:north_start + HALO + 1, :], jnp.zeros((2, b.shape[1]), F32)]
        return parts

    top = message(0, 0)
    bottom = message(grid_rows - HALO, grid_rows - HALO - 1)
    at = 0
    for low, high in zip(top, bottom):
        size = low.shape[0]
        first[at:at + size, :] = jnp.where(even, high, low)
        second[at:at + size, :] = jnp.where(even, low, high)
        at += size

    own[64:PIECE, :] = packed_inverse(inverse[...])
    own[PIECE:PIECE + 8, :] = link_rows_of(owned, links, q)


def prepare_kernel(owned, coarse_rows, r_in, b_in, e_in, n_in, links_in, coupling_in, inverses_in, support_in, basis_in,
                   block, r_out, b_out, e_out, n_out, basis, hots, sup_hots, support, links, inverses, sems):
    q = lax.rem(lax.axis_index("narrow"), owned)
    mine = lax.axis_index("wide") * owned + q
    wait_support = copy_all([(support_in, support)], sems.at[pl.ds(0, 1)])
    wait_rows = copy_all([(coupling_in.at[jnp.bitwise_xor(q, j)], block.at[pl.ds(j * PIECE, 64)]) for j in range(owned)]
                         + [(links_in, links), (inverses_in, inverses)], sems.at[pl.ds(13, owned + 2)])
    part = basis.shape[0] // 8
    parts = [pl.ds(part * i, part) for i in range(8)]
    wait = copy_all([(basis_in.at[at], basis.at[at]) for at in parts]
                    + [(r_in, r_out), (b_in, b_out), (e_in, e_out), (n_in, n_out)], sems.at[pl.ds(1, 12)])
    wait_rows()
    for j in range(owned):
        block[j * PIECE + 64:j * PIECE + PIECE, :] = packed_inverse(inverses[jnp.bitwise_xor(q, j)])
    block[owned * PIECE:owned * PIECE + 8, :] = link_rows_of(owned, links, q)
    wait_support()

    blocks = support.shape[1]
    rows4 = 4 * blocks
    size = 4 * coarse_rows

    def chosen(which, index):
        g, h = lax.shift_right_logical(index, 4), jnp.bitwise_and(lax.shift_right_logical(index, 3), 1)
        p = jnp.bitwise_and(lax.shift_right_logical(index, 2), 1)
        return jnp.where(which == g * 4 + p * 2 + h, 1.0, 0.0).astype(BF16)

    value = support[...].astype(F32).astype(BF16)
    column = dot_t(chosen(lanes((rows4, blocks)), rows((rows4, blocks))), value)
    line = dot(value, chosen(rows((blocks, rows4)), lanes((blocks, rows4))))
    line = line.astype(jnp.int32) * 4 + jnp.bitwise_and(lanes((4, rows4)), 3)
    at = rows((size, rows4))
    for k in range(4):
        base, left = (k % 2) * size, (k // 2) * rows4
        hots[base:base + size, left:left + rows4] = jnp.where(at == line[k:k + 1, :], 1.0, 0.0).astype(BF16)
    column = jnp.bitwise_xor(column.astype(jnp.int32), mine) * 4 + jnp.bitwise_and(rows((rows4, 4)), 3)
    across = lanes((rows4, size))
    for k in range(4):
        sup_hots[rows4 * k:rows4 * k + rows4, :] = jnp.where(across == column[:, k:k + 1], 1.0, 0.0).astype(BF16)

    wait()


def stack_kernel(*refs):
    fetched, gathered, far = refs[:-5], refs[-2], refs[-1]
    owned = far.shape[0] // len(fetched)
    for i, piece in enumerate(fetched):
        gathered[PIECE * i:PIECE * i + PIECE, :] = piece[0:PIECE, :]
        far[owned * i:owned * i + owned, :] = piece[PIECE:PIECE + owned, :]


def add_kernel(one, two, out):
    half = out.shape[0] // 2
    for i in range(2):
        block = slice(128 * i, 128 * i + 128)
        out[half * i:half * i + half, :] = one[0:half, block] + two[0:half, block]


class Fine:
    def __init__(self, r, b, e, n, from_first, from_second, rx, bx, ex, nx, field):
        line, count = place()
        even = lax.rem(line, 2) == 0
        low_ok, high_ok = line > 0, line < count - 1
        one, two = from_first[...], from_second[...]
        low = jnp.where(low_ok, jnp.where(even, two, one), 0.0)
        high = jnp.where(high_ok, jnp.where(even, one, two), 0.0)
        self.even, self.low_ok, self.high_ok = even, low_ok, high_ok
        self.adjoints, self.grid_rows, width = r.shape
        top = HALO + self.grid_rows
        zeros = jnp.zeros((8, width), F32)
        for a in range(self.adjoints):
            rx[a, 16:24, :] = zeros
            rx[a, 0:HALO, :] = low[3 * a:3 * a + 3]
            rx[a, HALO:top, :] = r[a]
            rx[a, top:top + HALO, :] = high[3 * a:3 * a + 3]
            field[a, 0:8, :] = zeros
            field[a, 32:40, :] = zeros
        bx[16:24, :] = zeros
        bx[0:HALO, :] = low[12:15]
        bx[HALO:top, :] = b[...]
        bx[top:top + HALO, :] = high[12:15]
        ex[16:24, :] = zeros
        ex[0:HALO, :] = low[15:18]
        ex[HALO:top, :] = e[...]
        ex[top:top + HALO, :] = high[15:18]
        nx[16:24, :] = zeros
        nx[24:32, :] = zeros
        nx[0:HALO + 1, :] = low[18:22]
        nx[HALO + 1:top + 1, :] = n[...]
        nx[top + 1:top + 1 + HALO, :] = high[18:21]
        self.r = rx[...]
        self.east = ex[...]
        self.north = nx[1:1 + FIELD, :]
        self.south = nx[0:FIELD, :]
        self.west = pltpu.roll(self.east, 1, 1)
        self.diagonal = bx[...] + self.east + self.west + self.north + self.south
        t = rows((FIELD, width))
        valid = ((t >= HALO) | low_ok) & ((t < top) | high_ok) & (t < top + HALO)
        self.scale = jnp.where(valid, relax_weight / jnp.where(valid, self.diagonal, 1.0), 0.0)
        self.field = field
        self.width = width

    def apply(self, x):
        self.field[:, 8:32, :] = x
        above = self.field[:, 7:31, :]
        below = self.field[:, 9:33, :]
        east = pltpu.roll(x, self.width - 1, 2)
        west = pltpu.roll(x, 1, 2)
        return self.diagonal * x - self.north * below - self.south * above - self.east * east - self.west * west

    def sweep(self, x):
        return x + self.scale * (self.r - self.apply(x))


    def keep(self, r_out, coef_out):
        r_out[...] = self.r
        for i, value in enumerate((self.diagonal, self.scale, self.north, self.south, self.east, self.west)):
            coef_out[i] = value


class Kept(Fine):
    def __init__(self, r, coef, field):
        line, count = place()
        self.even, self.low_ok, self.high_ok = lax.rem(line, 2) == 0, line > 0, line < count - 1
        self.r, self.field = r[...], field
        self.diagonal, self.scale, self.north, self.south, self.east, self.west = [coef[i] for i in range(6)]
        self.adjoints, _, self.width = r.shape


def fine_scratch(adjoints, width):
    return [
        pltpu.VMEM((adjoints, FIELD, width), F32),
        pltpu.VMEM((FIELD, width), F32),
        pltpu.VMEM((FIELD, width), F32),
        pltpu.VMEM((32, width), F32),
        pltpu.VMEM((adjoints, 40, width), F32),
    ]


def restrict_kernel(coarse_rows, r, b, e, n, from_second, from_first, basis, hots,
                    block, gathered, far, out, x_out, rx, bx, ex, nx, field, by_row, contrib):
    fine = Fine(r, b, e, n, from_first, from_second, rx, bx, ex, nx, field)
    x = fine.scale * fine.r
    for step in range(SWEEPS - 1):
        x = fine.sweep(x)
    resid = fine.r - fine.apply(x)
    for a in range(fine.adjoints):
        x_out[a] = field[a, 8 + HALO:8 + HALO + fine.grid_rows, :]
    field[:, 8:32, :] = resid
    for a in range(fine.adjoints):
        by_row[pl.ds(a, fine.grid_rows, stride=4), :] = field[a, 8 + HALO:8 + HALO + fine.grid_rows, :]
    left = lanes((8, 128)) < 64
    upper = rows((8, 128)) < 4
    for g in range(fine.grid_rows // 2):
        z = by_row[8 * g:8 * g + 8, :]
        parts = []
        for here in (left, ~left):
            held = jnp.where(here, z, 0.0)
            parts.append(jnp.concatenate([jnp.where(upper, held, 0.0), jnp.where(upper, 0.0, held)], axis=1))
        high, low = split(jnp.concatenate(parts, axis=0))
        near = slice(256 * g, 256 * g + 256)
        w_high, w_low = split(basis[near, :])
        both = dot(jnp.concatenate([high, low], axis=0), w_high)
        contrib[16 * g:16 * g + 16, :] = both[0:16] + both[16:32] + dot(high, w_low)
    c_high, c_low = split(contrib[...])
    weights = jnp.concatenate([
        jnp.concatenate([c_high[:, 0:128], c_low[:, 0:128]], axis=1),
        jnp.concatenate([c_high[:, 128:256], c_low[:, 128:256]], axis=1)], axis=0)
    size = 4 * coarse_rows
    total = dot(hots[...], weights)
    total = total[:, 0:128] + total[:, 128:256]
    here = lanes((size, 128)) < 64
    even = jnp.where(here, total[0:size], 0.0)
    odd = jnp.where(here, 0.0, total[size:2 * size])
    mid = size // 2
    packed = even[0:mid] + half_turn(odd[0:mid]) + half_turn(even[mid:size]) + odd[mid:size]
    half = mid // 2
    out[0:half, 0:128] = packed[0:half]
    out[0:half, 128:256] = packed[half:mid]
    out[half:half + block.shape[0], :] = block[...]
    at = half + block.shape[0]
    out[at:at + gathered.shape[0], :] = gathered[...]
    at += gathered.shape[0]
    out[at:at + far.shape[0], :] = far[...]


def prolong(group, high, low, basis):
    near = slice(16 * group, 16 * group + 16)
    block = slice(256 * group, 256 * group + 256)
    high = high[near, :]
    w_high, w_low = split(basis[block, :])
    both = dot_t(jnp.concatenate([high, low[near, :]], axis=0), w_high)
    got = both[0:16] + both[16:32] + dot_t(high, w_low)
    upper = rows((8, 128)) < 4
    halves = [jnp.where(upper, got[8 * h:8 * h + 8, 0:128], got[8 * h:8 * h + 8, 128:256]) for h in range(2)]
    return jnp.where(lanes((8, 128)) < 64, halves[0], halves[1])


def coarse_kernel(owned, coarse_rows, zs, rhs_ref, message, message_other, *refs):
    spread, spread_other = refs[:owned - 1], refs[owned - 1:2 * owned - 2]
    (basis, sup_hots, x_ref, coarse_ref, high_out, low_out, first, second,
     w_high, w_low, w_inv, link_rows, hots, product, u_ref, by_row) = refs[2 * owned - 2:]
    size = 4 * coarse_rows
    wide, narrow = lax.axis_index("wide"), lax.axis_index("narrow")
    q = lax.rem(narrow, owned)
    mine = wide * owned + q

    lane16 = lanes((16, 128)) < 64
    lane64 = lanes((64, 128)) < 64
    at_own = coarse_rows
    at_fetched = at_own + packed_rows(owned)
    for z_rel in range(zs):
        for c_rel, (fetched, others) in enumerate(((message, spread), (message_other, spread_other))):
            for j_rel in range(owned):
                i = (z_rel * 2 + c_rel) * owned + j_rel
                at_links = at_own + owned * PIECE + j_rel
                if z_rel > 0:
                    at_links = at_fetched + (zs - 1) * PIECE + (z_rel - 1) * owned + j_rel
                if z_rel == 0:
                    piece, base = fetched, at_own + j_rel * PIECE
                elif j_rel == 0:
                    piece, base = fetched, at_fetched + (z_rel - 1) * PIECE
                else:
                    piece, base = others[j_rel - 1], (z_rel - 1) * PIECE
                high, low = split(piece[base:base + 64, :])
                w_high[64 * i:64 * i + 64, :] = high
                w_low[64 * i:64 * i + 64, :] = low
                quarters = []
                for half in range(2):
                    packed = piece[base + 64:base + 80, 128 * half:128 * half + 128]
                    turned = half_turn(packed)
                    quarters += [jnp.where(lane16, packed, turned), jnp.where(lane16, turned, packed)]
                columns = jnp.concatenate(quarters, axis=0)
                if j_rel % 2:
                    high, low = split(jnp.where(lane64, before, columns))
                    at, to = i // 4 * 128, j_rel % 4 // 2 * 128
                    w_inv[at:at + 64, to:to + 128] = high
                    w_inv[at + 64:at + 128, to:to + 128] = low
                before = columns
                link_rows[4 * i:4 * i + 4, :] = jnp.broadcast_to(fetched[at_links:at_links + 1, 0:128], (4, 128))

    lane = lanes((size, size))
    a_col = jnp.bitwise_and(rows((size, 1)), 3)
    for l in range(4):
        target = jnp.bitwise_xor(link_rows[:, l:l + 1].astype(jnp.int32), mine) * 4 + a_col
        hots[size * l:size * l + size, :] = jnp.where(lane == target, 1.0, 0.0).astype(BF16)

    here = lanes((size, 128)) < 64
    packed = rhs_ref[...]
    turned = half_turn(packed)
    here_mid = here[0:size // 2]
    rhs = jnp.concatenate([jnp.where(here_mid, packed, turned), jnp.where(here_mid, turned, packed)], axis=0)

    def hi_lo(value):
        high, low = split(value)
        return jnp.concatenate([high, low], axis=1)

    u_ref[...] = rhs
    for i in range(coarse_rows):
        link_rows[4 * i:4 * i + 4, :] = u_ref[pl.ds(jnp.bitwise_xor(mine, i) * 4, 4), :]
    rhs = link_rows[...]

    own_block = jnp.bitwise_and(lax.shift_right_logical(rows((size, 256)), 2), 3) == lax.shift_right_logical(
        lanes((size, 256)), 6)

    def fold():
        value = jnp.where(own_block, product[...], 0.0)
        value = value[:, 0:128] + value[:, 128:256]
        return value + half_turn(value)

    def apply_inverse(value):
        high, low = split(value)
        low = jnp.where(here, low.astype(F32), 0.0).astype(BF16)
        for g in range(coarse_rows // 4):
            near = slice(16 * g, 16 * g + 16)
            both = dot(jnp.concatenate([high[near], low[near]], axis=0), w_inv[128 * g:128 * g + 128, :])
            product[near, :] = both[0:16] + both[16:32]
        return fold()

    def pick(got, step):
        sel = lanes((step, 128)) < 64
        high = [jnp.where(sel, got[step * k:step * k + step, 0:128], got[step * k + step:step * k + 2 * step, 0:128])
                for k in (0, 2)]
        low = [jnp.where(sel, got[step * k:step * k + step, 128:256],
                         got[step * k + step:step * k + 2 * step, 128:256]) for k in (0, 2)]
        return jnp.concatenate(high, axis=1).astype(BF16), jnp.concatenate(low, axis=1).astype(BF16)

    u = apply_inverse(rhs)
    for step in range(COARSE_SWEEPS):
        high, low = pick(dot(hots[...], hi_lo(u)), size)
        for g in range(coarse_rows // 4):
            near = slice(16 * g, 16 * g + 16)
            block = slice(256 * g, 256 * g + 256)
            both = dot_t(jnp.concatenate([high[near], low[near]], axis=0), w_high[block, :])
            product[near, :] = both[0:16] + both[16:32] + dot_t(high[near], w_low[block, :])
        u = apply_inverse(rhs + fold())

    u_ref[0:4 * owned, :] = u[0:4 * owned]
    here1 = lanes((1, 128)) < 64
    for j in range(owned):
        got = u_ref[pl.ds(jnp.bitwise_xor(q, j) * 4, 4), :]
        coarse_ref[j:j + 1, 0:128] = jnp.where(here1, got[0:1], got[1:2])
        coarse_ref[j:j + 1, 128:256] = jnp.where(here1, got[2:3], got[3:4])

    blocks4 = sup_hots.shape[0] // 4
    high, low = pick(dot(sup_hots[...], hi_lo(u)), blocks4)
    high_out[...] = high
    low_out[...] = low
    line, _ = place()
    even = lax.rem(line, 2) == 0
    adjoints, grid_rows, _ = x_ref.shape
    by_row[0:8, :] = prolong(0, high, low, basis)
    by_row[8:16, :] = prolong(grid_rows // 2 - 1, high, low, basis)
    for a in range(adjoints):
        edge = by_row[pl.ds(a, 4, stride=4), :]
        top = x_ref[a, 0:2, :] + edge[0:2]
        bottom = x_ref[a, grid_rows - 2:grid_rows, :] + edge[2:4]
        first[2 * a:2 * a + 2, :] = jnp.where(even, bottom, top)
        second[2 * a:2 * a + 2, :] = jnp.where(even, top, bottom)


def correct_kernel(r, b, e, n, from_second, from_first, x_ref, high, low, basis,
                   r_out, coef_out, y_out, rx, bx, ex, nx, field, by_row):
    Fine(r, b, e, n, from_first, from_second, rx, bx, ex, nx, field).keep(r_out, coef_out)
    adjoints, grid_rows, width = x_ref.shape
    for g in range(grid_rows // 2):
        by_row[8 * g:8 * g + 8, :] = prolong(g, high, low, basis)
    for a in range(adjoints):
        y_out[a, 0:8, :] = jnp.zeros((8, width), F32)
        y_out[a, 16:24, :] = jnp.zeros((8, width), F32)
        y_out[a, HALO:HALO + grid_rows, :] = x_ref[a] + by_row[pl.ds(a, grid_rows, stride=4), :]


def post_kernel(r, coef, y_ref, y_first, y_inner, y_outer, out, field):
    fine = Kept(r, coef, field)
    in_line = lax.rem(place()[0], 4)
    one, two = y_first[...], jnp.where((in_line == 1) | (in_line == 2), y_inner[...], y_outer[...])
    low = jnp.where(fine.low_ok, jnp.where(fine.even, two, one), 0.0)
    high = jnp.where(fine.high_ok, jnp.where(fine.even, one, two), 0.0)
    grid_rows = out.shape[1]
    start, top = 8 + HALO, 8 + HALO + grid_rows
    field[:, 0:8, :] = jnp.zeros((fine.adjoints, 8, fine.width), F32)
    field[:, 32:40, :] = jnp.zeros((fine.adjoints, 8, fine.width), F32)
    field[:, 8:32, :] = y_ref[...]
    for a in range(fine.adjoints):
        field[a, start - 2:start, :] = low[2 * a:2 * a + 2]
        field[a, top:top + 2, :] = high[2 * a:2 * a + 2]
    x = field[:, 8:32, :]
    for step in range(SWEEPS):
        x = fine.sweep(x)
    field[:, 8:32, :] = x
    for a in range(fine.adjoints):
        out[a] = field[a, start:top, :]


def shape(*dims, kind=F32):
    return jax.ShapeDtypeStruct(dims, kind)


def params(mebibytes):
    return pltpu.CompilerParams(vmem_limit_bytes=mebibytes * 2 ** 20)


def stay(array):
    return pltpu.with_memory_space_constraint(array, pltpu.HBM)


CHEAP = pl.CostEstimate(flops=1, bytes_accessed=1, transcendentals=0)


def body(right_sides, brinkman, east_faces, north_faces, support, basis, links, coarse_block_inverses, coarse_coupling):
    adjoints, grid_rows, width = right_sides.shape
    blocks, block_size, _ = basis.shape
    owned = coarse_block_inverses.shape[0]
    coarse_rows = owned * lax.axis_size("wide")
    zs = lax.axis_size("wide") // 2
    size = 4 * coarse_rows
    basis = basis.reshape(blocks * block_size, -1)

    in_hbm = pl.BlockSpec(memory_space=pltpu.HBM)
    anywhere = pl.BlockSpec(memory_space=pl.ANY)
    in_vmem = pl.BlockSpec(memory_space=pltpu.VMEM)
    row_dims = (grid_rows, width)
    message = shape(24, width)
    fine_inputs = tuple(map(stay, (right_sides, brinkman, east_faces, north_faces)))
    coarse_inputs = tuple(map(stay, (links, coarse_coupling, coarse_block_inverses)))
    to_first, to_second, own = pl.pallas_call(
        functools.partial(begin_kernel, owned),
        out_shape=(message, message, shape(packed_rows(1), 256)),
        in_specs=[in_hbm] * 7,
        scratch_shapes=[
            pltpu.VMEM((adjoints, *row_dims), F32), pltpu.VMEM(row_dims, F32), pltpu.VMEM(row_dims, F32),
            pltpu.VMEM(row_dims, F32), pltpu.SMEM(links.shape, jnp.int32),
            pltpu.VMEM(coarse_block_inverses.shape[1:], F32), pltpu.SemaphoreType.DMA((7,))],
        cost_estimate=CHEAP, compiler_params=params(16), name="begin",
    )(*fine_inputs, *coarse_inputs)
    from_first, from_second = pair_swaps(to_first, to_second)
    fetched = [swap(own, "wide", 2 * k) for k in range(1, zs)]

    rows4 = adjoints * blocks
    block, r, b, e, n, basis, hots, sup_hots = pl.pallas_call(
        functools.partial(prepare_kernel, owned, coarse_rows),
        out_shape=(shape(packed_rows(owned), 256), shape(adjoints, *row_dims), shape(*row_dims), shape(*row_dims),
                   shape(*row_dims), shape(*basis.shape), shape(2 * size, 2 * rows4, kind=BF16),
                   shape(4 * rows4, size, kind=BF16)),
        in_specs=[in_hbm] * 9,
        scratch_shapes=[
            pltpu.VMEM((4, blocks), jnp.int32), pltpu.SMEM(links.shape, jnp.int32),
            pltpu.VMEM(coarse_block_inverses.shape, F32), pltpu.SemaphoreType.DMA((13 + owned + 2,))],
        cost_estimate=CHEAP, compiler_params=params(16), name="prepare",
    )(*fine_inputs, *coarse_inputs, stay(support.T), stay(basis))

    height = (zs - 1) * PIECE
    far_rows = (zs - 1) * owned
    gathered, far = pl.pallas_call(
        stack_kernel, out_shape=(shape(height, 256), shape(far_rows, 256)),
        in_specs=[in_vmem] * (zs - 1) + [anywhere] * 3,
        cost_estimate=CHEAP, compiler_params=params(4), name="stack",
    )(*fetched, from_second, from_first, hots)
    spread = [swap(gathered, "narrow", k) for k in range(1, owned)]

    half = coarse_rows
    message, x = pl.pallas_call(
        functools.partial(restrict_kernel, coarse_rows),
        out_shape=(shape(half + packed_rows(owned) + height + far_rows, 256), shape(adjoints, *row_dims)),
        scratch_shapes=fine_scratch(adjoints, width) + [
            pltpu.VMEM((4 * grid_rows, width), F32), pltpu.VMEM((rows4, 256), F32)],
        cost_estimate=CHEAP, compiler_params=params(16), name="restrict",
    )(r, b, e, n, from_second, from_first, basis, hots, block, gathered, far)

    message_other = swap(message, "wide", 1)
    rhs = pl.pallas_call(
        add_kernel, out_shape=shape(2 * half, 128), cost_estimate=CHEAP, compiler_params=params(4), name="add",
    )(message, message_other)
    for masks in rounds_of(zs):
        rhs = sum_shared(rhs, "wide", [2 * k for k in masks])
    spread = tie(spread, rhs)
    spread_other = [swap(piece, "wide", 1) for piece in spread]
    for masks in rounds_of(lax.axis_size("narrow")):
        rhs = sum([swap(rhs, "narrow", k) for k in masks[::-1]], rhs)

    near = shape(rows4, 256, kind=BF16)
    coarse, high, low, y_first, y_second = pl.pallas_call(
        functools.partial(coarse_kernel, owned, coarse_rows, zs),
        out_shape=(shape(owned, 256), near, near, shape(8, width), shape(8, width)),
        scratch_shapes=[
            pltpu.VMEM((64 * coarse_rows, 256), BF16), pltpu.VMEM((64 * coarse_rows, 256), BF16),
            pltpu.VMEM((32 * coarse_rows, 256), BF16), pltpu.VMEM((size, 128), F32),
            pltpu.VMEM((4 * size, size), BF16), pltpu.VMEM((size, 256), F32),
            pltpu.VMEM((size, 128), F32), pltpu.VMEM((16, width), F32)],
        cost_estimate=CHEAP, compiler_params=params(min(48, 8 + coarse_rows // 3)), name="coarse",
    )(rhs, message, message_other, *spread, *spread_other, basis, sup_hots, x)

    y_from = pair_swaps_near(y_first, y_second)
    extended = shape(adjoints, FIELD, width)
    r, coef, y = pl.pallas_call(
        correct_kernel,
        out_shape=(extended, shape(6, FIELD, width), extended),
        scratch_shapes=fine_scratch(adjoints, width) + [pltpu.VMEM((4 * grid_rows, width), F32)],
        cost_estimate=CHEAP, compiler_params=params(16), name="correct",
    )(r, b, e, n, from_second, from_first, x, high, low, basis)
    field = pl.pallas_call(
        post_kernel,
        out_shape=shape(adjoints, *row_dims),
        scratch_shapes=[pltpu.VMEM((adjoints, 40, width), F32)],
        cost_estimate=CHEAP, compiler_params=params(16), name="post",
    )(r, coef, y, *y_from)
    return field, coarse


def solution(mesh):
    return jax.shard_map(
        body,
        mesh=mesh,
        in_specs=(
            P(None, ("wide", "narrow"), None),
            P(("wide", "narrow"), None),
            P(("wide", "narrow"), None),
            P(("wide", "narrow"), None),
            P(("wide", "narrow"), None),
            P(("wide", "narrow"), None, None),
            P("wide", None),
            P("wide", None, None),
            P("wide", None, None),
        ),
        out_specs=(P(None, ("wide", "narrow"), None), P("wide", None)),
        check_vma=False,
    )
```

```python
import functools

import jax
import jax.numpy as jnp
from jax import lax
from jax.experimental import pallas as pl
from jax.experimental.pallas import tpu as pltpu
from jax.sharding import PartitionSpec as P

SWEEPS = 2
COARSE_SWEEPS = 3
relax_weight = 0.7

BOTH = ("wide", "narrow")
HALO = 3
FIELD = 24
PIECE = 80
F32 = jnp.float32
BF16 = jnp.bfloat16


def swap(value, axis, bits):
    size = lax.axis_size(axis)
    return lax.ppermute(value, axis, [(i, i ^ bits) for i in range(size)])


def pair_swaps(to_first, to_second):
    count = lax.axis_size(BOTH)
    first = lax.ppermute(to_first, BOTH, [(i, i ^ 1) for i in range(count)])
    odd = [(i, i + 1) for i in range(1, count - 1, 2)] + [(count - 1, 0)]
    second = lax.ppermute(to_second, BOTH, odd + [(target, source) for source, target in odd])
    return first, second


def pair_swaps_near(to_first, to_second):
    count, across = lax.axis_size(BOTH), lax.axis_size("narrow")
    first = lax.ppermute(to_first, BOTH, [(i, i ^ 1) for i in range(count)])
    inner = lax.ppermute(to_second, BOTH, [(i, i ^ (3 if i % 4 in (1, 2) else across)) for i in range(count)])
    outer = [(i, i + 1) for i in range(3, count - 1, 4)]
    outer += [(i, i ^ across) for i in range(2, count, 4) if i < i ^ across]
    rest = [0] + list(range(1, count, 4)) + [count - 1]
    outer += list(zip(rest[::2], rest[1::2]))
    outer = lax.ppermute(to_second, BOTH, outer + [(target, source) for source, target in outer])
    return first, inner, outer


def tie(values, after):
    count = len(values)
    spec = pl.BlockSpec(memory_space=pl.ANY)
    return list(pl.pallas_call(
        lambda *refs: None, out_shape=[jax.ShapeDtypeStruct(v.shape, v.dtype) for v in values],
        in_specs=[spec] * (count + 1), out_specs=[spec] * count,
        input_output_aliases={i: i for i in range(count)}, cost_estimate=CHEAP, compiler_params=params(1), name="tie",
    )(*values, after))


def rounds_of(size):
    rounds, base = [], 1
    while base < size:
        span = 4 if base * 4 <= size else 2
        rounds.append([base * k for k in range(1, span)])
        base *= span
    return rounds


def share_kernel(value, one, two, out):
    second = lax.rem(lax.axis_index("wide"), 2) == 1
    out[...] = one[...] + jnp.where(second, two[...], value[...])


def sum_shared(value, axis, masks):
    if len(masks) == 1:
        return value + swap(value, axis, masks[0])
    count, across = lax.axis_size(BOTH), lax.axis_size("narrow")
    unit = across if axis == "wide" else 1
    near, farthest, far = [unit * mask for mask in masks]
    one = lax.ppermute(value, BOTH, [(i, i ^ (far if i & across else near)) for i in range(count)])
    two = lax.ppermute(value, BOTH, [(i, i ^ (farthest if i & across else near)) for i in range(count)])
    value = pl.pallas_call(
        share_kernel, out_shape=jax.ShapeDtypeStruct(value.shape, value.dtype),
        cost_estimate=CHEAP, compiler_params=params(1), name="share",
    )(value, one, two)
    return value + swap(value, "wide", 1)


def bits_of(size):
    return [1 << i for i in range(size.bit_length() - 1)]


def place():
    wide, narrow = lax.axis_index("wide"), lax.axis_index("narrow")
    line = wide * lax.axis_size("narrow") + narrow
    count = lax.axis_size("wide") * lax.axis_size("narrow")
    return line, count


def packed_rows(count):
    return count * PIECE + 8 * ((count + 7) // 8)


def lanes(shape):
    return lax.broadcasted_iota(jnp.int32, shape, len(shape) - 1)


def rows(shape):
    return lax.broadcasted_iota(jnp.int32, shape, len(shape) - 2)


def split(value):
    high = value.astype(BF16)
    return high, (value - high.astype(F32)).astype(BF16)


def dot(left, right):
    return lax.dot_general(left, right, (((1,), (0,)), ((), ())), preferred_element_type=F32)


def dot_t(left, right):
    return lax.dot_general(left, right, (((1,), (1,)), ((), ())), preferred_element_type=F32)


def half_turn(value):
    return pltpu.roll(value, 64, 1)


def copy_all(pairs, sems):
    copies = [pltpu.make_async_copy(source, target, sems.at[i]) for i, (source, target) in enumerate(pairs)]
    for copy in copies:
        copy.start()

    def wait():
        for copy in copies:
            copy.wait()

    return wait


def packed_inverse(inverse):
    return jnp.concatenate([inverse[16 * t:16 * t + 16, :] for t in range(4)], axis=1)


def link_rows_of(owned, links, q):
    lane, row = lanes((8, 256)), rows((8, 256))
    tail = jnp.zeros((8, 256), F32)
    for j_rel in range(owned):
        for l in range(links.shape[1]):
            link = links[jnp.bitwise_xor(q, j_rel), l].astype(F32)
            tail = jnp.where((row == j_rel) & (lane == l), link, tail)
    return tail


def begin_kernel(owned, r_in, b_in, e_in, n_in, links_in, coupling_in, inverses_in, first, second, own,
                 r, b, e, n, links, inverse, sems):
    q = lax.rem(lax.axis_index("narrow"), owned)
    wait = copy_all([(r_in, r), (b_in, b), (e_in, e), (n_in, n), (links_in, links),
                     (coupling_in.at[q], own.at[pl.ds(0, 64)]), (inverses_in.at[q], inverse)], sems)
    grid_rows = b.shape[0]
    line, _ = place()
    even = lax.rem(line, 2) == 0
    wait()

    def message(start, north_start):
        parts = [r[a, start:start + HALO, :] for a in range(r.shape[0])]
        parts += [b[start:start + HALO, :], e[start:start + HALO, :]]
        parts += [n[north_start:north_start + HALO + 1, :], jnp.zeros((2, b.shape[1]), F32)]
        return parts

    top = message(0, 0)
    bottom = message(grid_rows - HALO, grid_rows - HALO - 1)
    at = 0
    for low, high in zip(top, bottom):
        size = low.shape[0]
        first[at:at + size, :] = jnp.where(even, high, low)
        second[at:at + size, :] = jnp.where(even, low, high)
        at += size

    own[64:PIECE, :] = packed_inverse(inverse[...])
    own[PIECE:PIECE + 8, :] = link_rows_of(owned, links, q)


def prepare_kernel(owned, coarse_rows, r_in, b_in, e_in, n_in, links_in, coupling_in, inverses_in, support_in, basis_in,
                   block, r_out, b_out, e_out, n_out, basis, hots, sup_hots, support, links, inverses, sems):
    q = lax.rem(lax.axis_index("narrow"), owned)
    mine = lax.axis_index("wide") * owned + q
    wait_support = copy_all([(support_in, support)], sems.at[pl.ds(0, 1)])
    wait_rows = copy_all([(coupling_in.at[jnp.bitwise_xor(q, j)], block.at[pl.ds(j * PIECE, 64)]) for j in range(owned)]
                         + [(links_in, links), (inverses_in, inverses)], sems.at[pl.ds(13, owned + 2)])
    part = basis.shape[0] // 8
    parts = [pl.ds(part * i, part) for i in range(8)]
    wait = copy_all([(basis_in.at[at], basis.at[at]) for at in parts]
                    + [(r_in, r_out), (b_in, b_out), (e_in, e_out), (n_in, n_out)], sems.at[pl.ds(1, 12)])
    wait_rows()
    for j in range(owned):
        block[j * PIECE + 64:j * PIECE + PIECE, :] = packed_inverse(inverses[jnp.bitwise_xor(q, j)])
    block[owned * PIECE:owned * PIECE + 8, :] = link_rows_of(owned, links, q)
    wait_support()

    blocks = support.shape[1]
    rows4 = 4 * blocks
    size = 4 * coarse_rows

    def chosen(which, index):
        g, h = lax.shift_right_logical(index, 4), jnp.bitwise_and(lax.shift_right_logical(index, 3), 1)
        p = jnp.bitwise_and(lax.shift_right_logical(index, 2), 1)
        return jnp.where(which == g * 4 + p * 2 + h, 1.0, 0.0).astype(BF16)

    value = support[...].astype(F32).astype(BF16)
    column = dot_t(chosen(lanes((rows4, blocks)), rows((rows4, blocks))), value)
    line = dot(value, chosen(rows((blocks, rows4)), lanes((blocks, rows4))))
    line = line.astype(jnp.int32) * 4 + jnp.bitwise_and(lanes((4, rows4)), 3)
    at = rows((size, rows4))
    for k in range(4):
        base, left = (k % 2) * size, (k // 2) * rows4
        hots[base:base + size, left:left + rows4] = jnp.where(at == line[k:k + 1, :], 1.0, 0.0).astype(BF16)
    column = jnp.bitwise_xor(column.astype(jnp.int32), mine) * 4 + jnp.bitwise_and(rows((rows4, 4)), 3)
    across = lanes((rows4, size))
    for k in range(4):
        sup_hots[rows4 * k:rows4 * k + rows4, :] = jnp.where(across == column[:, k:k + 1], 1.0, 0.0).astype(BF16)

    wait()


def stack_kernel(*refs):
    fetched, gathered, far = refs[:-5], refs[-2], refs[-1]
    owned = far.shape[0] // len(fetched)
    for i, piece in enumerate(fetched):
        gathered[PIECE * i:PIECE * i + PIECE, :] = piece[0:PIECE, :]
        far[owned * i:owned * i + owned, :] = piece[PIECE:PIECE + owned, :]


def add_kernel(one, two, out):
    half = out.shape[0] // 2
    for i in range(2):
        block = slice(128 * i, 128 * i + 128)
        out[half * i:half * i + half, :] = one[0:half, block] + two[0:half, block]


class Fine:
    def __init__(self, r, b, e, n, from_first, from_second, rx, bx, ex, nx, field):
        line, count = place()
        even = lax.rem(line, 2) == 0
        low_ok, high_ok = line > 0, line < count - 1
        one, two = from_first[...], from_second[...]
        low = jnp.where(low_ok, jnp.where(even, two, one), 0.0)
        high = jnp.where(high_ok, jnp.where(even, one, two), 0.0)
        self.even, self.low_ok, self.high_ok = even, low_ok, high_ok
        self.adjoints, self.grid_rows, width = r.shape
        top = HALO + self.grid_rows
        zeros = jnp.zeros((8, width), F32)
        for a in range(self.adjoints):
            rx[a, 16:24, :] = zeros
            rx[a, 0:HALO, :] = low[3 * a:3 * a + 3]
            rx[a, HALO:top, :] = r[a]
            rx[a, top:top + HALO, :] = high[3 * a:3 * a + 3]
            field[a, 0:8, :] = zeros
            field[a, 32:40, :] = zeros
        bx[16:24, :] = zeros
        bx[0:HALO, :] = low[12:15]
        bx[HALO:top, :] = b[...]
        bx[top:top + HALO, :] = high[12:15]
        ex[16:24, :] = zeros
        ex[0:HALO, :] = low[15:18]
        ex[HALO:top, :] = e[...]
        ex[top:top + HALO, :] = high[15:18]
        nx[16:24, :] = zeros
        nx[24:32, :] = zeros
        nx[0:HALO + 1, :] = low[18:22]
        nx[HALO + 1:top + 1, :] = n[...]
        nx[top + 1:top + 1 + HALO, :] = high[18:21]
        self.r = rx[...]
        self.east = ex[...]
        self.north = nx[1:1 + FIELD, :]
        self.south = nx[0:FIELD, :]
        self.west = pltpu.roll(self.east, 1, 1)
        self.diagonal = bx[...] + self.east + self.west + self.north + self.south
        t = rows((FIELD, width))
        valid = ((t >= HALO) | low_ok) & ((t < top) | high_ok) & (t < top + HALO)
        self.scale = jnp.where(valid, relax_weight / jnp.where(valid, self.diagonal, 1.0), 0.0)
        self.field = field
        self.width = width

    def apply(self, x):
        self.field[:, 8:32, :] = x
        above = self.field[:, 7:31, :]
        below = self.field[:, 9:33, :]
        east = pltpu.roll(x, self.width - 1, 2)
        west = pltpu.roll(x, 1, 2)
        return self.diagonal * x - self.north * below - self.south * above - self.east * east - self.west * west

    def sweep(self, x):
        return x + self.scale * (self.r - self.apply(x))


    def keep(self, r_out, coef_out):
        r_out[...] = self.r
        for i, value in enumerate((self.diagonal, self.scale, self.north, self.south, self.east, self.west)):
            coef_out[i] = value


class Kept(Fine):
    def __init__(self, r, coef, field):
        line, count = place()
        self.even, self.low_ok, self.high_ok = lax.rem(line, 2) == 0, line > 0, line < count - 1
        self.r, self.field = r[...], field
        self.diagonal, self.scale, self.north, self.south, self.east, self.west = [coef[i] for i in range(6)]
        self.adjoints, _, self.width = r.shape


def fine_scratch(adjoints, width):
    return [
        pltpu.VMEM((adjoints, FIELD, width), F32),
        pltpu.VMEM((FIELD, width), F32),
        pltpu.VMEM((FIELD, width), F32),
        pltpu.VMEM((32, width), F32),
        pltpu.VMEM((adjoints, 40, width), F32),
    ]


def restrict_kernel(coarse_rows, r, b, e, n, from_second, from_first, basis, hots,
                    block, gathered, far, out, x_out, rx, bx, ex, nx, field, by_row, contrib):
    fine = Fine(r, b, e, n, from_first, from_second, rx, bx, ex, nx, field)
    x = fine.scale * fine.r
    for step in range(SWEEPS - 1):
        x = fine.sweep(x)
    resid = fine.r - fine.apply(x)
    for a in range(fine.adjoints):
        x_out[a] = field[a, 8 + HALO:8 + HALO + fine.grid_rows, :]
    field[:, 8:32, :] = resid
    for a in range(fine.adjoints):
        by_row[pl.ds(a, fine.grid_rows, stride=4), :] = field[a, 8 + HALO:8 + HALO + fine.grid_rows, :]
    left = lanes((8, 128)) < 64
    upper = rows((8, 128)) < 4
    for g in range(fine.grid_rows // 2):
        z = by_row[8 * g:8 * g + 8, :]
        parts = []
        for here in (left, ~left):
            held = jnp.where(here, z, 0.0)
            parts.append(jnp.concatenate([jnp.where(upper, held, 0.0), jnp.where(upper, 0.0, held)], axis=1))
        high, low = split(jnp.concatenate(parts, axis=0))
        near = slice(256 * g, 256 * g + 256)
        w_high, w_low = split(basis[near, :])
        both = dot(jnp.concatenate([high, low], axis=0), w_high)
        contrib[16 * g:16 * g + 16, :] = both[0:16] + both[16:32] + dot(high, w_low)
    c_high, c_low = split(contrib[...])
    weights = jnp.concatenate([
        jnp.concatenate([c_high[:, 0:128], c_low[:, 0:128]], axis=1),
        jnp.concatenate([c_high[:, 128:256], c_low[:, 128:256]], axis=1)], axis=0)
    size = 4 * coarse_rows
    total = dot(hots[...], weights)
    total = total[:, 0:128] + total[:, 128:256]
    here = lanes((size, 128)) < 64
    even = jnp.where(here, total[0:size], 0.0)
    odd = jnp.where(here, 0.0, total[size:2 * size])
    mid = size // 2
    packed = even[0:mid] + half_turn(odd[0:mid]) + half_turn(even[mid:size]) + odd[mid:size]
    half = mid // 2
    out[0:half, 0:128] = packed[0:half]
    out[0:half, 128:256] = packed[half:mid]
    out[half:half + block.shape[0], :] = block[...]
    at = half + block.shape[0]
    out[at:at + gathered.shape[0], :] = gathered[...]
    at += gathered.shape[0]
    out[at:at + far.shape[0], :] = far[...]


def prolong(group, high, low, basis):
    near = slice(16 * group, 16 * group + 16)
    block = slice(256 * group, 256 * group + 256)
    high = high[near, :]
    w_high, w_low = split(basis[block, :])
    both = dot_t(jnp.concatenate([high, low[near, :]], axis=0), w_high)
    got = both[0:16] + both[16:32] + dot_t(high, w_low)
    upper = rows((8, 128)) < 4
    halves = [jnp.where(upper, got[8 * h:8 * h + 8, 0:128], got[8 * h:8 * h + 8, 128:256]) for h in range(2)]
    return jnp.where(lanes((8, 128)) < 64, halves[0], halves[1])


def coarse_kernel(owned, coarse_rows, zs, rhs_ref, message, message_other, *refs):
    spread, spread_other = refs[:owned - 1], refs[owned - 1:2 * owned - 2]
    (basis, sup_hots, x_ref, coarse_ref, high_out, low_out, first, second,
     w_high, w_low, w_inv, link_rows, hots, product, u_ref, by_row) = refs[2 * owned - 2:]
    size = 4 * coarse_rows
    wide, narrow = lax.axis_index("wide"), lax.axis_index("narrow")
    q = lax.rem(narrow, owned)
    mine = wide * owned + q

    lane16 = lanes((16, 128)) < 64
    lane64 = lanes((64, 128)) < 64
    at_own = coarse_rows
    at_fetched = at_own + packed_rows(owned)
    for z_rel in range(zs):
        for c_rel, (fetched, others) in enumerate(((message, spread), (message_other, spread_other))):
            for j_rel in range(owned):
                i = (z_rel * 2 + c_rel) * owned + j_rel
                at_links = at_own + owned * PIECE + j_rel
                if z_rel > 0:
                    at_links = at_fetched + (zs - 1) * PIECE + (z_rel - 1) * owned + j_rel
                if z_rel == 0:
                    piece, base = fetched, at_own + j_rel * PIECE
                elif j_rel == 0:
                    piece, base = fetched, at_fetched + (z_rel - 1) * PIECE
                else:
                    piece, base = others[j_rel - 1], (z_rel - 1) * PIECE
                high, low = split(piece[base:base + 64, :])
                w_high[64 * i:64 * i + 64, :] = high
                w_low[64 * i:64 * i + 64, :] = low
                quarters = []
                for half in range(2):
                    packed = piece[base + 64:base + 80, 128 * half:128 * half + 128]
                    turned = half_turn(packed)
                    quarters += [jnp.where(lane16, packed, turned), jnp.where(lane16, turned, packed)]
                high, low = split(jnp.concatenate(quarters, axis=0))
                w_inv[64 * i:64 * i + 64, :] = jnp.where(lane64, high.astype(F32), low.astype(F32)).astype(BF16)
                link_rows[4 * i:4 * i + 4, :] = jnp.broadcast_to(fetched[at_links:at_links + 1, 0:128], (4, 128))

    lane = lanes((size, size))
    a_col = jnp.bitwise_and(rows((size, 1)), 3)
    for l in range(4):
        target = jnp.bitwise_xor(link_rows[:, l:l + 1].astype(jnp.int32), mine) * 4 + a_col
        hots[size * l:size * l + size, :] = jnp.where(lane == target, 1.0, 0.0).astype(BF16)

    here = lanes((size, 128)) < 64
    packed = rhs_ref[...]
    turned = half_turn(packed)
    here_mid = here[0:size // 2]
    rhs = jnp.concatenate([jnp.where(here_mid, packed, turned), jnp.where(here_mid, turned, packed)], axis=0)

    def hi_lo(value):
        high, low = split(value)
        return jnp.concatenate([high, low], axis=1)

    u_ref[...] = rhs
    for i in range(coarse_rows):
        link_rows[4 * i:4 * i + 4, :] = u_ref[pl.ds(jnp.bitwise_xor(mine, i) * 4, 4), :]
    rhs = link_rows[...]

    own_block = jnp.bitwise_and(lax.shift_right_logical(rows((size, 256)), 2), 3) == lax.shift_right_logical(
        lanes((size, 256)), 6)

    def fold():
        value = jnp.where(own_block, product[...], 0.0)
        value = value[:, 0:128] + value[:, 128:256]
        return value + half_turn(value)

    def apply_inverse(value):
        high, low = split(value)
        low = jnp.where(here, low.astype(F32), 0.0).astype(BF16)
        for g in range(coarse_rows // 4):
            near = slice(16 * g, 16 * g + 16)
            both = dot_t(jnp.concatenate([high[near], low[near]], axis=0), w_inv[256 * g:256 * g + 256, :])
            product[near, :] = both[0:16] + both[16:32]
        return fold()

    def pick(got, step):
        sel = lanes((step, 128)) < 64
        high = [jnp.where(sel, got[step * k:step * k + step, 0:128], got[step * k + step:step * k + 2 * step, 0:128])
                for k in (0, 2)]
        low = [jnp.where(sel, got[step * k:step * k + step, 128:256],
                         got[step * k + step:step * k + 2 * step, 128:256]) for k in (0, 2)]
        return jnp.concatenate(high, axis=1).astype(BF16), jnp.concatenate(low, axis=1).astype(BF16)

    u = apply_inverse(rhs)
    for step in range(COARSE_SWEEPS):
        high, low = pick(dot(hots[...], hi_lo(u)), size)
        for g in range(coarse_rows // 4):
            near = slice(16 * g, 16 * g + 16)
            block = slice(256 * g, 256 * g + 256)
            both = dot_t(jnp.concatenate([high[near], low[near]], axis=0), w_high[block, :])
            product[near, :] = both[0:16] + both[16:32] + dot_t(high[near], w_low[block, :])
        u = apply_inverse(rhs + fold())

    u_ref[0:4 * owned, :] = u[0:4 * owned]
    here1 = lanes((1, 128)) < 64
    for j in range(owned):
        got = u_ref[pl.ds(jnp.bitwise_xor(q, j) * 4, 4), :]
        coarse_ref[j:j + 1, 0:128] = jnp.where(here1, got[0:1], got[1:2])
        coarse_ref[j:j + 1, 128:256] = jnp.where(here1, got[2:3], got[3:4])

    blocks4 = sup_hots.shape[0] // 4
    high, low = pick(dot(sup_hots[...], hi_lo(u)), blocks4)
    high_out[...] = high
    low_out[...] = low
    line, _ = place()
    even = lax.rem(line, 2) == 0
    adjoints, grid_rows, _ = x_ref.shape
    by_row[0:8, :] = prolong(0, high, low, basis)
    by_row[8:16, :] = prolong(grid_rows // 2 - 1, high, low, basis)
    for a in range(adjoints):
        edge = by_row[pl.ds(a, 4, stride=4), :]
        top = x_ref[a, 0:2, :] + edge[0:2]
        bottom = x_ref[a, grid_rows - 2:grid_rows, :] + edge[2:4]
        first[2 * a:2 * a + 2, :] = jnp.where(even, bottom, top)
        second[2 * a:2 * a + 2, :] = jnp.where(even, top, bottom)


def correct_kernel(r, b, e, n, from_second, from_first, x_ref, high, low, basis,
                   r_out, coef_out, y_out, rx, bx, ex, nx, field, by_row):
    Fine(r, b, e, n, from_first, from_second, rx, bx, ex, nx, field).keep(r_out, coef_out)
    adjoints, grid_rows, width = x_ref.shape
    for g in range(grid_rows // 2):
        by_row[8 * g:8 * g + 8, :] = prolong(g, high, low, basis)
    for a in range(adjoints):
        y_out[a, 0:8, :] = jnp.zeros((8, width), F32)
        y_out[a, 16:24, :] = jnp.zeros((8, width), F32)
        y_out[a, HALO:HALO + grid_rows, :] = x_ref[a] + by_row[pl.ds(a, grid_rows, stride=4), :]


def post_kernel(r, coef, y_ref, y_first, y_inner, y_outer, out, field):
    fine = Kept(r, coef, field)
    in_line = lax.rem(place()[0], 4)
    one, two = y_first[...], jnp.where((in_line == 1) | (in_line == 2), y_inner[...], y_outer[...])
    low = jnp.where(fine.low_ok, jnp.where(fine.even, two, one), 0.0)
    high = jnp.where(fine.high_ok, jnp.where(fine.even, one, two), 0.0)
    grid_rows = out.shape[1]
    start, top = 8 + HALO, 8 + HALO + grid_rows
    field[:, 0:8, :] = jnp.zeros((fine.adjoints, 8, fine.width), F32)
    field[:, 32:40, :] = jnp.zeros((fine.adjoints, 8, fine.width), F32)
    field[:, 8:32, :] = y_ref[...]
    for a in range(fine.adjoints):
        field[a, start - 2:start, :] = low[2 * a:2 * a + 2]
        field[a, top:top + 2, :] = high[2 * a:2 * a + 2]
    x = field[:, 8:32, :]
    for step in range(SWEEPS):
        x = fine.sweep(x)
    field[:, 8:32, :] = x
    for a in range(fine.adjoints):
        out[a] = field[a, start:top, :]


def shape(*dims, kind=F32):
    return jax.ShapeDtypeStruct(dims, kind)


def params(mebibytes):
    return pltpu.CompilerParams(vmem_limit_bytes=mebibytes * 2 ** 20)


def stay(array):
    return pltpu.with_memory_space_constraint(array, pltpu.HBM)


CHEAP = pl.CostEstimate(flops=1, bytes_accessed=1, transcendentals=0)


def body(right_sides, brinkman, east_faces, north_faces, support, basis, links, coarse_block_inverses, coarse_coupling):
    adjoints, grid_rows, width = right_sides.shape
    blocks, block_size, _ = basis.shape
    owned = coarse_block_inverses.shape[0]
    coarse_rows = owned * lax.axis_size("wide")
    zs = lax.axis_size("wide") // 2
    size = 4 * coarse_rows
    basis = basis.reshape(blocks * block_size, -1)

    in_hbm = pl.BlockSpec(memory_space=pltpu.HBM)
    anywhere = pl.BlockSpec(memory_space=pl.ANY)
    in_vmem = pl.BlockSpec(memory_space=pltpu.VMEM)
    row_dims = (grid_rows, width)
    message = shape(24, width)
    fine_inputs = tuple(map(stay, (right_sides, brinkman, east_faces, north_faces)))
    coarse_inputs = tuple(map(stay, (links, coarse_coupling, coarse_block_inverses)))
    to_first, to_second, own = pl.pallas_call(
        functools.partial(begin_kernel, owned),
        out_shape=(message, message, shape(packed_rows(1), 256)),
        in_specs=[in_hbm] * 7,
        scratch_shapes=[
            pltpu.VMEM((adjoints, *row_dims), F32), pltpu.VMEM(row_dims, F32), pltpu.VMEM(row_dims, F32),
            pltpu.VMEM(row_dims, F32), pltpu.SMEM(links.shape, jnp.int32),
            pltpu.VMEM(coarse_block_inverses.shape[1:], F32), pltpu.SemaphoreType.DMA((7,))],
        cost_estimate=CHEAP, compiler_params=params(16), name="begin",
    )(*fine_inputs, *coarse_inputs)
    from_first, from_second = pair_swaps(to_first, to_second)
    fetched = [swap(own, "wide", 2 * k) for k in range(1, zs)]

    rows4 = adjoints * blocks
    block, r, b, e, n, basis, hots, sup_hots = pl.pallas_call(
        functools.partial(prepare_kernel, owned, coarse_rows),
        out_shape=(shape(packed_rows(owned), 256), shape(adjoints, *row_dims), shape(*row_dims), shape(*row_dims),
                   shape(*row_dims), shape(*basis.shape), shape(2 * size, 2 * rows4, kind=BF16),
                   shape(4 * rows4, size, kind=BF16)),
        in_specs=[in_hbm] * 9,
        scratch_shapes=[
            pltpu.VMEM((4, blocks), jnp.int32), pltpu.SMEM(links.shape, jnp.int32),
            pltpu.VMEM(coarse_block_inverses.shape, F32), pltpu.SemaphoreType.DMA((13 + owned + 2,))],
        cost_estimate=CHEAP, compiler_params=params(16), name="prepare",
    )(*fine_inputs, *coarse_inputs, stay(support.T), stay(basis))

    height = (zs - 1) * PIECE
    far_rows = (zs - 1) * owned
    gathered, far = pl.pallas_call(
        stack_kernel, out_shape=(shape(height, 256), shape(far_rows, 256)),
        in_specs=[in_vmem] * (zs - 1) + [anywhere] * 3,
        cost_estimate=CHEAP, compiler_params=params(4), name="stack",
    )(*fetched, from_second, from_first, hots)
    spread = [swap(gathered, "narrow", k) for k in range(1, owned)]

    half = coarse_rows
    message, x = pl.pallas_call(
        functools.partial(restrict_kernel, coarse_rows),
        out_shape=(shape(half + packed_rows(owned) + height + far_rows, 256), shape(adjoints, *row_dims)),
        scratch_shapes=fine_scratch(adjoints, width) + [
            pltpu.VMEM((4 * grid_rows, width), F32), pltpu.VMEM((rows4, 256), F32)],
        cost_estimate=CHEAP, compiler_params=params(16), name="restrict",
    )(r, b, e, n, from_second, from_first, basis, hots, block, gathered, far)

    message_other = swap(message, "wide", 1)
    rhs = pl.pallas_call(
        add_kernel, out_shape=shape(2 * half, 128), cost_estimate=CHEAP, compiler_params=params(4), name="add",
    )(message, message_other)
    for masks in rounds_of(zs):
        rhs = sum_shared(rhs, "wide", [2 * k for k in masks])
    spread = tie(spread, rhs)
    spread_other = [swap(piece, "wide", 1) for piece in spread]
    for masks in rounds_of(lax.axis_size("narrow")):
        rhs = sum([swap(rhs, "narrow", k) for k in masks], rhs)

    near = shape(rows4, 256, kind=BF16)
    coarse, high, low, y_first, y_second = pl.pallas_call(
        functools.partial(coarse_kernel, owned, coarse_rows, zs),
        out_shape=(shape(owned, 256), near, near, shape(8, width), shape(8, width)),
        scratch_shapes=[
            pltpu.VMEM((64 * coarse_rows, 256), BF16), pltpu.VMEM((64 * coarse_rows, 256), BF16),
            pltpu.VMEM((64 * coarse_rows, 128), BF16), pltpu.VMEM((size, 128), F32),
            pltpu.VMEM((4 * size, size), BF16), pltpu.VMEM((size, 256), F32),
            pltpu.VMEM((size, 128), F32), pltpu.VMEM((16, width), F32)],
        cost_estimate=CHEAP, compiler_params=params(min(48, 8 + coarse_rows // 3)), name="coarse",
    )(rhs, message, message_other, *spread, *spread_other, basis, sup_hots, x)

    y_from = pair_swaps_near(y_first, y_second)
    extended = shape(adjoints, FIELD, width)
    r, coef, y = pl.pallas_call(
        correct_kernel,
        out_shape=(extended, shape(6, FIELD, width), extended),
        scratch_shapes=fine_scratch(adjoints, width) + [pltpu.VMEM((4 * grid_rows, width), F32)],
        cost_estimate=CHEAP, compiler_params=params(16), name="correct",
    )(r, b, e, n, from_second, from_first, x, high, low, basis)
    field = pl.pallas_call(
        post_kernel,
        out_shape=shape(adjoints, *row_dims),
        scratch_shapes=[pltpu.VMEM((adjoints, 40, width), F32)],
        cost_estimate=CHEAP, compiler_params=params(16), name="post",
    )(r, coef, y, *y_from)
    return field, coarse


def solution(mesh):
    return jax.shard_map(
        body,
        mesh=mesh,
        in_specs=(
            P(None, ("wide", "narrow"), None),
            P(("wide", "narrow"), None),
            P(("wide", "narrow"), None),
            P(("wide", "narrow"), None),
            P(("wide", "narrow"), None),
            P(("wide", "narrow"), None, None),
            P("wide", None),
            P("wide", None, None),
            P("wide", None, None),
        ),
        out_specs=(P(None, ("wide", "narrow"), None), P("wide", None)),
        check_vma=False,
    )
```
